128 devices in a mesh: dp: 16 (over z, x_lo, core), fsdp: 8 (over y, x_hi).
Axes of the slice: x: 4 (x_hi: 2, x_lo: 2; x = x_hi * 2 + x_lo), y: 4, z: 4, core: 2. Of those that a mesh axis runs over, the one named last changes fastest.
Arguments:
- images: bfloat16 [256, 8, 8, 3072], P(('dp', 'fsdp')), may hold values from -6 to 6
- grad_out: bfloat16 [256, 8, 8, 3072], P(('dp', 'fsdp')), may hold values from -6 to 6
- dw_weight: float32 [7, 7, 3072], replicated, may hold values from -0.875 to 0.875
- dw_bias: float32 [3072], replicated, may hold values from -3 to 3
- ln_gain: float32 [3072], replicated, may hold values from 0.1 to 1.9
- ln_bias: float32 [3072], replicated, may hold values from -2 to 2
- w_up: bfloat16 [3072, 6144], P(None, 'fsdp'), may hold values from -0.109375 to 0.109375
- b_up: float32 [6144], P('fsdp'), may hold values from -3 to 3
- w_down: bfloat16 [6144, 3072], P('fsdp'), may hold values from -0.15625 to 0.15625
- b_down: float32 [3072], replicated, may hold values from -3 to 3
- layer_scale: float32 [3072], replicated, may hold values from 0.3 to 1.5
Outputs:
- out_images: bfloat16 [256, 8, 8, 3072], P(('dp', 'fsdp'))
- grad_images: bfloat16 [256, 8, 8, 3072], P(('dp', 'fsdp'))
- grad_w_up: bfloat16 [3072, 6144], P(None, 'fsdp')
- grad_b_up: bfloat16 [6144], P('fsdp')
- grad_w_down: bfloat16 [6144, 3072], P('fsdp')
- grad_dw_weight: float32 [7, 7, 3072], replicated
- grad_dw_bias: float32 [3072], replicated
- grad_ln_gain: float32 [3072], replicated
- grad_ln_bias: float32 [3072], replicated
- grad_b_down: float32 [3072], replicated
- grad_layer_scale: float32 [3072], replicated
The draws below stay inside these ranges and needn't reach their ends.
All inputs are finite; a program needn't handle non-finite values.
Results may differ from the reference program's by a relative error of at most 0.025.
Values may be sent and summed in bfloat16 or wider, within the bound.
A program may use at most 256 MiB of HBM per device.

```python
import math
import jax
import jax.numpy as jnp
from jax import lax

WIDTH = 3072
HIDDEN_SIZE = 6144
SIDE = 8
KERNEL = 7
IMG_DEV = 2
IMAGES = 256
TOKENS = 16384
N_DP = 16
N_FSDP = 8


def shard_levels(rng, shape, pieces, least, high):
    loudness, own = 1.0, jax.random.fold_in(rng, 6)
    for position, shards_of in pieces:
        draws = jnp.exp(jax.random.uniform(jax.random.fold_in(own, position), (shards_of,), jnp.float32, least / len(pieces), high / len(pieces)))
        loudness = loudness * jnp.repeat(draws, shape[position] // shards_of).reshape([-1 if axis == position else 1 for axis in range(len(shape))])
    return loudness


def scatter_about(own_key, shape, width, bound, pieces=(), dtype=jnp.bfloat16):
    values = jax.random.normal(own_key, shape, jnp.float32) * width
    if len(pieces) > 0:
        values = shard_levels(own_key, shape, pieces, -0.22, 0.18) * values
    return jnp.clip(values, min=-bound, max=bound).astype(dtype)


def setup_inputs(seed: int = 0) -> dict:
    keys = jax.random.split(jax.random.key(seed), 12)
    images = scatter_about(keys[0], (IMAGES, SIDE, SIDE, WIDTH), 1.0, 6.0, ((0, 128),))
    grad_out = scatter_about(keys[1], (IMAGES, SIDE, SIDE, WIDTH), 1.0, 6.0, ((0, 128),))
    dw_weight = scatter_about(keys[2], (KERNEL, KERNEL, WIDTH), (KERNEL * KERNEL) ** -0.5, 0.875, (), jnp.float32)
    dw_bias = scatter_about(keys[3], (WIDTH,), 0.5, 3.0, (), jnp.float32)
    ln_gain = jnp.clip(1.0 + 0.18 * jax.random.normal(keys[4], (WIDTH,), jnp.float32), 0.1, 1.9)
    ln_bias = scatter_about(keys[5], (WIDTH,), 0.3, 2.0, (), jnp.float32)
    w_up = scatter_about(keys[6], (WIDTH, HIDDEN_SIZE), WIDTH ** -0.5, 0.109375, ((1, 8),))
    b_up = scatter_about(keys[7], (HIDDEN_SIZE,), 0.5, 3.0, ((0, 8),), jnp.float32)
    w_down = scatter_about(keys[8], (HIDDEN_SIZE, WIDTH), (HIDDEN_SIZE // 4) ** -0.5, 0.15625, ((0, 8),))
    b_down = scatter_about(keys[9], (WIDTH,), 0.5, 3.0, (), jnp.float32)
    layer_scale = jnp.clip(jnp.exp(jax.random.uniform(keys[10], (WIDTH,), jnp.float32, math.log(0.3), math.log(1.5))), 0.3, 1.5)
    return dict(images=images, grad_out=grad_out, dw_weight=dw_weight, dw_bias=dw_bias, ln_gain=ln_gain, ln_bias=ln_bias, w_up=w_up, b_up=b_up, w_down=w_down, b_down=b_down, layer_scale=layer_scale)


def depthwise(pixels, kernel, offset):
    margin = kernel.shape[0] // 2
    extent = pixels.shape[1]
    padded = jnp.pad(pixels, ((0, 0), (margin, margin), (margin, margin), (0, 0)))
    summed = jnp.zeros(pixels.shape, jnp.float32)
    for vertical in range(kernel.shape[0]):
        for horizontal in range(kernel.shape[1]):
            summed = summed + padded[:, vertical:vertical + extent, horizontal:horizontal + extent, :] * kernel[vertical, horizontal]
    return summed + offset

def layer_norm(before_norm, gain, offset):
    average = lax.optimization_barrier(jnp.mean(before_norm, axis=-1, keepdims=True))
    centred = before_norm - average
    inv_std = lax.rsqrt(lax.optimization_barrier(jnp.mean(centred * centred, axis=-1, keepdims=True)) + 1e-06)
    standard = centred * inv_std
    return (standard * gain + offset, standard, inv_std)

def norm_back(grad_normed, standard, inv_std, gain):
    grad_hat = grad_normed * gain
    centred_grad = grad_hat - lax.optimization_barrier(jnp.mean(grad_hat, axis=-1, keepdims=True)) - standard * lax.optimization_barrier(jnp.mean(grad_hat * standard, axis=-1, keepdims=True))
    return (inv_std * centred_grad, lax.optimization_barrier(jnp.sum(grad_normed * standard, axis=(0, 1, 2))), lax.optimization_barrier(jnp.sum(grad_normed, axis=(0, 1, 2))))

def gelu_exact(values):
    return 0.5 * values * (1.0 + lax.erf(values * 0.7071067811865476))

def gelu_slope(values):
    return 0.5 * (1.0 + lax.erf(values * 0.7071067811865476)) + values * jnp.exp(-0.5 * values * values) * 0.3989422804014327

def rounded(values):
    return lax.optimization_barrier(values.astype(jnp.bfloat16)).astype(jnp.float32)

def reference(images, grad_out, dw_weight, dw_bias, ln_gain, ln_bias, w_up, b_up, w_down, b_down, layer_scale):
    channels = images.shape[-1]
    share_width = HIDDEN_SIZE // N_FSDP
    grouped_images = images.reshape(N_DP, IMG_DEV * N_FSDP, SIDE, SIDE, channels)
    grouped_grads = grad_out.reshape(N_DP, IMG_DEV * N_FSDP, SIDE, SIDE, channels)
    up_transposed = w_up.T
    down_transposed = w_down.T

    def blocked(left, right):
        summed = jnp.zeros((left.shape[0], right.shape[1]), jnp.float32)
        for segment in range(N_FSDP):
            lower = segment * share_width
            partial_sum = jnp.dot(left[:, lower:lower + share_width], right[lower:lower + share_width], preferred_element_type=jnp.float32)
            summed = summed + rounded(partial_sum)
        return summed

    def group_step(running, inputs):
        group_images, grad_block = inputs
        pixels = group_images.astype(jnp.float32)
        upstream = grad_block.astype(jnp.float32)
        before_norm = depthwise(pixels, dw_weight, dw_bias)
        normed_full, standard, inv_std = layer_norm(before_norm, ln_gain, ln_bias)
        normed = normed_full.reshape(-1, channels).astype(jnp.bfloat16)
        pre_up = jnp.dot(normed, w_up, preferred_element_type=jnp.float32) + b_up
        hidden = gelu_exact(pre_up).astype(jnp.bfloat16)
        branch = (blocked(hidden, w_down) + b_down).reshape(pixels.shape)
        result = (pixels + layer_scale * branch).astype(jnp.bfloat16)
        scaled = (layer_scale * upstream).reshape(-1, channels).astype(jnp.bfloat16)
        grad_hidden = jnp.dot(scaled, down_transposed, preferred_element_type=jnp.float32)
        grad_pre = (grad_hidden * gelu_slope(pre_up)).astype(jnp.bfloat16)
        part_up = jnp.dot(normed.T, grad_pre, preferred_element_type=jnp.float32)
        part_down = jnp.dot(hidden.T, scaled, preferred_element_type=jnp.float32)
        part_bias = lax.optimization_barrier(jnp.sum(grad_pre.astype(jnp.float32), axis=0))
        grad_normed = blocked(grad_pre, up_transposed).reshape(pixels.shape)
        grad_conv, grad_gain, grad_shift = norm_back(grad_normed, standard, inv_std, ln_gain)
        unused, pullback = jax.vjp(depthwise, pixels, dw_weight, dw_bias)
        grad_pixels, grad_kernel, grad_conv_bias = pullback(grad_conv)
        grad_result = (upstream + grad_pixels).astype(jnp.bfloat16)
        grad_down_bias = lax.optimization_barrier(jnp.sum(scaled.astype(jnp.float32), axis=0))
        grad_scale = lax.optimization_barrier(jnp.sum(upstream * branch, axis=(0, 1, 2)))
        updated = (running[0] + rounded(part_up), running[1] + rounded(part_down), running[2] + rounded(part_bias), running[3] + grad_kernel, running[4] + grad_conv_bias, running[5] + grad_gain, running[6] + grad_shift, running[7] + grad_down_bias, running[8] + grad_scale)
        return (updated, (result, grad_result))
    start_carry = (jnp.zeros((channels, HIDDEN_SIZE), jnp.float32), jnp.zeros((HIDDEN_SIZE, channels), jnp.float32), jnp.zeros((HIDDEN_SIZE,), jnp.float32), jnp.zeros(dw_weight.shape, jnp.float32), jnp.zeros((channels,), jnp.float32), jnp.zeros((channels,), jnp.float32), jnp.zeros((channels,), jnp.float32), jnp.zeros((channels,), jnp.float32), jnp.zeros((channels,), jnp.float32))
    totals, stacked = lax.scan(group_step, start_carry, (grouped_images, grouped_grads))
    factor = 1.0 / math.sqrt(TOKENS)
    out_images = stacked[0].reshape(images.shape)
    grad_images = stacked[1].reshape(images.shape)
    return (out_images, grad_images, (totals[0] * factor).astype(jnp.bfloat16), (totals[2] * factor).astype(jnp.bfloat16), (totals[1] * factor).astype(jnp.bfloat16), totals[3] * factor, totals[4] * factor, totals[5] * factor, totals[6] * factor, totals[7] * factor, totals[8] * factor)
```

```python
import math

import jax
import jax.numpy as jnp
from jax import lax
from jax.experimental import pallas as pl
from jax.experimental.pallas import tpu as pltpu
from jax.sharding import PartitionSpec as P

MESH = pl.DeviceIdType.MESH
F32 = jnp.float32
BF16 = jnp.bfloat16
CH = 3072
HID = 768
ROWS = 128
LANES = 128
BLOCKS = CH // LANES
ANY = pl.BlockSpec(memory_space=pl.ANY)
VMEM = pl.BlockSpec(memory_space=pltpu.VMEM)


class Place:
    def __init__(self):
        d = lax.axis_index("dp")
        f = lax.axis_index("fsdp")
        self.z = lax.div(d, 4)
        self.x_lo = lax.rem(lax.div(d, 2), 2)
        self.core = lax.rem(d, 2)
        self.y = lax.div(f, 2)
        self.x_hi = lax.rem(f, 2)
        self.x = self.x_hi * 2 + self.x_lo
        self.other_core = 1 - self.core
        self.x_cut = 3 - self.x
        self.x_pair = self.x_hi * 2 + (1 - self.x_lo)

    def at(self, x=None, y=None, z=None, core=None):
        x = self.x if x is None else x
        y = self.y if y is None else y
        z = self.z if z is None else z
        core = self.core if core is None else core
        return (z * 4 + lax.rem(x, 2) * 2 + core, y * 2 + lax.div(x, 2))

    def ring(self, axis):
        me = getattr(self, axis)
        right, left, far = lax.rem(me + 1, 4), lax.rem(me + 3, 4), lax.rem(me + 2, 4)
        return self.at(**{axis: right}), self.at(**{axis: left}), me, right, left, far


class Copies:
    def __init__(self, send, recv, local):
        self.send, self.recv, self.local = send, recv, local
        self.used = 0
        self.used_local = 0
        self.sent = []

    def remote(self, src, dst, device):
        index = self.used
        self.used += 1
        return pltpu.make_async_remote_copy(
            src_ref=src,
            dst_ref=dst,
            send_sem=self.send.at[index],
            recv_sem=self.recv.at[index],
            device_id=device,
            device_id_type=MESH,
        )

    def push(self, src, dst, device):
        copy = self.remote(src, dst, device)
        copy.start()
        self.sent.append(copy)
        return copy

    def here(self, src, dst):
        index = self.used_local
        self.used_local += 1
        copy = pltpu.make_async_copy(src, dst, self.local.at[index])
        copy.start()
        return copy

    def drain(self):
        for copy in self.sent:
            copy.wait_send()


def greet(devices):
    barrier = pltpu.get_barrier_semaphore()
    for device in devices:
        pl.semaphore_signal(barrier, inc=1, device_id=device, device_id_type=MESH)
    pl.semaphore_wait(barrier, len(devices))


def rows_at(start, size):
    return pl.ds(pl.multiple_of(start, 16), size)


def lanes_at(block):
    return pl.ds(pl.multiple_of(block * LANES, LANES), LANES)


def shifted(row, by):
    if by == 0:
        return row
    moved = pltpu.roll(row, (-by) % 8, 0)
    place = lax.broadcasted_iota(jnp.int32, row.shape, 0)
    inside = (place + by >= 0) & (place + by < 8)
    return jnp.where(inside, moved, 0.0)


def tile_rows(ref, block):
    tiles = []
    for pair in range(8):
        both = ref[16 * pair : 16 * pair + 16, lanes_at(block)].astype(F32)
        tiles += [both[:8], both[8:]]
    return tiles


def conv_block(block, img, dww, dwb, out):
    pixels = tile_rows(img, block)
    cs = lanes_at(block)
    sums = [jnp.broadcast_to(dwb[0:1, cs], (8, LANES))] * 16
    for horizontal in range(7):
        moved = [shifted(tile, horizontal - 3) for tile in pixels]
        for vertical in range(7):
            tap = vertical * 7 + horizontal
            weight = jnp.broadcast_to(dww[tap : tap + 1, cs], (8, LANES))
            for image in range(2):
                for p in range(8):
                    source = p + vertical - 3
                    if 0 <= source < 8:
                        sums[image * 8 + p] = sums[image * 8 + p] + moved[image * 8 + source] * weight
    for r in range(16):
        out[8 * r : 8 * r + 8, cs] = sums[r]


def first_kernel(
    img, gout, dww, dwb, gain, shift, lscale, wu, wd, bu,
    gn, gs, std, inv, wuo, wdo, buo,
    scaled, normed, bu_v, send, recv, local,
):
    me = Place()
    copies = Copies(send, recv, local)
    right, left, y, y_right, y_left, y_far = me.ring("y")
    cut = me.at(x=me.x_cut)
    pair = me.at(x=me.x_pair)
    mate = me.at(core=me.other_core)
    greet([right, left, cut, pair, mate])

    up_rows, down_rows, parts = 192, 48, 4
    theirs = (1 - me.x_lo) * 2 + me.core
    mine = me.x_lo * 2 + me.core
    pairs = (1 - me.x_lo) * 2 + me.core

    def chunk(matrix, quarter, part):
        size = up_rows if matrix == 0 else down_rows
        return rows_at(quarter * (size * parts) + part * size, size)

    order = [(m, k) for k in range(parts) for m in range(2)]
    over_cut = []
    bias = copies.push(bu, buo, cut)
    for m, k in order:
        src, dst = ((wu, wuo), (wd, wdo))[m]
        at = chunk(m, theirs, k)
        over_cut.append(copies.push(src.at[at], dst.at[at], cut))

    def scale_block(block, carry):
        cs = lanes_at(block)
        scaled[:, cs] = (gout[:, cs].astype(F32) * lscale[0:1, cs]).astype(BF16)
        return carry

    lax.fori_loop(0, BLOCKS, scale_block, 0)

    half = ROWS // 2
    low, high = pl.ds(0, half), pl.ds(half, half)

    def spread(src, dst):
        first = [copies.push(src.at[low], dst.at[y, low], right), copies.push(src.at[high], dst.at[y, high], left)]
        second = [copies.push(src.at[high], dst.at[y, high], right), copies.push(src.at[low], dst.at[y, low], left)]
        return first, second, copies.here(src, dst.at[y])

    def forward(first, dst):
        first[0].wait_recv()
        to_right = copies.push(dst.at[y_left, low], dst.at[y_left, low], right)
        first[1].wait_recv()
        to_left = copies.push(dst.at[y_right, high], dst.at[y_right, high], left)
        return [to_right, to_left]

    s_first, s_second, s_own = spread(scaled, gs)

    def conv_step(block, carry):
        conv_block(block, img, dww, dwb, std)
        return carry

    lax.fori_loop(0, BLOCKS, conv_step, 0)

    def add_block(block, total):
        return total + std[:, lanes_at(block)]

    zero = jnp.zeros((ROWS, LANES), F32)
    mean = jnp.sum(lax.fori_loop(0, BLOCKS, add_block, zero), axis=1, keepdims=True) * (1.0 / CH)

    def square_block(block, total):
        centred = std[:, lanes_at(block)] - mean
        return total + centred * centred

    variance = jnp.sum(lax.fori_loop(0, BLOCKS, square_block, zero), axis=1, keepdims=True) * (1.0 / CH)
    inv_std = lax.rsqrt(variance + 1e-06)
    inv[...] = jnp.broadcast_to(inv_std, (ROWS, LANES))

    def norm_block(block, carry):
        cs = lanes_at(block)
        standard = (std[:, cs] - mean) * inv_std
        std[:, cs] = standard
        normed[:, cs] = (standard * gain[0:1, cs] + shift[0:1, cs]).astype(BF16)
        return carry

    lax.fori_loop(0, BLOCKS, norm_block, 0)
    n_first, n_second, n_own = spread(normed, gn)
    s_last = forward(s_first, gs)

    def relay(index):
        m, k = order[index]
        dst = (wuo, wdo)[m]
        over_cut[index].wait_recv()
        at = chunk(m, mine, k)
        return copies.push(dst.at[at], dst.at[at], mate), copies.push(dst.at[at], dst.at[at], pair)

    def relay_pair(index, from_pair):
        m, k = order[index]
        dst = (wuo, wdo)[m]
        from_pair.wait_recv()
        at = chunk(m, pairs, k)
        return copies.push(dst.at[at], dst.at[at], mate)

    relayed, last = [], []
    for index in range(len(order)):
        relayed.append(relay(index))
        if index == 4:
            n_last = forward(n_first, gn)
        if index >= 1:
            last.append(relay_pair(index - 1, relayed[index - 1][1]))
    last.append(relay_pair(len(order) - 1, relayed[-1][1]))

    bias.wait_recv()
    for copy in s_second + n_second + s_last + n_last + [r[0] for r in relayed] + last:
        copy.wait_recv()
    s_own.wait()
    n_own.wait()
    copies.drain()


def first_call(img, gout, dww, dwb, gain, shift, lscale, wu, wd, bu):
    remote = 48
    return pl.pallas_call(
        first_kernel,
        out_shape=(
            jax.ShapeDtypeStruct((4, ROWS, CH), BF16),
            jax.ShapeDtypeStruct((4, ROWS, CH), BF16),
            jax.ShapeDtypeStruct((ROWS, CH), F32),
            jax.ShapeDtypeStruct((ROWS, LANES), F32),
            jax.ShapeDtypeStruct((CH, HID), BF16),
            jax.ShapeDtypeStruct((HID, CH), BF16),
            jax.ShapeDtypeStruct((8, LANES), F32),
        ),
        in_specs=[VMEM] * 7 + [ANY] * 3,
        out_specs=(ANY, ANY, VMEM, VMEM, ANY, ANY, ANY),
        scratch_shapes=[
            pltpu.VMEM((ROWS, CH), BF16),
            pltpu.VMEM((ROWS, CH), BF16),
            pltpu.VMEM((8, LANES), F32),
            pltpu.SemaphoreType.DMA((remote,)),
            pltpu.SemaphoreType.DMA((remote,)),
            pltpu.SemaphoreType.DMA((2,)),
        ],
        compiler_params=pltpu.CompilerParams(
            collective_id=0, has_side_effects=True, vmem_limit_bytes=40 * 1024 * 1024
        ),
    )(img, gout, dww, dwb, gain, shift, lscale, wu, wd, bu)


def add_rows(dst, dst_row, sources, rows, column, columns, step=16):
    def body(index, carry):
        at = rows_at(dst_row + index * step, step)
        cs = pl.ds(column, columns)
        total = dst[at, cs].astype(F32)
        for ref, row, first in sources:
            total = total + ref[rows_at(row + index * step, step), pl.ds(first, columns)].astype(F32)
        dst[at, cs] = total.astype(dst.dtype)
        return carry

    lax.fori_loop(0, rows // step, body, 0)


class RingSum:
    def __init__(self, copies, where, data, base, rows, near, far, step=16):
        self.copies, self.data, self.base, self.rows = copies, data, base, rows
        self.right, self.left, self.me, self.at_right, self.at_left, self.at_far = where
        self.near, self.far, self.step = near, far, step
        self.half = data.shape[1] // 2

    def block(self, which):
        return self.base + which * self.rows

    def begin(self):
        at = rows_at(self.block(self.at_far), self.rows) if self.step == 16 else pl.ds(self.block(self.at_far), self.rows)
        h = self.half
        self.one = [
            self.copies.push(self.data.at[at, pl.ds(0, h)], self.far.at[0], self.right),
            self.copies.push(self.data.at[at, pl.ds(h, h)], self.far.at[1], self.left),
        ]

    def middle(self):
        h = self.half
        self.two = []
        for side, (device, block) in enumerate(((self.right, self.at_right), (self.left, self.at_left))):
            self.one[side].wait_recv()
            start = self.block(block)
            add_rows(self.data, start, [(self.far.at[side], 0, 0)], self.rows, side * h, h, self.step)
            at = rows_at(start, self.rows)
            self.two.append(self.copies.push(self.data.at[at], self.near.at[side], device))

    def end(self):
        for copy in self.two:
            copy.wait_recv()
        add_rows(
            self.data,
            self.block(self.me),
            [(self.near.at[0], 0, 0), (self.near.at[1], 0, 0)],
            self.rows,
            0,
            2 * self.half,
            self.step,
        )


def small_add(dst, row, sources, rows):
    total = dst[row, :]
    for source in sources:
        total = total + source
    dst[row, :] = total


def second_kernel(
    pn, pb, gu, gd, img, gout, std, inv, dww, gain, lscale, bdown, pbias,
    out_img, grad_img, out_up, out_down, out_small,
    guv, gdv, cu, cd, d1a, d1b, u1a, u1b, d2a, d2b, u2a, u2b, tq, fd, fu,
    nv, bv, n1, n2, b1, b2, gcv, sm, smc, sya, syb, sx, sz, smo,
    send, recv, local,
):
    me = Place()
    copies = Copies(send, recv, local)
    ring_x, ring_y, ring_z = me.ring("x"), me.ring("y"), me.ring("z")
    mate = me.at(core=me.other_core)
    x_cut = me.at(x=me.x_cut)
    x_pair = me.at(x=me.x_pair)
    greet([ring_x[0], ring_x[1], ring_y[0], ring_y[1], ring_z[0], ring_z[1], mate])
    x, y, z = me.x, me.y, me.z
    factor = 1.0 / math.sqrt(16384.0)

    keep = lax.rem(me.x_hi + me.core, 2)
    give = 1 - keep
    z_far, z_right, z_left = ring_z[5], ring_z[3], ring_z[4]
    x_far, x_right, x_left = ring_x[5], ring_x[3], ring_x[4]
    order = [(0, z_far), (1, x_far), (0, z_right), (1, x_right), (0, z_left), (1, x_left), (0, z), (1, x)]
    swaps, loads = [], []

    def piece(matrix, which):
        return rows_at(which * 192, 192) if matrix == 0 else rows_at(which * 768, 768)

    for m, which in order:
        src, dst, mine = ((gd, cd, gdv), (gu, cu, guv))[m]
        at = piece(m, which)
        swaps.append(copies.push(src.at[give, at], dst.at[at], mate))
        loads.append(copies.here(src.at[keep, at], mine.at[at]))

    y_far = ring_y[5]
    load_n = copies.here(pn, nv)
    load_b = copies.here(pb, bv)
    load_n.wait()
    rs_n = RingSum(copies, ring_y, nv, 0, ROWS, n2, n1)
    rs_n.begin()
    load_b.wait()
    rs_b = RingSum(copies, ring_y, bv, 0, ROWS, b2, b1)

    def merge(index):
        m, which = order[index]
        mine, other = ((gdv, cd), (guv, cu))[m]
        rows = 192 if m == 0 else 768
        loads[index].wait()
        swaps[index].wait_recv()
        add_rows(mine, which * rows, [(other, which * rows, 0)], rows, 0, mine.shape[1], 16 if m == 0 else 64)

    rs_d1 = RingSum(copies, ring_z, gdv, 0, 192, d1b, d1a)
    rs_u1 = RingSum(copies, ring_x, guv, 0, 768, u1b, u1a)
    merge(0)
    rs_d1.begin()
    merge(1)
    rs_u1.begin()
    rs_b.begin()
    merge(2)
    merge(3)
    rs_n.middle()
    merge(4)
    merge(5)
    rs_d1.middle()
    rs_u1.middle()
    rs_b.middle()
    merge(6)
    merge(7)

    rs_n.end()
    own = y * ROWS
    zero = jnp.zeros((ROWS, LANES), F32)

    def own_rows(ref, cs):
        return ref[rows_at(own, ROWS), cs].astype(F32)

    def norm_sums(block, totals):
        cs = lanes_at(block)
        grad_normed = own_rows(nv, cs)
        standard = std[:, cs]
        product = grad_normed * standard
        sm[50:51, cs] = jnp.sum(product, axis=0, keepdims=True)
        sm[51:52, cs] = jnp.sum(grad_normed, axis=0, keepdims=True)
        weight = gain[0:1, cs]
        return totals[0] + grad_normed * weight, totals[1] + product * weight

    total_g, total_gs = lax.fori_loop(0, BLOCKS, norm_sums, (zero, zero))
    mean_g = jnp.sum(total_g, axis=1, keepdims=True) * (1.0 / CH)
    mean_gs = jnp.sum(total_gs, axis=1, keepdims=True) * (1.0 / CH)
    inv_std = inv[...]

    def norm_apply(block, carry):
        cs = lanes_at(block)
        grad_hat = own_rows(nv, cs) * gain[0:1, cs]
        grad_conv = inv_std * (grad_hat - mean_g - std[:, cs] * mean_gs)
        gcv[:, cs] = grad_conv
        sm[49:50, cs] = jnp.sum(grad_conv, axis=0, keepdims=True)
        upstream = gout[:, cs].astype(F32)
        scaled = (upstream * lscale[0:1, cs]).astype(BF16).astype(F32)
        sm[52:53, cs] = jnp.sum(scaled, axis=0, keepdims=True)
        return carry

    lax.fori_loop(0, BLOCKS, norm_apply, 0)

    rs_d1.end()
    rs_d2 = RingSum(copies, ring_x, gdv, z * 192, 48, d2b, d2a)
    rs_d2.begin()
    rs_u1.end()
    rs_u2 = RingSum(copies, ring_z, guv, x * 768, 192, u2b, u2a)
    rs_u2.begin()

    def conv_back(block, carry):
        cs = lanes_at(block)
        pixels = tile_rows(img, block)
        upstream = tile_rows(gout, block)
        grads = [gcv[8 * r : 8 * r + 8, cs] for r in range(16)]
        sums = upstream
        for horizontal in range(7):
            moved = [shifted(tile, 3 - horizontal) for tile in grads]
            for vertical in range(7):
                tap = vertical * 7 + horizontal
                weight = jnp.broadcast_to(dww[tap : tap + 1, cs], (8, LANES))
                taps = jnp.zeros((8, LANES), F32)
                for image in range(2):
                    for p in range(8):
                        source = p - (vertical - 3)
                        if 0 <= source < 8:
                            tile = moved[image * 8 + source]
                            sums[image * 8 + p] = sums[image * 8 + p] + tile * weight
                            taps = taps + tile * pixels[image * 8 + p]
                sm[tap : tap + 1, cs] = jnp.sum(taps, axis=0, keepdims=True)
        for r in range(8):
            grad_img[16 * r : 16 * r + 16, cs] = jnp.concatenate(sums[2 * r : 2 * r + 2], axis=0).astype(BF16)
        return carry

    lax.fori_loop(0, BLOCKS, conv_back, 0)

    rs_d2.middle()
    rs_u2.middle()

    rs_b.end()

    def result_block(block, carry):
        cs = lanes_at(block)
        branch = own_rows(bv, cs) + bdown[0:1, cs]
        upstream = gout[:, cs].astype(F32)
        sm[53:54, cs] = jnp.sum(upstream * branch, axis=0, keepdims=True)
        out_img[:, cs] = (img[:, cs].astype(F32) + lscale[0:1, cs] * branch).astype(BF16)
        return carry

    lax.fori_loop(0, BLOCKS, result_block, 0)

    sm[54:64, :] = jnp.zeros((10, CH), F32)
    for s in range(2):
        shard = y * 2 + (me.x_hi if s == 0 else 1 - me.x_hi)
        for line in range(2):

            @pl.when(lax.div(shard, 4) == line)
            def _(s=s, line=line):
                at = pl.ds(pl.multiple_of(lax.rem(shard, 4) * HID, LANES), HID)
                sm[54 + line : 55 + line, at] = pbias[s : s + 1, :]

    swap_small = copies.push(sm.at[pl.ds(pl.multiple_of(me.other_core * 32, 8), 32)], smc, mate)

    rs_d2.end()
    rs_u2.end()
    at_d = z * 192 + x * 48
    at_u = x * 768 + z * 192
    fd[...] = (gdv[rows_at(at_d, 48), :].astype(F32) * factor).astype(BF16)
    fu[...] = (guv[rows_at(at_u, 192), :].astype(F32) * factor).astype(BF16)
    needed = me.x_hi == me.core

    zr, zl = ring_z[0], ring_z[1]

    def slot(which):
        return rows_at(which * 192, 192)

    tq_own = copies.here(fu, tq.at[slot(z)])
    up_one = [copies.push(fu, tq.at[slot(z)], zr), copies.push(fu, tq.at[slot(z)], zl)]

    def drow(which_x, which_z=None):
        return rows_at((z if which_z is None else which_z) * 192 + which_x * 48, 48)

    d_cut = copies.remote(fd, out_down.at[drow(x)], x_cut)
    d_swap = copies.remote(fd, out_down.at[drow(x)], x_pair)
    d_cut_swap = copies.remote(out_down.at[drow(me.x_cut)], out_down.at[drow(me.x_cut)], x_pair)

    @pl.when(jnp.logical_not(needed))
    def _():
        d_cut.start()

    d_own = pltpu.make_async_copy(fd, out_down.at[drow(x)], local.at[20])

    @pl.when(needed)
    def _():
        d_own.start()
        d_swap.start()

    small_rows = me.core * 32
    swap_small.wait_recv()
    sm_at = pl.ds(pl.multiple_of(small_rows, 8), 32)
    sm[sm_at, :] = sm[sm_at, :] + smc[...]

    yr, yl, yy, y_right, y_left, y_far = ring_y

    def small_piece(which):
        return pl.ds(pl.multiple_of(small_rows + which * 8, 8), 8)

    h = CH // 2
    s_one = [
        copies.push(sm.at[small_piece(y_far), pl.ds(0, h)], sya.at[0], yr),
        copies.push(sm.at[small_piece(y_far), pl.ds(h, h)], sya.at[1], yl),
    ]

    up_one[0].wait_recv()
    z_left_slot, z_right_slot = slot(z_left), slot(z_right)
    hu = HID // 2
    up_two = [copies.push(tq.at[z_left_slot, pl.ds(0, hu)], tq.at[z_left_slot, pl.ds(0, hu)], zr)]
    up_one[1].wait_recv()
    up_two.append(copies.push(tq.at[z_right_slot, pl.ds(hu, hu)], tq.at[z_right_slot, pl.ds(hu, hu)], zl))

    s_two = []
    for side, (device, which) in enumerate(((yr, y_right), (yl, y_left))):
        s_one[side].wait_recv()
        at = small_piece(which)
        sm[at, pl.ds(side * h, h)] = sm[at, pl.ds(side * h, h)] + sya[side]
        s_two.append(copies.push(sm.at[at], syb.at[side], device))

    @pl.when(needed)
    def _():
        d_cut.wait_recv()
        d_cut_swap.start()

    for side in range(2):
        s_two[side].wait_recv()
    at = small_piece(yy)
    sx[pl.ds(x, 1)] = (sm[at, :] + syb[0] + syb[1])[None]

    def small_all(buffer, ring):
        to_right, to_left, where, _, at_left, _ = ring[0], ring[1], ring[2], ring[3], ring[4], ring[5]
        at_right = ring[3]
        one = [
            copies.push(buffer.at[where], buffer.at[where], to_right),
            copies.push(buffer.at[where], buffer.at[where], to_left),
        ]
        one[0].wait_recv()
        lo, hi = pl.ds(0, h), pl.ds(h, h)
        two = [copies.push(buffer.at[at_left, :, lo], buffer.at[at_left, :, lo], to_right)]
        one[1].wait_recv()
        two.append(copies.push(buffer.at[at_right, :, hi], buffer.at[at_right, :, hi], to_left))
        for copy in two:
            copy.wait_recv()
        return buffer[0] + buffer[1] + buffer[2] + buffer[3]

    sz[pl.ds(z, 1)] = small_all(sx, ring_x)[None]

    for copy in up_two:
        copy.wait_recv()
    tq_own.wait()

    def urow(which_x):
        return rows_at(which_x * 768, 768)

    u_cut = copies.remote(tq, out_up.at[urow(x)], x_cut)
    u_swap = copies.remote(tq, out_up.at[urow(x)], x_pair)
    u_mate = copies.remote(tq, out_up.at[urow(x)], mate)
    u_own = pltpu.make_async_copy(tq, out_up.at[urow(x)], local.at[21])

    @pl.when(jnp.logical_not(needed))
    def _():
        u_cut.start()

    @pl.when(needed)
    def _():
        u_swap.start()
        u_mate.start()
        u_own.start()

    total = small_all(sz, ring_z)
    smo_at = small_piece(yy)
    smo[smo_at, :] = total * factor

    def small_back():
        one = [
            copies.push(smo.at[smo_at], smo.at[smo_at], yr),
            copies.push(smo.at[smo_at], smo.at[smo_at], yl),
        ]
        lo, hi = pl.ds(0, h), pl.ds(h, h)
        from_left, from_right = small_piece(y_left), small_piece(y_right)
        one[0].wait_recv()
        two = [copies.push(smo.at[from_left, lo], smo.at[from_left, lo], yr)]
        one[1].wait_recv()
        two.append(copies.push(smo.at[from_right, hi], smo.at[from_right, hi], yl))
        for copy in two:
            copy.wait_recv()
        return copies.push(smo.at[sm_at], smo.at[sm_at], mate)

    small_mate = small_back()

    def dblock(which):
        return rows_at(which * 192, 192)

    hd = CH // 2
    lo, hi = pl.ds(0, hd), pl.ds(hd, hd)
    block, block_l, block_r, block_f = dblock(z), dblock(z_left), dblock(z_right), dblock(z_far)
    d_right = copies.remote(out_down.at[block], out_down.at[block], zr)
    d_left = copies.remote(out_down.at[block], out_down.at[block], zl)
    d_mate = copies.remote(out_down.at[block], out_down.at[block], mate)
    d_fwd_right = copies.remote(out_down.at[block_l, lo], out_down.at[block_l, lo], zr)
    d_fwd_left = copies.remote(out_down.at[block_r, hi], out_down.at[block_r, hi], zl)
    d_mate_l = copies.remote(out_down.at[block_l], out_down.at[block_l], mate)
    d_mate_r = copies.remote(out_down.at[block_r], out_down.at[block_r], mate)
    d_mate_f = copies.remote(out_down.at[block_f], out_down.at[block_f], mate)
    q_cut, q_pair, q_far = urow(me.x_cut), urow(me.x_pair), urow(3 - me.x_pair)
    u_cut_swap = copies.remote(out_up.at[q_cut], out_up.at[q_cut], x_pair)
    u_mate_c = copies.remote(out_up.at[q_cut], out_up.at[q_cut], mate)
    u_mate_p = copies.remote(out_up.at[q_pair], out_up.at[q_pair], mate)
    u_mate_f = copies.remote(out_up.at[q_far], out_up.at[q_far], mate)

    @pl.when(needed)
    def _():
        d_own.wait()
        d_swap.wait_recv()
        d_cut_swap.wait_recv()
        d_right.start()
        d_left.start()
        d_mate.start()
        u_cut.wait_recv()
        u_cut_swap.start()
        u_mate_c.start()
        d_right.wait_recv()
        d_fwd_right.start()
        d_mate_l.start()
        d_left.wait_recv()
        d_fwd_left.start()
        d_mate_r.start()
        u_swap.wait_recv()
        u_mate_p.start()
        d_fwd_right.wait_recv()
        d_fwd_left.wait_recv()
        d_mate_f.start()
        u_cut_swap.wait_recv()
        u_mate_f.start()
        u_own.wait()
        for copy in (
            d_swap, d_cut_swap, d_right, d_left, d_mate, d_fwd_right, d_fwd_left, d_mate_l, d_mate_r, d_mate_f,
            u_swap, u_mate, u_cut_swap, u_mate_c, u_mate_p, u_mate_f,
        ):
            copy.wait_send()

    @pl.when(jnp.logical_not(needed))
    def _():
        for copy in (d_mate, d_mate_l, d_mate_r, d_mate_f, u_mate, u_mate_c, u_mate_p, u_mate_f):
            copy.wait_recv()
        d_cut.wait_send()
        u_cut.wait_send()

    small_mate.wait_recv()
    out_small[...] = smo[...]
    copies.drain()


def second_call(*operands):
    remote = 80
    bf = lambda *shape: pltpu.VMEM(shape, BF16)
    fl = lambda *shape: pltpu.VMEM(shape, F32)
    return pl.pallas_call(
        second_kernel,
        out_shape=(
            jax.ShapeDtypeStruct((ROWS, CH), BF16),
            jax.ShapeDtypeStruct((ROWS, CH), BF16),
            jax.ShapeDtypeStruct((CH, HID), BF16),
            jax.ShapeDtypeStruct((HID, CH), BF16),
            jax.ShapeDtypeStruct((64, CH), F32),
        ),
        in_specs=[ANY] * 4 + [VMEM] * 9,
        out_specs=(VMEM, VMEM, ANY, ANY, VMEM),
        scratch_shapes=[
            bf(CH, HID), bf(HID, CH), bf(CH, HID), bf(HID, CH),
            bf(2, 192, 1536), bf(2, 192, 3072), bf(2, 768, 384), bf(2, 768, 768),
            bf(2, 48, 1536), bf(2, 48, 3072), bf(2, 192, 384), bf(2, 192, 768),
            bf(768, 768), bf(48, 3072), bf(192, 768),
            bf(512, CH), bf(512, CH),
            bf(2, 128, 1536), bf(2, 128, 3072), bf(2, 128, 1536), bf(2, 128, 3072),
            fl(ROWS, CH), fl(64, CH), fl(32, CH), fl(2, 8, 1536), fl(2, 8, CH),
            fl(4, 8, CH), fl(4, 8, CH), fl(64, CH),
            pltpu.SemaphoreType.DMA((remote,)),
            pltpu.SemaphoreType.DMA((remote,)),
            pltpu.SemaphoreType.DMA((24,)),
        ],
        compiler_params=pltpu.CompilerParams(
            collective_id=1, has_side_effects=True, vmem_limit_bytes=60 * 1024 * 1024
        ),
    )(*operands)


def gelu_exact(values):
    return 0.5 * values * (1.0 + lax.erf(values * 0.7071067811865476))


def gelu_slope(values):
    return (
        0.5 * (1.0 + lax.erf(values * 0.7071067811865476))
        + values * jnp.exp(-0.5 * values * values) * 0.3989422804014327
    )


def mlp(gn, gs, shards):
    nt = (((1,), (1,)), ((), ()))
    tn = (((0,), (0,)), ((), ()))
    branch = normed = 0.0
    ups, downs, biases = [], [], []
    for wu, wd, bu in shards:
        pre_up = jnp.dot(gn, wu, preferred_element_type=F32) + bu
        hidden = gelu_exact(pre_up).astype(BF16)
        grad_hidden = lax.dot_general(gs, wd, nt, preferred_element_type=F32)
        grad_pre = (grad_hidden * gelu_slope(pre_up)).astype(BF16)
        biases.append(jnp.sum(grad_pre, axis=0, dtype=F32))
        branch = branch + jnp.dot(hidden, wd, preferred_element_type=F32)
        normed = normed + lax.dot_general(grad_pre, wu, nt, preferred_element_type=F32)
        ups.append(lax.dot_general(gn, grad_pre, tn, preferred_element_type=F32).astype(BF16))
        downs.append(lax.dot_general(hidden, gs, tn, preferred_element_type=F32).astype(BF16))
    return normed.astype(BF16), branch.astype(BF16), jnp.stack(ups), jnp.stack(downs), jnp.stack(biases)


def on_device(
    images, grad_out, dw_weight, dw_bias, ln_gain, ln_bias, w_up, b_up, w_down, b_down, layer_scale
):
    img = images.reshape(ROWS, CH)
    gout = grad_out.reshape(ROWS, CH)
    dww = dw_weight.reshape(49, CH)
    row = lambda vector: vector.reshape(1, CH)
    bu = jnp.pad(b_up.reshape(6, LANES), ((0, 2), (0, 0)))
    gn, gs, std, inv, wuo, wdo, buo = first_call(
        img, gout, dww, row(dw_bias), row(ln_gain), row(ln_bias), row(layer_scale), w_up, w_down, bu
    )
    b_other = buo[:6].reshape(HID)
    pn, pb, gu, gd, pbias = mlp(
        gn.reshape(4 * ROWS, CH), gs.reshape(4 * ROWS, CH), ((w_up, w_down, b_up), (wuo, wdo, b_other))
    )
    out_img, grad_img, out_up, out_down, small = second_call(
        pn, pb, gu, gd, img, gout, std, inv, dww, row(ln_gain), row(layer_scale), row(b_down), pbias
    )
    shard = lax.axis_index("fsdp")
    grad_b_up = lax.dynamic_slice(small[54:56].reshape(-1), (shard * HID,), (HID,)).astype(BF16)
    return (
        out_img.reshape(images.shape),
        grad_img.reshape(images.shape),
        out_up,
        grad_b_up,
        out_down,
        small[:49].reshape(dw_weight.shape),
        small[49],
        small[50],
        small[51],
        small[52],
        small[53],
    )


def solution(mesh):
    tokens = P(("dp", "fsdp"), None, None, None)
    up, bias, down = P(None, "fsdp"), P("fsdp"), P("fsdp", None)
    return jax.shard_map(
        on_device,
        mesh=mesh,
        in_specs=(tokens, tokens, P(), P(), P(), P(), up, bias, down, P(), P()),
        out_specs=(tokens, tokens, up, bias, down, P(), P(), P(), P(), P(), P()),
        check_vma=False,
    )
```

```python
import math

import jax
import jax.numpy as jnp
from jax import lax
from jax.experimental import pallas as pl
from jax.experimental.pallas import tpu as pltpu
from jax.sharding import PartitionSpec as P

MESH = pl.DeviceIdType.MESH
F32 = jnp.float32
BF16 = jnp.bfloat16
CH = 3072
HID = 768
ROWS = 128
LANES = 128
BLOCKS = CH // LANES
ANY = pl.BlockSpec(memory_space=pl.ANY)
VMEM = pl.BlockSpec(memory_space=pltpu.VMEM)


class Place:
    def __init__(self):
        d = lax.axis_index("dp")
        f = lax.axis_index("fsdp")
        self.z = lax.div(d, 4)
        self.x_lo = lax.rem(lax.div(d, 2), 2)
        self.core = lax.rem(d, 2)
        self.y = lax.div(f, 2)
        self.x_hi = lax.rem(f, 2)
        self.x = self.x_hi * 2 + self.x_lo
        self.other_core = 1 - self.core
        self.x_cut = 3 - self.x
        self.x_pair = self.x_hi * 2 + (1 - self.x_lo)

    def at(self, x=None, y=None, z=None, core=None):
        x = self.x if x is None else x
        y = self.y if y is None else y
        z = self.z if z is None else z
        core = self.core if core is None else core
        return (z * 4 + lax.rem(x, 2) * 2 + core, y * 2 + lax.div(x, 2))

    def ring(self, axis):
        me = getattr(self, axis)
        right, left, far = lax.rem(me + 1, 4), lax.rem(me + 3, 4), lax.rem(me + 2, 4)
        return self.at(**{axis: right}), self.at(**{axis: left}), me, right, left, far


class Copies:
    def __init__(self, send, recv, local):
        self.send, self.recv, self.local = send, recv, local
        self.used = 0
        self.used_local = 0
        self.sent = []

    def remote(self, src, dst, device):
        index = self.used
        self.used += 1
        return pltpu.make_async_remote_copy(
            src_ref=src,
            dst_ref=dst,
            send_sem=self.send.at[index],
            recv_sem=self.recv.at[index],
            device_id=device,
            device_id_type=MESH,
        )

    def push(self, src, dst, device):
        copy = self.remote(src, dst, device)
        copy.start()
        self.sent.append(copy)
        return copy

    def here(self, src, dst):
        index = self.used_local
        self.used_local += 1
        copy = pltpu.make_async_copy(src, dst, self.local.at[index])
        copy.start()
        return copy

    def drain(self):
        for copy in self.sent:
            copy.wait_send()


def greet(devices):
    barrier = pltpu.get_barrier_semaphore()
    for device in devices:
        pl.semaphore_signal(barrier, inc=1, device_id=device, device_id_type=MESH)
    pl.semaphore_wait(barrier, len(devices))


def rows_at(start, size):
    return pl.ds(pl.multiple_of(start, 16), size)


def lanes_at(block):
    return pl.ds(pl.multiple_of(block * LANES, LANES), LANES)


def shifted(row, by):
    if by == 0:
        return row
    moved = pltpu.roll(row, (-by) % 8, 0)
    place = lax.broadcasted_iota(jnp.int32, row.shape, 0)
    inside = (place + by >= 0) & (place + by < 8)
    return jnp.where(inside, moved, 0.0)


def tile_rows(ref, block):
    tiles = []
    for pair in range(8):
        both = ref[16 * pair : 16 * pair + 16, lanes_at(block)].astype(F32)
        tiles += [both[:8], both[8:]]
    return tiles


def conv_block(block, img, dww, dwb, out):
    pixels = tile_rows(img, block)
    cs = lanes_at(block)
    sums = [jnp.broadcast_to(dwb[0:1, cs], (8, LANES))] * 16
    for horizontal in range(7):
        moved = [shifted(tile, horizontal - 3) for tile in pixels]
        for vertical in range(7):
            tap = vertical * 7 + horizontal
            weight = jnp.broadcast_to(dww[tap : tap + 1, cs], (8, LANES))
            for image in range(2):
                for p in range(8):
                    source = p + vertical - 3
                    if 0 <= source < 8:
                        sums[image * 8 + p] = sums[image * 8 + p] + moved[image * 8 + source] * weight
    for r in range(16):
        out[8 * r : 8 * r + 8, cs] = sums[r]


def gelu_parts(values):
    cdf = 0.5 * (1.0 + lax.erf(values * 0.7071067811865476))
    return values * cdf, cdf + values * jnp.exp(-0.5 * values * values) * 0.3989422804014327


NT = (((1,), (1,)), ((), ()))
TN = (((0,), (0,)), ((), ()))


def first_kernel(
    img, gout, dww, dwb, gain, shift, lscale, wu, wd, bu,
    std, inv, pn, pb, keep_up, keep_down, got_up, got_down, bias_sums,
    gn, gs, wuv, wdv, bo, hid, gp, keep32, pnv, pbv, up_v, down_v,
    send, recv, local,
):
    me = Place()
    copies = Copies(send, recv, local)
    right, left, y, y_right, y_left, y_far = me.ring("y")
    cut = me.at(x=me.x_cut)
    pair = me.at(x=me.x_pair)
    mate = me.at(core=me.other_core)
    wu_load = copies.here(wu, wuv.at[0])
    wd_load = copies.here(wd, wdv.at[0])
    greet([right, left, cut, pair, mate])

    up_rows, down_rows, parts = 192, 48, 4
    theirs = (1 - me.x_lo) * 2 + me.core
    mine = me.x_lo * 2 + me.core
    pairs = (1 - me.x_lo) * 2 + me.core
    weights = (wuv.at[1], wdv.at[1])

    def chunk(matrix, quarter, part):
        size = up_rows if matrix == 0 else down_rows
        return rows_at(quarter * (size * parts) + part * size, size)

    order = [(m, k) for m in range(2) for k in range(parts)]
    bias = copies.push(bu, bo, cut)
    over_cut = []
    for m, k in order:
        at = chunk(m, theirs, k)
        over_cut.append(copies.push((wu, wd)[m].at[at], weights[m].at[at], cut))

    own = rows_at(y * ROWS, ROWS)

    def scale_block(block, carry):
        cs = lanes_at(block)
        gs[own, cs] = (gout[:, cs].astype(F32) * lscale[0:1, cs]).astype(BF16)
        return carry

    lax.fori_loop(0, BLOCKS, scale_block, 0)

    half = ROWS // 2

    def halves(position):
        return rows_at(position * ROWS, half), rows_at(position * ROWS + half, half)

    def spread(buffer):
        low, high = halves(y)
        first = [copies.push(buffer.at[low], buffer.at[low], right), copies.push(buffer.at[high], buffer.at[high], left)]
        second = [copies.push(buffer.at[high], buffer.at[high], right), copies.push(buffer.at[low], buffer.at[low], left)]
        return first, second

    def forward(first, buffer):
        low, high = halves(y_left)[0], halves(y_right)[1]
        first[0].wait_recv()
        to_right = copies.push(buffer.at[low], buffer.at[low], right)
        first[1].wait_recv()
        to_left = copies.push(buffer.at[high], buffer.at[high], left)
        return [to_right, to_left]

    relayed, last = {}, {}

    def relay(index):
        m, k = order[index]
        over_cut[index].wait_recv()
        at = chunk(m, mine, k)
        ref = weights[m].at[at]
        relayed[index] = copies.push(ref, ref, pair), copies.push(ref, ref, mate)

    def relay_pair(index):
        m, k = order[index]
        relayed[index][0].wait_recv()
        at = chunk(m, pairs, k)
        ref = weights[m].at[at]
        last[index] = copies.push(ref, ref, mate)

    def arrived(indices):
        for index in indices:
            relayed[index][1].wait_recv()
            last[index].wait_recv()

    s_first, s_second = spread(gs)

    def conv_step(block, carry):
        conv_block(block, img, dww, dwb, std)
        return carry

    lax.fori_loop(0, BLOCKS // 2, conv_step, 0)
    relay(0)
    lax.fori_loop(BLOCKS // 2, BLOCKS, conv_step, 0)

    def add_block(block, total):
        return total + std[:, lanes_at(block)]

    zero = jnp.zeros((ROWS, LANES), F32)
    mean = jnp.sum(lax.fori_loop(0, BLOCKS, add_block, zero), axis=1, keepdims=True) * (1.0 / CH)

    def square_block(block, total):
        centred = std[:, lanes_at(block)] - mean
        return total + centred * centred

    variance = jnp.sum(lax.fori_loop(0, BLOCKS, square_block, zero), axis=1, keepdims=True) * (1.0 / CH)
    inv_std = lax.rsqrt(variance + 1e-06)
    inv[...] = jnp.broadcast_to(inv_std, (ROWS, LANES))

    def norm_block(block, carry):
        cs = lanes_at(block)
        standard = (std[:, cs] - mean) * inv_std
        std[:, cs] = standard
        gn[own, cs] = (standard * gain[0:1, cs] + shift[0:1, cs]).astype(BF16)
        return carry

    lax.fori_loop(0, BLOCKS, norm_block, 0)
    n_first, n_second = spread(gn)
    relay(1)
    s_last = forward(s_first, gs)

    tile = 256

    def hidden_tile(index):
        return pl.ds(pl.multiple_of(index * tile, tile), tile)

    bias_sums[...] = jnp.zeros_like(bias_sums)

    def up_rows_of(s, position):
        at = rows_at(position * ROWS, ROWS)

        def body(index, carry):
            cs = hidden_tile(index)
            pre = jnp.dot(gn[at, :], wuv[s, :, cs], preferred_element_type=F32)
            value, slope = gelu_parts(pre + (bu if s == 0 else bo)[0:1, cs])
            hid[s, at, cs] = value.astype(BF16)
            keep32[s, at, cs] = slope
            return carry

        lax.fori_loop(0, HID // tile, body, 0)

    def grad_of(s):
        def body(index, carry):
            cs = hidden_tile(index)
            grad = lax.dot_general(gs[...], wdv[s, cs, :], NT, preferred_element_type=F32)
            pre = (grad * keep32[s, :, cs]).astype(BF16)
            gp[s, :, cs] = pre
            bias_sums[s : s + 1, cs] = jnp.sum(pre.astype(F32), axis=0, keepdims=True)
            return carry

        lax.fori_loop(0, HID // tile, body, 0)

    keep = lax.rem(me.x_hi + me.core, 2)
    moves = {}

    def place(matrix, s, part):
        if matrix == 0:
            at = (pl.ds(part * 768, 768), slice(None))
            mine, there, ref = keep_up, got_up, up_v
        else:
            at = (slice(None), pl.ds(part * 768, 768))
            mine, there, ref = keep_down, got_down, down_v
        if (matrix, part) not in moves:
            index = copies.used_local
            copies.used_local += 1
            moves[matrix, part] = (
                copies.remote(ref.at[at], there.at[at], mate),
                pltpu.make_async_copy(ref.at[at], mine.at[at], local.at[index]),
            )
        away, stay = moves[matrix, part]

        @pl.when(keep != s)
        def _():
            away.start()

        @pl.when(keep == s)
        def _():
            stay.start()

    def placed(matrix, s, part):
        away, stay = moves[matrix, part]

        @pl.when(keep != s)
        def _():
            away.wait_send()

        @pl.when(keep == s)
        def _():
            stay.wait()

    def part_up(s):
        for part in range(4):
            if s == 1:
                placed(0, 0, part)

            def body(index, carry, part=part):
                rows = pl.ds(pl.multiple_of(part * 768 + index * tile, tile), tile)
                up_v[rows, :] = lax.dot_general(gn[:, rows], gp[s], TN, preferred_element_type=F32).astype(BF16)
                return carry

            lax.fori_loop(0, 768 // tile, body, 0)
            place(0, s, part)

    def part_down(s):
        for part in range(4):
            if s == 1:
                placed(1, 0, part)

            def body(index, carry, part=part):
                cs = pl.ds(pl.multiple_of(part * 768 + index * tile, tile), tile)
                down_v[:, cs] = lax.dot_general(hid[s], gs[:, cs], TN, preferred_element_type=F32).astype(BF16)
                return carry

            lax.fori_loop(0, 768 // tile, body, 0)
            place(1, s, part)

    wu_load.wait()
    relay(2)
    relay_pair(0)
    up_rows_of(0, y)
    relay_pair(1)
    relay(3)
    relay_pair(2)
    n_last = forward(n_first, gn)
    relay(4)
    relay_pair(3)
    for copy in n_second:
        copy.wait_recv()
    up_rows_of(0, y_right)
    up_rows_of(0, y_left)
    relay(5)
    relay_pair(4)
    bias.wait_recv()
    arrived(range(4))
    up_rows_of(1, y)
    up_rows_of(1, y_right)
    relay(6)
    relay_pair(5)
    up_rows_of(1, y_left)
    wd_load.wait()
    for copy in s_second + s_last:
        copy.wait_recv()
    relay(7)
    relay_pair(6)
    for copy in n_last:
        copy.wait_recv()
    up_rows_of(0, y_far)
    relay_pair(7)
    grad_of(0)
    up_rows_of(1, y_far)
    part_up(0)
    part_down(0)
    arrived(range(4, 8))
    grad_of(1)
    part_up(1)
    part_down(1)

    def normed_back(index, carry):
        cs = pl.ds(pl.multiple_of(index * tile, tile), tile)
        total = lax.dot_general(gp[0], wuv[0, cs, :], NT, preferred_element_type=F32)
        total = total + lax.dot_general(gp[1], wuv[1, cs, :], NT, preferred_element_type=F32)
        pnv[:, cs] = total.astype(BF16)
        return carry

    lax.fori_loop(0, CH // tile, normed_back, 0)
    pn_out = copies.here(pnv, pn)

    def branch_tile(index, carry):
        cs = pl.ds(pl.multiple_of(index * tile, tile), tile)
        total = jnp.dot(hid[0], wdv[0, :, cs], preferred_element_type=F32)
        total = total + jnp.dot(hid[1], wdv[1, :, cs], preferred_element_type=F32)
        pbv[:, cs] = total.astype(BF16)
        return carry

    lax.fori_loop(0, CH // tile, branch_tile, 0)
    pb_out = copies.here(pbv, pb)

    pn_out.wait()
    pb_out.wait()
    for matrix in range(2):
        for part in range(4):
            placed(matrix, 1, part)
            moves[matrix, part][0].wait_recv()
    copies.drain()


def first_call(img, gout, dww, dwb, gain, shift, lscale, wu, wd, bu):
    remote = 56
    rows = 4 * ROWS
    return pl.pallas_call(
        first_kernel,
        out_shape=(
            jax.ShapeDtypeStruct((ROWS, CH), F32),
            jax.ShapeDtypeStruct((ROWS, LANES), F32),
            jax.ShapeDtypeStruct((rows, CH), BF16),
            jax.ShapeDtypeStruct((rows, CH), BF16),
            jax.ShapeDtypeStruct((CH, HID), BF16),
            jax.ShapeDtypeStruct((HID, CH), BF16),
            jax.ShapeDtypeStruct((CH, HID), BF16),
            jax.ShapeDtypeStruct((HID, CH), BF16),
            jax.ShapeDtypeStruct((8, HID), F32),
        ),
        in_specs=[VMEM] * 7 + [ANY, ANY, VMEM],
        out_specs=(VMEM, VMEM, ANY, ANY, ANY, ANY, ANY, ANY, VMEM),
        scratch_shapes=[
            pltpu.VMEM((rows, CH), BF16),
            pltpu.VMEM((rows, CH), BF16),
            pltpu.VMEM((2, CH, HID), BF16),
            pltpu.VMEM((2, HID, CH), BF16),
            pltpu.VMEM((8, HID), F32),
            pltpu.VMEM((2, rows, HID), BF16),
            pltpu.VMEM((2, rows, HID), BF16),
            pltpu.VMEM((2, rows, HID), F32),
            pltpu.VMEM((rows, CH), BF16),
            pltpu.VMEM((rows, CH), BF16),
            pltpu.VMEM((CH, HID), BF16),
            pltpu.VMEM((HID, CH), BF16),
            pltpu.SemaphoreType.DMA((remote,)),
            pltpu.SemaphoreType.DMA((remote,)),
            pltpu.SemaphoreType.DMA((12,)),
        ],
        compiler_params=pltpu.CompilerParams(
            collective_id=0, has_side_effects=True, vmem_limit_bytes=62 * 1024 * 1024
        ),
    )(img, gout, dww, dwb, gain, shift, lscale, wu, wd, bu)


def add_rows(dst, dst_row, sources, rows, column, columns, step=16):
    def body(index, carry):
        at = rows_at(dst_row + index * step, step)
        cs = pl.ds(column, columns)
        total = dst[at, cs].astype(F32)
        for ref, row, first in sources:
            total = total + ref[rows_at(row + index * step, step), pl.ds(first, columns)].astype(F32)
        dst[at, cs] = total.astype(dst.dtype)
        return carry

    lax.fori_loop(0, rows // step, body, 0)


class RingSum:
    def __init__(self, copies, where, data, base, rows, near, far, step=16):
        self.copies, self.data, self.base, self.rows = copies, data, base, rows
        self.right, self.left, self.me, self.at_right, self.at_left, self.at_far = where
        self.near, self.far, self.step = near, far, step
        self.half = data.shape[1] // 2

    def block(self, which):
        return self.base + which * self.rows

    def begin(self):
        at = rows_at(self.block(self.at_far), self.rows) if self.step == 16 else pl.ds(self.block(self.at_far), self.rows)
        h = self.half
        self.one = [
            self.copies.push(self.data.at[at, pl.ds(0, h)], self.far.at[0], self.right),
            self.copies.push(self.data.at[at, pl.ds(h, h)], self.far.at[1], self.left),
        ]

    def middle(self):
        h = self.half
        self.two = []
        for side, (device, block) in enumerate(((self.right, self.at_right), (self.left, self.at_left))):
            self.one[side].wait_recv()
            start = self.block(block)
            add_rows(self.data, start, [(self.far.at[side], 0, 0)], self.rows, side * h, h, self.step)
            at = rows_at(start, self.rows)
            self.two.append(self.copies.push(self.data.at[at], self.near.at[side], device))

    def end(self):
        for copy in self.two:
            copy.wait_recv()
        add_rows(
            self.data,
            self.block(self.me),
            [(self.near.at[0], 0, 0), (self.near.at[1], 0, 0)],
            self.rows,
            0,
            2 * self.half,
            self.step,
        )


def small_add(dst, row, sources, rows):
    total = dst[row, :]
    for source in sources:
        total = total + source
    dst[row, :] = total


def second_kernel(
    pn, pb, gu, gd, ru, rd, img, gout, std, inv, dww, gain, lscale, bdown, pbias,
    out_img, grad_img, out_up, out_down, out_small,
    guv, gdv, cu, cd, d1a, d1b, u1a, u1b, d2a, d2b, u2a, u2b, tq, fd, fu,
    nv, bv, n1, n2, b1, b2, gcv, sm, smc, sya, syb, sx, sz, smo,
    send, recv, local,
):
    me = Place()
    copies = Copies(send, recv, local)
    ring_x, ring_y, ring_z = me.ring("x"), me.ring("y"), me.ring("z")
    mate = me.at(core=me.other_core)
    x_cut = me.at(x=me.x_cut)
    x_pair = me.at(x=me.x_pair)
    greet([ring_x[0], ring_x[1], ring_y[0], ring_y[1], ring_z[0], ring_z[1], mate])
    x, y, z = me.x, me.y, me.z
    factor = 1.0 / math.sqrt(16384.0)

    z_far, z_right, z_left = ring_z[5], ring_z[3], ring_z[4]
    x_far, x_right, x_left = ring_x[5], ring_x[3], ring_x[4]
    order = [(0, z_far), (1, x_far), (0, z_right), (1, x_right), (0, z_left), (1, x_left), (0, z), (1, x)]
    swaps, loads = [], []

    def piece(matrix, which):
        return rows_at(which * 192, 192) if matrix == 0 else rows_at(which * 768, 768)

    for m, which in order:
        src, got, dst, mine = ((gd, rd, cd, gdv), (gu, ru, cu, guv))[m]
        at = piece(m, which)
        swaps.append(copies.here(got.at[at], dst.at[at]))
        loads.append(copies.here(src.at[at], mine.at[at]))

    y_far = ring_y[5]
    load_n = copies.here(pn, nv)
    load_b = copies.here(pb, bv)
    load_n.wait()
    rs_n = RingSum(copies, ring_y, nv, 0, ROWS, n2, n1)
    rs_n.begin()
    load_b.wait()
    rs_b = RingSum(copies, ring_y, bv, 0, ROWS, b2, b1)

    def merge(index):
        m, which = order[index]
        mine, other = ((gdv, cd), (guv, cu))[m]
        rows = 192 if m == 0 else 768
        loads[index].wait()
        swaps[index].wait()
        add_rows(mine, which * rows, [(other, which * rows, 0)], rows, 0, mine.shape[1], 16 if m == 0 else 64)

    rs_d1 = RingSum(copies, ring_z, gdv, 0, 192, d1b, d1a)
    rs_u1 = RingSum(copies, ring_x, guv, 0, 768, u1b, u1a)
    merge(0)
    rs_d1.begin()
    merge(1)
    rs_u1.begin()
    rs_b.begin()
    merge(2)
    merge(3)
    rs_n.middle()
    merge(4)
    merge(5)
    rs_d1.middle()
    rs_u1.middle()
    rs_b.middle()
    merge(6)
    merge(7)

    rs_n.end()
    own = y * ROWS
    zero = jnp.zeros((ROWS, LANES), F32)

    def own_rows(ref, cs):
        return ref[rows_at(own, ROWS), cs].astype(F32)

    def norm_sums(block, totals):
        cs = lanes_at(block)
        grad_normed = own_rows(nv, cs)
        standard = std[:, cs]
        product = grad_normed * standard
        sm[50:51, cs] = jnp.sum(product, axis=0, keepdims=True)
        sm[51:52, cs] = jnp.sum(grad_normed, axis=0, keepdims=True)
        weight = gain[0:1, cs]
        return totals[0] + grad_normed * weight, totals[1] + product * weight

    total_g, total_gs = lax.fori_loop(0, BLOCKS, norm_sums, (zero, zero))
    mean_g = jnp.sum(total_g, axis=1, keepdims=True) * (1.0 / CH)
    mean_gs = jnp.sum(total_gs, axis=1, keepdims=True) * (1.0 / CH)
    inv_std = inv[...]

    def norm_apply(block, carry):
        cs = lanes_at(block)
        grad_hat = own_rows(nv, cs) * gain[0:1, cs]
        grad_conv = inv_std * (grad_hat - mean_g - std[:, cs] * mean_gs)
        gcv[:, cs] = grad_conv
        sm[49:50, cs] = jnp.sum(grad_conv, axis=0, keepdims=True)
        upstream = gout[:, cs].astype(F32)
        scaled = (upstream * lscale[0:1, cs]).astype(BF16).astype(F32)
        sm[52:53, cs] = jnp.sum(scaled, axis=0, keepdims=True)
        return carry

    lax.fori_loop(0, BLOCKS, norm_apply, 0)

    rs_d1.end()
    rs_d2 = RingSum(copies, ring_x, gdv, z * 192, 48, d2b, d2a)
    rs_d2.begin()
    rs_u1.end()
    rs_u2 = RingSum(copies, ring_z, guv, x * 768, 192, u2b, u2a)
    rs_u2.begin()

    def conv_back(block, carry):
        cs = lanes_at(block)
        pixels = tile_rows(img, block)
        upstream = tile_rows(gout, block)
        grads = [gcv[8 * r : 8 * r + 8, cs] for r in range(16)]
        sums = upstream
        for horizontal in range(7):
            moved = [shifted(tile, 3 - horizontal) for tile in grads]
            for vertical in range(7):
                tap = vertical * 7 + horizontal
                weight = jnp.broadcast_to(dww[tap : tap + 1, cs], (8, LANES))
                taps = jnp.zeros((8, LANES), F32)
                for image in range(2):
                    for p in range(8):
                        source = p - (vertical - 3)
                        if 0 <= source < 8:
                            tile = moved[image * 8 + source]
                            sums[image * 8 + p] = sums[image * 8 + p] + tile * weight
                            taps = taps + tile * pixels[image * 8 + p]
                sm[tap : tap + 1, cs] = jnp.sum(taps, axis=0, keepdims=True)
        for r in range(8):
            grad_img[16 * r : 16 * r + 16, cs] = jnp.concatenate(sums[2 * r : 2 * r + 2], axis=0).astype(BF16)
        return carry

    lax.fori_loop(0, BLOCKS, conv_back, 0)

    rs_d2.middle()
    rs_u2.middle()

    rs_b.end()

    def result_block(block, carry):
        cs = lanes_at(block)
        branch = own_rows(bv, cs) + bdown[0:1, cs]
        upstream = gout[:, cs].astype(F32)
        sm[53:54, cs] = jnp.sum(upstream * branch, axis=0, keepdims=True)
        out_img[:, cs] = (img[:, cs].astype(F32) + lscale[0:1, cs] * branch).astype(BF16)
        return carry

    lax.fori_loop(0, BLOCKS, result_block, 0)

    sm[54:64, :] = jnp.zeros((10, CH), F32)
    for s in range(2):
        shard = y * 2 + (me.x_hi if s == 0 else 1 - me.x_hi)
        for line in range(2):

            @pl.when(lax.div(shard, 4) == line)
            def _(s=s, line=line):
                at = pl.ds(pl.multiple_of(lax.rem(shard, 4) * HID, LANES), HID)
                sm[54 + line : 55 + line, at] = pbias[s : s + 1, :]

    swap_small = copies.push(sm.at[pl.ds(pl.multiple_of(me.other_core * 32, 8), 32)], smc, mate)

    rs_d2.end()
    rs_u2.end()
    at_d = z * 192 + x * 48
    at_u = x * 768 + z * 192
    fd[...] = (gdv[rows_at(at_d, 48), :].astype(F32) * factor).astype(BF16)
    fu[...] = (guv[rows_at(at_u, 192), :].astype(F32) * factor).astype(BF16)
    needed = me.x_hi == me.core

    zr, zl = ring_z[0], ring_z[1]

    def slot(which):
        return rows_at(which * 192, 192)

    tq_own = copies.here(fu, tq.at[slot(z)])
    up_one = [copies.push(fu, tq.at[slot(z)], zr), copies.push(fu, tq.at[slot(z)], zl)]

    def drow(which_x, which_z=None):
        return rows_at((z if which_z is None else which_z) * 192 + which_x * 48, 48)

    d_cut = copies.remote(fd, out_down.at[drow(x)], x_cut)
    d_swap = copies.remote(fd, out_down.at[drow(x)], x_pair)
    d_cut_swap = copies.remote(out_down.at[drow(me.x_cut)], out_down.at[drow(me.x_cut)], x_pair)

    @pl.when(jnp.logical_not(needed))
    def _():
        d_cut.start()

    d_own = pltpu.make_async_copy(fd, out_down.at[drow(x)], local.at[30])

    @pl.when(needed)
    def _():
        d_own.start()
        d_swap.start()

    small_rows = me.core * 32
    swap_small.wait_recv()
    sm_at = pl.ds(pl.multiple_of(small_rows, 8), 32)
    sm[sm_at, :] = sm[sm_at, :] + smc[...]

    yr, yl, yy, y_right, y_left, y_far = ring_y

    def small_piece(which):
        return pl.ds(pl.multiple_of(small_rows + which * 8, 8), 8)

    h = CH // 2
    s_one = [
        copies.push(sm.at[small_piece(y_far), pl.ds(0, h)], sya.at[0], yr),
        copies.push(sm.at[small_piece(y_far), pl.ds(h, h)], sya.at[1], yl),
    ]

    up_one[0].wait_recv()
    z_left_slot, z_right_slot = slot(z_left), slot(z_right)
    hu = HID // 2
    up_two = [copies.push(tq.at[z_left_slot, pl.ds(0, hu)], tq.at[z_left_slot, pl.ds(0, hu)], zr)]
    up_one[1].wait_recv()
    up_two.append(copies.push(tq.at[z_right_slot, pl.ds(hu, hu)], tq.at[z_right_slot, pl.ds(hu, hu)], zl))

    s_two = []
    for side, (device, which) in enumerate(((yr, y_right), (yl, y_left))):
        s_one[side].wait_recv()
        at = small_piece(which)
        sm[at, pl.ds(side * h, h)] = sm[at, pl.ds(side * h, h)] + sya[side]
        s_two.append(copies.push(sm.at[at], syb.at[side], device))

    @pl.when(needed)
    def _():
        d_cut.wait_recv()
        d_cut_swap.start()

    for side in range(2):
        s_two[side].wait_recv()
    at = small_piece(yy)
    sx[pl.ds(x, 1)] = (sm[at, :] + syb[0] + syb[1])[None]

    def small_all(buffer, ring):
        to_right, to_left, where, _, at_left, _ = ring[0], ring[1], ring[2], ring[3], ring[4], ring[5]
        at_right = ring[3]
        one = [
            copies.push(buffer.at[where], buffer.at[where], to_right),
            copies.push(buffer.at[where], buffer.at[where], to_left),
        ]
        one[0].wait_recv()
        lo, hi = pl.ds(0, h), pl.ds(h, h)
        two = [copies.push(buffer.at[at_left, :, lo], buffer.at[at_left, :, lo], to_right)]
        one[1].wait_recv()
        two.append(copies.push(buffer.at[at_right, :, hi], buffer.at[at_right, :, hi], to_left))
        for copy in two:
            copy.wait_recv()
        return buffer[0] + buffer[1] + buffer[2] + buffer[3]

    sz[pl.ds(z, 1)] = small_all(sx, ring_x)[None]

    for copy in up_two:
        copy.wait_recv()
    tq_own.wait()

    def urow(which_x):
        return rows_at(which_x * 768, 768)

    u_cut = copies.remote(tq, out_up.at[urow(x)], x_cut)
    u_swap = copies.remote(tq, out_up.at[urow(x)], x_pair)
    u_mate = copies.remote(tq, out_up.at[urow(x)], mate)
    u_own = pltpu.make_async_copy(tq, out_up.at[urow(x)], local.at[31])

    @pl.when(jnp.logical_not(needed))
    def _():
        u_cut.start()

    @pl.when(needed)
    def _():
        u_swap.start()
        u_mate.start()
        u_own.start()

    total = small_all(sz, ring_z)
    smo_at = small_piece(yy)
    smo[smo_at, :] = total * factor

    def small_back():
        one = [
            copies.push(smo.at[smo_at], smo.at[smo_at], yr),
            copies.push(smo.at[smo_at], smo.at[smo_at], yl),
        ]
        lo, hi = pl.ds(0, h), pl.ds(h, h)
        from_left, from_right = small_piece(y_left), small_piece(y_right)
        one[0].wait_recv()
        two = [copies.push(smo.at[from_left, lo], smo.at[from_left, lo], yr)]
        one[1].wait_recv()
        two.append(copies.push(smo.at[from_right, hi], smo.at[from_right, hi], yl))
        for copy in two:
            copy.wait_recv()
        return copies.push(smo.at[sm_at], smo.at[sm_at], mate)

    small_mate = small_back()

    def dblock(which):
        return rows_at(which * 192, 192)

    hd = CH // 2
    lo, hi = pl.ds(0, hd), pl.ds(hd, hd)
    block, block_l, block_r, block_f = dblock(z), dblock(z_left), dblock(z_right), dblock(z_far)
    d_right = copies.remote(out_down.at[block], out_down.at[block], zr)
    d_left = copies.remote(out_down.at[block], out_down.at[block], zl)
    d_mate = copies.remote(out_down.at[block], out_down.at[block], mate)
    d_fwd_right = copies.remote(out_down.at[block_l, lo], out_down.at[block_l, lo], zr)
    d_fwd_left = copies.remote(out_down.at[block_r, hi], out_down.at[block_r, hi], zl)
    d_mate_l = copies.remote(out_down.at[block_l], out_down.at[block_l], mate)
    d_mate_r = copies.remote(out_down.at[block_r], out_down.at[block_r], mate)
    d_mate_f = copies.remote(out_down.at[block_f], out_down.at[block_f], mate)
    q_cut, q_pair, q_far = urow(me.x_cut), urow(me.x_pair), urow(3 - me.x_pair)
    u_cut_swap = copies.remote(out_up.at[q_cut], out_up.at[q_cut], x_pair)
    u_mate_c = copies.remote(out_up.at[q_cut], out_up.at[q_cut], mate)
    u_mate_p = copies.remote(out_up.at[q_pair], out_up.at[q_pair], mate)
    u_mate_f = copies.remote(out_up.at[q_far], out_up.at[q_far], mate)

    @pl.when(needed)
    def _():
        d_own.wait()
        d_swap.wait_recv()
        d_cut_swap.wait_recv()
        d_right.start()
        d_left.start()
        d_mate.start()
        u_cut.wait_recv()
        u_cut_swap.start()
        u_mate_c.start()
        d_right.wait_recv()
        d_fwd_right.start()
        d_mate_l.start()
        d_left.wait_recv()
        d_fwd_left.start()
        d_mate_r.start()
        u_swap.wait_recv()
        u_mate_p.start()
        d_fwd_right.wait_recv()
        d_fwd_left.wait_recv()
        d_mate_f.start()
        u_cut_swap.wait_recv()
        u_mate_f.start()
        u_own.wait()
        for copy in (
            d_swap, d_cut_swap, d_right, d_left, d_mate, d_fwd_right, d_fwd_left, d_mate_l, d_mate_r, d_mate_f,
            u_swap, u_mate, u_cut_swap, u_mate_c, u_mate_p, u_mate_f,
        ):
            copy.wait_send()

    @pl.when(jnp.logical_not(needed))
    def _():
        for copy in (d_mate, d_mate_l, d_mate_r, d_mate_f, u_mate, u_mate_c, u_mate_p, u_mate_f):
            copy.wait_recv()
        d_cut.wait_send()
        u_cut.wait_send()

    small_mate.wait_recv()
    out_small[...] = smo[...]
    copies.drain()


def second_call(*operands):
    remote = 80
    bf = lambda *shape: pltpu.VMEM(shape, BF16)
    fl = lambda *shape: pltpu.VMEM(shape, F32)
    return pl.pallas_call(
        second_kernel,
        out_shape=(
            jax.ShapeDtypeStruct((ROWS, CH), BF16),
            jax.ShapeDtypeStruct((ROWS, CH), BF16),
            jax.ShapeDtypeStruct((CH, HID), BF16),
            jax.ShapeDtypeStruct((HID, CH), BF16),
            jax.ShapeDtypeStruct((64, CH), F32),
        ),
        in_specs=[ANY] * 6 + [VMEM] * 9,
        out_specs=(VMEM, VMEM, ANY, ANY, VMEM),
        scratch_shapes=[
            bf(CH, HID), bf(HID, CH), bf(CH, HID), bf(HID, CH),
            bf(2, 192, 1536), bf(2, 192, 3072), bf(2, 768, 384), bf(2, 768, 768),
            bf(2, 48, 1536), bf(2, 48, 3072), bf(2, 192, 384), bf(2, 192, 768),
            bf(768, 768), bf(48, 3072), bf(192, 768),
            bf(512, CH), bf(512, CH),
            bf(2, 128, 1536), bf(2, 128, 3072), bf(2, 128, 1536), bf(2, 128, 3072),
            fl(ROWS, CH), fl(64, CH), fl(32, CH), fl(2, 8, 1536), fl(2, 8, CH),
            fl(4, 8, CH), fl(4, 8, CH), fl(64, CH),
            pltpu.SemaphoreType.DMA((remote,)),
            pltpu.SemaphoreType.DMA((remote,)),
            pltpu.SemaphoreType.DMA((32,)),
        ],
        compiler_params=pltpu.CompilerParams(
            collective_id=1, has_side_effects=True, vmem_limit_bytes=60 * 1024 * 1024
        ),
    )(*operands)


def on_device(
    images, grad_out, dw_weight, dw_bias, ln_gain, ln_bias, w_up, b_up, w_down, b_down, layer_scale
):
    img = images.reshape(ROWS, CH)
    gout = grad_out.reshape(ROWS, CH)
    dww = dw_weight.reshape(49, CH)
    row = lambda vector: vector.reshape(1, CH)
    bu = jnp.broadcast_to(b_up.reshape(1, HID), (8, HID))
    std, inv, pn, pb, keep_up, keep_down, got_up, got_down, pbias = first_call(
        img, gout, dww, row(dw_bias), row(ln_gain), row(ln_bias), row(layer_scale), w_up, w_down, bu
    )
    out_img, grad_img, out_up, out_down, small = second_call(
        pn, pb, keep_up, keep_down, got_up, got_down, img, gout, std, inv, dww, row(ln_gain), row(layer_scale), row(b_down), pbias
    )
    shard = lax.axis_index("fsdp")
    grad_b_up = lax.dynamic_slice(small[54:56].reshape(-1), (shard * HID,), (HID,)).astype(BF16)
    return (
        out_img.reshape(images.shape),
        grad_img.reshape(images.shape),
        out_up,
        grad_b_up,
        out_down,
        small[:49].reshape(dw_weight.shape),
        small[49],
        small[50],
        small[51],
        small[52],
        small[53],
    )


def solution(mesh):
    tokens = P(("dp", "fsdp"), None, None, None)
    up, bias, down = P(None, "fsdp"), P("fsdp"), P("fsdp", None)
    return jax.shard_map(
        on_device,
        mesh=mesh,
        in_specs=(tokens, tokens, P(), P(), P(), P(), up, bias, down, P(), P()),
        out_specs=(tokens, tokens, up, bias, down, P(), P(), P(), P(), P(), P()),
        check_vma=False,
    )
```

```python
import math

import jax
import jax.numpy as jnp
from jax import lax
from jax.experimental import pallas as pl
from jax.experimental.pallas import tpu as pltpu
from jax.sharding import PartitionSpec as P

MESH = pl.DeviceIdType.MESH
F32 = jnp.float32
BF16 = jnp.bfloat16
CH = 3072
HID = 768
ROWS = 128
LANES = 128
BLOCKS = CH // LANES
ANY = pl.BlockSpec(memory_space=pl.ANY)
VMEM = pl.BlockSpec(memory_space=pltpu.VMEM)


class Place:
    def __init__(self):
        d = lax.axis_index("dp")
        f = lax.axis_index("fsdp")
        self.z = lax.div(d, 4)
        self.x_lo = lax.rem(lax.div(d, 2), 2)
        self.core = lax.rem(d, 2)
        self.y = lax.div(f, 2)
        self.x_hi = lax.rem(f, 2)
        self.x = self.x_hi * 2 + self.x_lo
        self.other_core = 1 - self.core
        self.x_cut = 3 - self.x
        self.x_pair = self.x_hi * 2 + (1 - self.x_lo)

    def at(self, x=None, y=None, z=None, core=None):
        x = self.x if x is None else x
        y = self.y if y is None else y
        z = self.z if z is None else z
        core = self.core if core is None else core
        return (z * 4 + lax.rem(x, 2) * 2 + core, y * 2 + lax.div(x, 2))

    def ring(self, axis):
        me = getattr(self, axis)
        right, left, far = lax.rem(me + 1, 4), lax.rem(me + 3, 4), lax.rem(me + 2, 4)
        return self.at(**{axis: right}), self.at(**{axis: left}), me, right, left, far


class Copies:
    def __init__(self, send, recv, local):
        self.send, self.recv, self.local = send, recv, local
        self.used = 0
        self.used_local = 0
        self.sent = []

    def remote(self, src, dst, device):
        index = self.used
        self.used += 1
        return pltpu.make_async_remote_copy(
            src_ref=src,
            dst_ref=dst,
            send_sem=self.send.at[index],
            recv_sem=self.recv.at[index],
            device_id=device,
            device_id_type=MESH,
        )

    def push(self, src, dst, device):
        copy = self.remote(src, dst, device)
        copy.start()
        self.sent.append(copy)
        return copy

    def here(self, src, dst):
        index = self.used_local
        self.used_local += 1
        copy = pltpu.make_async_copy(src, dst, self.local.at[index])
        copy.start()
        return copy

    def drain(self):
        for copy in self.sent:
            copy.wait_send()


def greet(devices):
    barrier = pltpu.get_barrier_semaphore()
    for device in devices:
        pl.semaphore_signal(barrier, inc=1, device_id=device, device_id_type=MESH)
    pl.semaphore_wait(barrier, len(devices))


def rows_at(start, size):
    return pl.ds(pl.multiple_of(start, 16), size)


def lanes_at(block):
    return pl.ds(pl.multiple_of(block * LANES, LANES), LANES)


def shifted(row, by):
    if by == 0:
        return row
    moved = pltpu.roll(row, (-by) % 8, 0)
    place = lax.broadcasted_iota(jnp.int32, row.shape, 0)
    inside = (place + by >= 0) & (place + by < 8)
    return jnp.where(inside, moved, 0.0)


def tile_rows(ref, block):
    tiles = []
    for pair in range(8):
        both = ref[16 * pair : 16 * pair + 16, lanes_at(block)].astype(F32)
        tiles += [both[:8], both[8:]]
    return tiles


def conv_block(block, img, dww, dwb, out):
    pixels = tile_rows(img, block)
    cs = lanes_at(block)
    sums = [jnp.broadcast_to(dwb[0:1, cs], (8, LANES))] * 16
    for horizontal in range(7):
        moved = [shifted(tile, horizontal - 3) for tile in pixels]
        for vertical in range(7):
            weight = jnp.broadcast_to(dww[vertical, horizontal : horizontal + 1, cs], (8, LANES))
            for image in range(2):
                for p in range(8):
                    source = p + vertical - 3
                    if 0 <= source < 8:
                        sums[image * 8 + p] = sums[image * 8 + p] + moved[image * 8 + source] * weight
    for r in range(16):
        out[8 * r : 8 * r + 8, cs] = sums[r]


def gelu_parts(values):
    cdf = 0.5 * (1.0 + lax.erf(values * 0.7071067811865476))
    return values * cdf, cdf + values * jnp.exp(-0.5 * values * values) * 0.3989422804014327


NT = (((1,), (1,)), ((), ()))
TN = (((0,), (0,)), ((), ()))


def first_kernel(
    img, gout, dww, dwb, gain, shift, lscale, wu, wd, bu,
    std, inv, pn, pb, keep_up, keep_down, got_up, got_down, bias_sums, scale_sums,
    gn, gs, wuv, wdv, b_own, bo, hid, gp, keep32, pnv, pbv, up_v, down_v,
    send, recv, local,
):
    me = Place()
    copies = Copies(send, recv, local)
    right, left, y, y_right, y_left, y_far = me.ring("y")
    cut = me.at(x=me.x_cut)
    pair = me.at(x=me.x_pair)
    mate = me.at(core=me.other_core)
    wu_load = copies.here(wu, wuv.at[0])
    wd_load = copies.here(wd, wdv.at[0])
    b_own[...] = jnp.broadcast_to(bu[...], (8, HID))
    z_right_chip, z_left_chip, z, z_right, z_left, z_far = me.ring("z")
    greet([right, left, cut, pair, mate, z_right_chip, z_left_chip])

    weights = (wuv.at[1], wdv.at[1])
    sizes = (192, 48)
    sides = (me.x_lo, 1 - me.x_lo)

    def piece(m, side, which):
        return rows_at((side * 8 + which * 2 + me.core) * sizes[m], sizes[m])

    def held(m, k, which):
        return weights[m].at[piece(m, sides[k], which)]

    bias = copies.push(b_own, bo, cut)
    over_cut = []
    for m in range(2):
        at = piece(m, sides[1], z)
        over_cut.append(copies.push((wu, wd)[m].at[at], weights[m].at[at], cut))
    swapped, ring_one, ring_two, mates = {}, {}, {}, {0: [], 1: []}

    def to_mate(m, ref):
        mates[m].append(copies.push(ref, ref, mate))

    def around(m, k):
        ref = held(m, k, z)
        ring_one[m, k] = copies.push(ref, ref, z_right_chip), copies.push(ref, ref, z_left_chip)
        to_mate(m, ref)

    def from_cut(m):
        over_cut[m].wait_recv()
        ref = held(m, 0, z)
        swapped[m] = copies.push(ref, ref, pair)
        around(m, 0)

    def from_pair(m):
        swapped[m].wait_recv()
        around(m, 1)

    def from_ring(m, k):
        width = (HID, CH)[m] // 2
        ring_one[m, k][0].wait_recv()
        ref = held(m, k, z_left)
        part = weights[m].at[piece(m, sides[k], z_left), pl.ds(0, width)]
        one = copies.push(part, part, z_right_chip)
        to_mate(m, ref)
        ring_one[m, k][1].wait_recv()
        ref = held(m, k, z_right)
        part = weights[m].at[piece(m, sides[k], z_right), pl.ds(width, width)]
        ring_two[m, k] = one, copies.push(part, part, z_left_chip)
        to_mate(m, ref)

    def from_far(m, k):
        for copy in ring_two[m, k]:
            copy.wait_recv()
        to_mate(m, held(m, k, z_far))

    def arrived(m):
        for copy in mates[m]:
            copy.wait_recv()

    own = rows_at(y * ROWS, ROWS)

    def scale_block(block, carry):
        cs = lanes_at(block)
        gs[own, cs] = (gout[:, cs].astype(F32) * lscale[0:1, cs]).astype(BF16)
        return carry

    lax.fori_loop(0, BLOCKS, scale_block, 0)

    half = ROWS // 2

    def halves(position):
        return rows_at(position * ROWS, half), rows_at(position * ROWS + half, half)

    def spread(buffer):
        low, high = halves(y)
        first = [copies.push(buffer.at[low], buffer.at[low], right), copies.push(buffer.at[high], buffer.at[high], left)]
        second = [copies.push(buffer.at[high], buffer.at[high], right), copies.push(buffer.at[low], buffer.at[low], left)]
        return first, second

    def forward(first, buffer):
        low, high = halves(y_left)[0], halves(y_right)[1]
        first[0].wait_recv()
        to_right = copies.push(buffer.at[low], buffer.at[low], right)
        first[1].wait_recv()
        to_left = copies.push(buffer.at[high], buffer.at[high], left)
        return [to_right, to_left]

    s_first, s_second = spread(gs)

    def conv_step(block, carry):
        conv_block(block, img, dww, dwb, std)
        return carry

    lax.fori_loop(0, BLOCKS // 2, conv_step, 0)
    from_cut(0)
    lax.fori_loop(BLOCKS // 2, BLOCKS, conv_step, 0)

    def add_block(block, total):
        return total + std[:, lanes_at(block)]

    zero = jnp.zeros((ROWS, LANES), F32)
    mean = jnp.sum(lax.fori_loop(0, BLOCKS, add_block, zero), axis=1, keepdims=True) * (1.0 / CH)

    def square_block(block, total):
        centred = std[:, lanes_at(block)] - mean
        return total + centred * centred

    variance = jnp.sum(lax.fori_loop(0, BLOCKS, square_block, zero), axis=1, keepdims=True) * (1.0 / CH)
    inv_std = lax.rsqrt(variance + 1e-06)
    inv[...] = jnp.broadcast_to(inv_std, (ROWS, LANES))

    def norm_block(block, carry):
        cs = lanes_at(block)
        standard = (std[:, cs] - mean) * inv_std
        std[:, cs] = standard
        gn[own, cs] = (standard * gain[0:1, cs] + shift[0:1, cs]).astype(BF16)
        return carry

    lax.fori_loop(0, BLOCKS, norm_block, 0)
    n_first, n_second = spread(gn)
    s_last = forward(s_first, gs)
    from_cut(1)

    tile = 256

    def hidden_tile(index):
        return pl.ds(pl.multiple_of(index * tile, tile), tile)

    bias_sums[...] = jnp.zeros_like(bias_sums)

    def own_grad_hidden():
        def body(index, carry):
            cs = hidden_tile(index)
            keep32[0, :, cs] = lax.dot_general(gs[...], wdv[0, cs, :], NT, preferred_element_type=F32)
            return carry

        lax.fori_loop(0, HID // tile, body, 0)

    def up_rows_of(s, position):
        at = rows_at(position * ROWS, ROWS)
        pre = jnp.dot(gn[at, :], wuv[s], preferred_element_type=F32)
        value, slope = gelu_parts(pre + (b_own if s == 0 else bo)[0:1, :])
        hid[s, at, :] = value.astype(BF16)
        if s == 0:
            grad = (keep32[0, at, :] * slope).astype(BF16)
            gp[0, at, :] = grad
            bias_sums[0:1, :] = bias_sums[0:1, :] + jnp.sum(grad.astype(F32), axis=0, keepdims=True)
        else:
            keep32[1, at, :] = slope

    def other_grad():
        def body(index, carry):
            cs = hidden_tile(index)
            grad = lax.dot_general(gs[...], wdv[1, cs, :], NT, preferred_element_type=F32)
            pre = (grad * keep32[1, :, cs]).astype(BF16)
            gp[1, :, cs] = pre
            bias_sums[1:2, cs] = jnp.sum(pre.astype(F32), axis=0, keepdims=True)
            return carry

        lax.fori_loop(0, HID // tile, body, 0)

    keep = lax.rem(me.x_hi + me.core, 2)
    moves = {}

    def place(matrix, s, part):
        if matrix == 0:
            at = (pl.ds(part * 768, 768), slice(None))
            mine, there, ref = keep_up, got_up, up_v
        else:
            at = (slice(None), pl.ds(part * 768, 768))
            mine, there, ref = keep_down, got_down, down_v
        if (matrix, part) not in moves:
            index = copies.used_local
            copies.used_local += 1
            moves[matrix, part] = (
                copies.remote(ref.at[at], there.at[at], mate),
                pltpu.make_async_copy(ref.at[at], mine.at[at], local.at[index]),
            )
        away, stay = moves[matrix, part]

        @pl.when(keep != s)
        def _():
            away.start()

        @pl.when(keep == s)
        def _():
            stay.start()

    def placed(matrix, s, part):
        away, stay = moves[matrix, part]

        @pl.when(keep != s)
        def _():
            away.wait_send()

        @pl.when(keep == s)
        def _():
            stay.wait()

    def part_up(s):
        for part in range(4):
            if s == 1:
                placed(0, 0, part)
            rows = pl.ds(part * 768, 768)
            up_v[rows, :] = lax.dot_general(gn[:, rows], gp[s], TN, preferred_element_type=F32).astype(BF16)
            place(0, s, part)

    def part_down(s):
        for part in range(4):
            if s == 1:
                placed(1, 0, part)
            cs = pl.ds(part * 768, 768)
            down_v[:, cs] = lax.dot_general(hid[s], gs[:, cs], TN, preferred_element_type=F32).astype(BF16)
            place(1, s, part)

    from_pair(0)
    from_ring(0, 0)
    from_pair(1)
    from_ring(0, 1)
    wu_load.wait()
    wd_load.wait()
    for copy in s_second + s_last:
        copy.wait_recv()
    own_grad_hidden()
    from_ring(1, 0)
    from_ring(1, 1)
    n_last = forward(n_first, gn)
    up_rows_of(0, y)
    from_far(0, 0)
    from_far(0, 1)
    bias.wait_recv()
    for copy in n_second:
        copy.wait_recv()
    up_rows_of(0, y_right)
    up_rows_of(0, y_left)
    from_far(1, 0)
    from_far(1, 1)
    arrived(0)
    up_rows_of(1, y)
    up_rows_of(1, y_right)
    up_rows_of(1, y_left)
    for copy in n_last:
        copy.wait_recv()
    up_rows_of(0, y_far)
    up_rows_of(1, y_far)
    part_down(0)
    part_up(0)
    part_down(1)
    arrived(1)
    other_grad()
    part_up(1)
    wide = 768

    def normed_back(index, carry):
        cs = pl.ds(pl.multiple_of(index * wide, wide), wide)
        total = lax.dot_general(gp[0], wuv[0, cs, :], NT, preferred_element_type=F32)
        total = total + lax.dot_general(gp[1], wuv[1, cs, :], NT, preferred_element_type=F32)
        pnv[:, cs] = total.astype(BF16)
        return carry

    lax.fori_loop(0, CH // wide, normed_back, 0)
    pn_out = copies.here(pnv, pn)

    def branch_tile(index, carry):
        cs = pl.ds(pl.multiple_of(index * wide, wide), wide)
        total = jnp.dot(hid[0], wdv[0, :, cs], preferred_element_type=F32)
        total = total + jnp.dot(hid[1], wdv[1, :, cs], preferred_element_type=F32)
        pbv[:, cs] = total.astype(BF16)
        product = jnp.sum(total * gs[:, cs].astype(F32), axis=0, keepdims=True)
        scale_sums[0:1, cs] = product / lscale[0:1, cs]
        return carry

    lax.fori_loop(0, CH // wide, branch_tile, 0)
    pb_out = copies.here(pbv, pb)

    pn_out.wait()
    pb_out.wait()
    for matrix in range(2):
        for part in range(4):
            placed(matrix, 1, part)
            moves[matrix, part][0].wait_recv()
    copies.drain()


def first_call(img, gout, dww, dwb, gain, shift, lscale, wu, wd, bu):
    remote = 64
    rows = 4 * ROWS
    return pl.pallas_call(
        first_kernel,
        out_shape=(
            jax.ShapeDtypeStruct((ROWS, CH), F32),
            jax.ShapeDtypeStruct((ROWS, LANES), F32),
            jax.ShapeDtypeStruct((rows, CH), BF16),
            jax.ShapeDtypeStruct((rows, CH), BF16),
            jax.ShapeDtypeStruct((CH, HID), BF16),
            jax.ShapeDtypeStruct((HID, CH), BF16),
            jax.ShapeDtypeStruct((CH, HID), BF16),
            jax.ShapeDtypeStruct((HID, CH), BF16),
            jax.ShapeDtypeStruct((8, HID), F32),
            jax.ShapeDtypeStruct((8, CH), F32),
        ),
        in_specs=[VMEM] * 7 + [ANY, ANY, VMEM],
        out_specs=(VMEM, VMEM, ANY, ANY, ANY, ANY, ANY, ANY, VMEM, VMEM),
        scratch_shapes=[
            pltpu.VMEM((rows, CH), BF16),
            pltpu.VMEM((rows, CH), BF16),
            pltpu.VMEM((2, CH, HID), BF16),
            pltpu.VMEM((2, HID, CH), BF16),
            pltpu.VMEM((8, HID), F32),
            pltpu.VMEM((8, HID), F32),
            pltpu.VMEM((2, rows, HID), BF16),
            pltpu.VMEM((2, rows, HID), BF16),
            pltpu.VMEM((2, rows, HID), F32),
            pltpu.VMEM((rows, CH), BF16),
            pltpu.VMEM((rows, CH), BF16),
            pltpu.VMEM((CH, HID), BF16),
            pltpu.VMEM((HID, CH), BF16),
            pltpu.SemaphoreType.DMA((remote,)),
            pltpu.SemaphoreType.DMA((remote,)),
            pltpu.SemaphoreType.DMA((12,)),
        ],
        compiler_params=pltpu.CompilerParams(
            collective_id=0, has_side_effects=True, vmem_limit_bytes=62 * 1024 * 1024
        ),
    )(img, gout, dww, dwb, gain, shift, lscale, wu, wd, bu)


def add_rows(dst, dst_row, sources, rows, column, columns, step=16):
    def body(index, carry):
        at = rows_at(dst_row + index * step, step)
        cs = pl.ds(column, columns)
        total = dst[at, cs].astype(F32)
        for ref, row, first in sources:
            total = total + ref[rows_at(row + index * step, step), pl.ds(first, columns)].astype(F32)
        dst[at, cs] = total.astype(dst.dtype)
        return carry

    lax.fori_loop(0, rows // step, body, 0)


class RingSum:
    def __init__(self, copies, where, data, base, rows, near, far, step=16):
        self.copies, self.data, self.base, self.rows = copies, data, base, rows
        self.right, self.left, self.me, self.at_right, self.at_left, self.at_far = where
        self.near, self.far, self.step = near, far, step
        self.half = data.shape[1] // 2

    def block(self, which):
        return self.base + which * self.rows

    def begin(self):
        at = rows_at(self.block(self.at_far), self.rows)
        h = self.half
        self.one = [
            self.copies.push(self.data.at[at, pl.ds(0, h)], self.far.at[0], self.right),
            self.copies.push(self.data.at[at, pl.ds(h, h)], self.far.at[1], self.left),
        ]

    def sides(self):
        return enumerate(((self.right, self.at_right), (self.left, self.at_left)))

    def own_halves(self):
        h = self.half
        self.two = []
        for side, (device, block) in self.sides():
            at, cs = rows_at(self.block(block), self.rows), pl.ds((1 - side) * h, h)
            self.two.append(self.copies.push(self.data.at[at, cs], self.near.at[side, :, cs], device))

    def middle(self):
        h = self.half
        for side, (device, block) in self.sides():
            self.one[side].wait_recv()
            start = self.block(block)
            add_rows(self.data, start, [(self.far.at[side], 0, 0)], self.rows, side * h, h, self.step)
            at, cs = rows_at(start, self.rows), pl.ds(side * h, h)
            self.two.append(self.copies.push(self.data.at[at, cs], self.near.at[side, :, cs], device))

    def end(self):
        for copy in self.two:
            copy.wait_recv()
        add_rows(
            self.data,
            self.block(self.me),
            [(self.near.at[0], 0, 0), (self.near.at[1], 0, 0)],
            self.rows,
            0,
            2 * self.half,
            self.step,
        )


def small_add(dst, row, sources, rows):
    total = dst[row, :]
    for source in sources:
        total = total + source
    dst[row, :] = total


def second_kernel(
    pn, pb, gu, gd, ru, rd, img, gout, std, inv, dww, gain, lscale, bdown, pbias, pscale,
    out_img, grad_img, out_up, out_down, out_small,
    guv, gdv, cu, cd, d1a, d1b, u1a, u1b, d2a, d2b, u2a, u2b, tq, fd, fu,
    nv, bv, n1, n2, b1, b2, gcv, sm, smc, sya, syb, sx, sz, smo,
    send, recv, local,
):
    me = Place()
    copies = Copies(send, recv, local)
    ring_x, ring_y, ring_z = me.ring("x"), me.ring("y"), me.ring("z")
    mate = me.at(core=me.other_core)
    x_cut = me.at(x=me.x_cut)
    x_pair = me.at(x=me.x_pair)
    x, y, z = me.x, me.y, me.z
    factor = 1.0 / math.sqrt(16384.0)

    z_far, z_right, z_left = ring_z[5], ring_z[3], ring_z[4]
    x_far, x_right, x_left = ring_x[5], ring_x[3], ring_x[4]
    order = [(0, z_far), (1, x_far), (0, z_right), (1, x_right), (0, z_left), (1, x_left), (0, z), (1, x)]
    swaps, loads = [], []
    load_n = copies.here(pn, nv)

    def piece(matrix, which):
        return rows_at(which * 192, 192) if matrix == 0 else rows_at(which * 768, 768)

    for m, which in order:
        src, got, dst, mine = ((gd, rd, cd, gdv), (gu, ru, cu, guv))[m]
        at = piece(m, which)
        swaps.append(copies.here(got.at[at], dst.at[at]))
        loads.append(copies.here(src.at[at], mine.at[at]))
    load_b = copies.here(pb, bv)
    greet([ring_x[0], ring_x[1], ring_y[0], ring_y[1], ring_z[0], ring_z[1], mate])

    y_far = ring_y[5]
    load_n.wait()
    rs_n = RingSum(copies, ring_y, nv, 0, ROWS, n2, n1)
    rs_n.begin()
    rs_n.own_halves()
    rs_b = RingSum(copies, ring_y, bv, 0, ROWS, b2, b1)

    def merge(index):
        m, which = order[index]
        mine, other = ((gdv, cd), (guv, cu))[m]
        rows = 192 if m == 0 else 768
        loads[index].wait()
        swaps[index].wait()
        add_rows(mine, which * rows, [(other, which * rows, 0)], rows, 0, mine.shape[1], 16 if m == 0 else 64)

    rs_d1 = RingSum(copies, ring_z, gdv, 0, 192, d1b, d1a)
    rs_u1 = RingSum(copies, ring_x, guv, 0, 768, u1b, u1a)
    merge(0)
    rs_d1.begin()
    merge(1)
    rs_u1.begin()
    for index in range(2, 6):
        merge(index)
    rs_d1.own_halves()
    rs_u1.own_halves()
    load_b.wait()
    rs_b.begin()
    rs_n.middle()
    rs_b.own_halves()
    rs_d1.middle()
    rs_u1.middle()
    merge(6)
    merge(7)

    rs_n.end()
    own = y * ROWS
    zero = jnp.zeros((ROWS, LANES), F32)

    def own_rows(ref, cs):
        return ref[rows_at(own, ROWS), cs].astype(F32)

    def norm_sums(block, totals):
        cs = lanes_at(block)
        grad_normed = own_rows(nv, cs)
        standard = std[:, cs]
        product = grad_normed * standard
        sm[50:51, cs] = jnp.sum(product, axis=0, keepdims=True)
        sm[51:52, cs] = jnp.sum(grad_normed, axis=0, keepdims=True)
        weight = gain[0:1, cs]
        return totals[0] + grad_normed * weight, totals[1] + product * weight

    total_g, total_gs = lax.fori_loop(0, BLOCKS, norm_sums, (zero, zero))
    mean_g = jnp.sum(total_g, axis=1, keepdims=True) * (1.0 / CH)
    mean_gs = jnp.sum(total_gs, axis=1, keepdims=True) * (1.0 / CH)
    inv_std = inv[...]

    def norm_apply(block, carry):
        cs = lanes_at(block)
        grad_hat = own_rows(nv, cs) * gain[0:1, cs]
        grad_conv = inv_std * (grad_hat - mean_g - std[:, cs] * mean_gs)
        gcv[:, cs] = grad_conv
        sm[49:50, cs] = jnp.sum(grad_conv, axis=0, keepdims=True)
        upstream = gout[:, cs].astype(F32)
        scaled = (upstream * lscale[0:1, cs]).astype(BF16).astype(F32)
        sm[52:53, cs] = jnp.sum(scaled, axis=0, keepdims=True)
        return carry

    lax.fori_loop(0, BLOCKS, norm_apply, 0)

    def conv_back(block, carry):
        cs = lanes_at(block)
        pixels = tile_rows(img, block)
        upstream = tile_rows(gout, block)
        grads = [gcv[8 * r : 8 * r + 8, cs] for r in range(16)]
        sums = upstream
        for horizontal in range(7):
            moved = [shifted(tile, 3 - horizontal) for tile in grads]
            for vertical in range(7):
                tap = vertical * 7 + horizontal
                weight = jnp.broadcast_to(dww[vertical, horizontal : horizontal + 1, cs], (8, LANES))
                taps = jnp.zeros((8, LANES), F32)
                for image in range(2):
                    for p in range(8):
                        source = p - (vertical - 3)
                        if 0 <= source < 8:
                            tile = moved[image * 8 + source]
                            sums[image * 8 + p] = sums[image * 8 + p] + tile * weight
                            taps = taps + tile * pixels[image * 8 + p]
                sm[tap : tap + 1, cs] = jnp.sum(taps, axis=0, keepdims=True)
        for r in range(8):
            grad_img[16 * r : 16 * r + 16, cs] = jnp.concatenate(sums[2 * r : 2 * r + 2], axis=0).astype(BF16)
        return carry

    lax.fori_loop(0, BLOCKS, conv_back, 0)

    def scale_block(block, carry):
        cs = lanes_at(block)
        upstream = jnp.sum(gout[:, cs].astype(F32), axis=0, keepdims=True)
        sm[53:54, cs] = pscale[0:1, cs] + upstream * bdown[0:1, cs]
        return carry

    lax.fori_loop(0, BLOCKS, scale_block, 0)
    sm[54:64, :] = jnp.zeros((10, CH), F32)
    for s in range(2):
        shard = y * 2 + (me.x_hi if s == 0 else 1 - me.x_hi)
        for line in range(2):

            @pl.when(lax.div(shard, 4) == line)
            def _(s=s, line=line):
                at = pl.ds(pl.multiple_of(lax.rem(shard, 4) * HID, LANES), HID)
                sm[54 + line : 55 + line, at] = pbias[s : s + 1, :]

    swap_small = copies.push(sm.at[pl.ds(pl.multiple_of(me.other_core * 32, 8), 32)], smc, mate)
    small_rows = me.core * 32
    sm_at = pl.ds(pl.multiple_of(small_rows, 8), 32)
    yr, yl, yy, y_right, y_left, y_far = ring_y
    zr, zl = ring_z[0], ring_z[1]
    h = CH // 2
    lo, hi = pl.ds(0, h), pl.ds(h, h)

    def small_piece(which):
        return pl.ds(pl.multiple_of(small_rows + which * 8, 8), 8)

    def all_begin(buffer, ring):
        where = ring[2]
        return [
            copies.push(buffer.at[where], buffer.at[where], ring[0]),
            copies.push(buffer.at[where], buffer.at[where], ring[1]),
        ]

    def all_middle(buffer, ring, one):
        at_right, at_left = ring[3], ring[4]
        one[0].wait_recv()
        two = [copies.push(buffer.at[at_left, :, lo], buffer.at[at_left, :, lo], ring[0])]
        one[1].wait_recv()
        two.append(copies.push(buffer.at[at_right, :, hi], buffer.at[at_right, :, hi], ring[1]))
        return two

    def all_end(buffer, two):
        for copy in two:
            copy.wait_recv()
        return buffer[0] + buffer[1] + buffer[2] + buffer[3]

    rs_b.middle()
    swap_small.wait_recv()
    sm[sm_at, :] = sm[sm_at, :] + smc[...]
    s_one = [
        copies.push(sm.at[small_piece(y_far), lo], sya.at[0], yr),
        copies.push(sm.at[small_piece(y_far), hi], sya.at[1], yl),
    ]

    rs_d1.end()
    rs_d2 = RingSum(copies, ring_x, gdv, z * 192, 48, d2b, d2a)
    rs_d2.begin()
    rs_d2.own_halves()
    rs_u1.end()
    rs_u2 = RingSum(copies, ring_z, guv, x * 768, 192, u2b, u2a)
    rs_u2.begin()
    rs_u2.own_halves()

    s_two = []
    for side, (device, which) in enumerate(((yr, y_right), (yl, y_left))):
        s_one[side].wait_recv()
        at = small_piece(which)
        sm[at, pl.ds(side * h, h)] = sm[at, pl.ds(side * h, h)] + sya[side]
        s_two.append(copies.push(sm.at[at], syb.at[side], device))
    rs_d2.middle()
    rs_u2.middle()
    for side in range(2):
        s_two[side].wait_recv()
    at = small_piece(yy)
    sx[pl.ds(x, 1)] = (sm[at, :] + syb[0] + syb[1])[None]
    sx_one = all_begin(sx, ring_x)

    rs_d2.end()
    at_d = z * 192 + x * 48
    at_u = x * 768 + z * 192
    fd[...] = (gdv[rows_at(at_d, 48), :].astype(F32) * factor).astype(BF16)
    needed = me.x_hi == me.core

    def drow(which_x):
        return rows_at(z * 192 + which_x * 48, 48)

    d_cut = copies.remote(fd, out_down.at[drow(x)], x_cut)
    d_swap = copies.remote(fd, out_down.at[drow(x)], x_pair)
    d_cut_swap = copies.remote(out_down.at[drow(me.x_cut)], out_down.at[drow(me.x_cut)], x_pair)
    d_own = pltpu.make_async_copy(fd, out_down.at[drow(x)], local.at[30])

    @pl.when(jnp.logical_not(needed))
    def _():
        d_cut.start()

    @pl.when(needed)
    def _():
        d_own.start()
        d_swap.start()

    rs_u2.end()
    fu[...] = (guv[rows_at(at_u, 192), :].astype(F32) * factor).astype(BF16)

    def slot(which):
        return rows_at(which * 192, 192)

    tq_own = copies.here(fu, tq.at[slot(z)])
    up_one = [copies.push(fu, tq.at[slot(z)], zr), copies.push(fu, tq.at[slot(z)], zl)]
    sx_two = all_middle(sx, ring_x, sx_one)

    rs_b.end()

    def result_block(block, carry):
        cs = lanes_at(block)
        branch = own_rows(bv, cs) + bdown[0:1, cs]
        out_img[:, cs] = (img[:, cs].astype(F32) + lscale[0:1, cs] * branch).astype(BF16)
        return carry

    lax.fori_loop(0, BLOCKS, result_block, 0)

    @pl.when(needed)
    def _():
        d_cut.wait_recv()
        d_cut_swap.start()

    sz[pl.ds(z, 1)] = all_end(sx, sx_two)[None]
    sz_one = all_begin(sz, ring_z)
    hu = HID // 2
    z_left_slot, z_right_slot = slot(z_left), slot(z_right)
    up_one[0].wait_recv()
    up_two = [copies.push(tq.at[z_left_slot, pl.ds(0, hu)], tq.at[z_left_slot, pl.ds(0, hu)], zr)]
    up_one[1].wait_recv()
    up_two.append(copies.push(tq.at[z_right_slot, pl.ds(hu, hu)], tq.at[z_right_slot, pl.ds(hu, hu)], zl))
    sz_two = all_middle(sz, ring_z, sz_one)

    def dblock(which):
        return rows_at(which * 192, 192)

    block = dblock(z)
    d_right = copies.remote(out_down.at[block], out_down.at[block], zr)
    d_left = copies.remote(out_down.at[block], out_down.at[block], zl)
    d_mate = copies.remote(out_down.at[block], out_down.at[block], mate)

    @pl.when(needed)
    def _():
        d_own.wait()
        d_swap.wait_recv()
        d_cut_swap.wait_recv()
        d_right.start()
        d_left.start()
        d_mate.start()

    for copy in up_two:
        copy.wait_recv()
    tq_own.wait()

    def urow(which_x):
        return rows_at(which_x * 768, 768)

    u_cut = copies.remote(tq, out_up.at[urow(x)], x_cut)
    u_swap = copies.remote(tq, out_up.at[urow(x)], x_pair)
    u_mate = copies.remote(tq, out_up.at[urow(x)], mate)
    u_own = pltpu.make_async_copy(tq, out_up.at[urow(x)], local.at[31])

    @pl.when(jnp.logical_not(needed))
    def _():
        u_cut.start()

    @pl.when(needed)
    def _():
        u_swap.start()
        u_mate.start()
        u_own.start()

    total = all_end(sz, sz_two)
    smo_at = small_piece(yy)
    smo[smo_at, :] = total * factor
    so_one = [
        copies.push(smo.at[smo_at], smo.at[smo_at], yr),
        copies.push(smo.at[smo_at], smo.at[smo_at], yl),
    ]
    from_left, from_right = small_piece(y_left), small_piece(y_right)
    so_one[0].wait_recv()
    so_two = [copies.push(smo.at[from_left, lo], smo.at[from_left, lo], yr)]
    so_one[1].wait_recv()
    so_two.append(copies.push(smo.at[from_right, hi], smo.at[from_right, hi], yl))
    for copy in so_two:
        copy.wait_recv()
    small_mate = copies.push(smo.at[sm_at], smo.at[sm_at], mate)

    block_l, block_r, block_f = dblock(z_left), dblock(z_right), dblock(z_far)
    d_fwd_right = copies.remote(out_down.at[block_l, lo], out_down.at[block_l, lo], zr)
    d_fwd_left = copies.remote(out_down.at[block_r, hi], out_down.at[block_r, hi], zl)
    d_mate_l = copies.remote(out_down.at[block_l], out_down.at[block_l], mate)
    d_mate_r = copies.remote(out_down.at[block_r], out_down.at[block_r], mate)
    d_mate_f = copies.remote(out_down.at[block_f], out_down.at[block_f], mate)
    q_cut, q_pair, q_far = urow(me.x_cut), urow(me.x_pair), urow(3 - me.x_pair)
    u_cut_swap = copies.remote(out_up.at[q_cut], out_up.at[q_cut], x_pair)
    u_mate_c = copies.remote(out_up.at[q_cut], out_up.at[q_cut], mate)
    u_mate_p = copies.remote(out_up.at[q_pair], out_up.at[q_pair], mate)
    u_mate_f = copies.remote(out_up.at[q_far], out_up.at[q_far], mate)

    @pl.when(needed)
    def _():
        u_cut.wait_recv()
        u_cut_swap.start()
        u_mate_c.start()
        d_right.wait_recv()
        d_fwd_right.start()
        d_mate_l.start()
        d_left.wait_recv()
        d_fwd_left.start()
        d_mate_r.start()
        u_swap.wait_recv()
        u_mate_p.start()
        d_fwd_right.wait_recv()
        d_fwd_left.wait_recv()
        d_mate_f.start()
        u_cut_swap.wait_recv()
        u_mate_f.start()
        u_own.wait()
        for copy in (
            d_swap, d_cut_swap, d_right, d_left, d_mate, d_fwd_right, d_fwd_left, d_mate_l, d_mate_r, d_mate_f,
            u_swap, u_mate, u_cut_swap, u_mate_c, u_mate_p, u_mate_f,
        ):
            copy.wait_send()

    @pl.when(jnp.logical_not(needed))
    def _():
        for copy in (d_mate, d_mate_l, d_mate_r, d_mate_f, u_mate, u_mate_c, u_mate_p, u_mate_f):
            copy.wait_recv()
        d_cut.wait_send()
        u_cut.wait_send()

    small_mate.wait_recv()
    out_small[...] = smo[...]
    copies.drain()


def second_call(*operands):
    remote = 96
    bf = lambda *shape: pltpu.VMEM(shape, BF16)
    fl = lambda *shape: pltpu.VMEM(shape, F32)
    return pl.pallas_call(
        second_kernel,
        out_shape=(
            jax.ShapeDtypeStruct((ROWS, CH), BF16),
            jax.ShapeDtypeStruct((ROWS, CH), BF16),
            jax.ShapeDtypeStruct((CH, HID), BF16),
            jax.ShapeDtypeStruct((HID, CH), BF16),
            jax.ShapeDtypeStruct((64, CH), F32),
        ),
        in_specs=[ANY] * 6 + [VMEM] * 10,
        out_specs=(VMEM, VMEM, ANY, ANY, VMEM),
        scratch_shapes=[
            bf(CH, HID), bf(HID, CH), bf(CH, HID), bf(HID, CH),
            bf(2, 192, 1536), bf(2, 192, 3072), bf(2, 768, 384), bf(2, 768, 768),
            bf(2, 48, 1536), bf(2, 48, 3072), bf(2, 192, 384), bf(2, 192, 768),
            bf(768, 768), bf(48, 3072), bf(192, 768),
            bf(512, CH), bf(512, CH),
            bf(2, 128, 1536), bf(2, 128, 3072), bf(2, 128, 1536), bf(2, 128, 3072),
            fl(ROWS, CH), fl(64, CH), fl(32, CH), fl(2, 8, 1536), fl(2, 8, CH),
            fl(4, 8, CH), fl(4, 8, CH), fl(64, CH),
            pltpu.SemaphoreType.DMA((remote,)),
            pltpu.SemaphoreType.DMA((remote,)),
            pltpu.SemaphoreType.DMA((32,)),
        ],
        compiler_params=pltpu.CompilerParams(
            collective_id=1, has_side_effects=True, vmem_limit_bytes=60 * 1024 * 1024
        ),
    )(*operands)


def last_kernel(oimg, gimg, up, down, small, o1, o2, o3, o4, dw, r1, r2, r3, r4, r5, gb, v1, v2, v3, v4, load, store):
    trips = [(oimg, v1, o1), (gimg, v2, o2)]
    for part in range(4):
        rows = pl.ds(part * 768, 768)
        trips.append((up.at[rows], v3.at[rows], o3.at[rows]))
    for part in range(4):
        rows = pl.ds(part * 192, 192)
        trips.append((down.at[rows], v4.at[rows], o4.at[rows]))
    loads = [pltpu.make_async_copy(src, mid, load.at[i]) for i, (src, mid, dst) in enumerate(trips)]
    stores = [pltpu.make_async_copy(mid, dst, store.at[i]) for i, (src, mid, dst) in enumerate(trips)]
    for move in loads:
        move.start()
    for vertical in range(7):
        dw[vertical] = small[vertical * 7 : vertical * 7 + 7, :]
    for index, ref in enumerate((r1, r2, r3, r4, r5)):
        ref[...] = small[49 + index, :]
    shard = lax.axis_index("fsdp")
    at = pl.ds(pl.multiple_of(lax.rem(shard, 4) * HID, LANES), HID)
    line = lax.div(shard, 4)
    gb[...] = jnp.where(line == 0, small[54:55, at], small[55:56, at]).astype(BF16)
    for first, second in zip(loads, stores):
        first.wait()
        second.start()
    for move in stores:
        move.wait()


def last_call(oimg, gimg, up, down, small):
    wide = jax.ShapeDtypeStruct((ROWS, CH), BF16)
    line = jax.ShapeDtypeStruct((CH,), F32)
    return pl.pallas_call(
        last_kernel,
        out_shape=(
            wide,
            wide,
            jax.ShapeDtypeStruct((CH, HID), BF16),
            jax.ShapeDtypeStruct((HID, CH), BF16),
            jax.ShapeDtypeStruct((7, 7, CH), F32),
            line,
            line,
            line,
            line,
            line,
            jax.ShapeDtypeStruct((1, HID), BF16),
        ),
        in_specs=[ANY] * 4 + [VMEM],
        out_specs=tuple([ANY] * 4 + [VMEM] * 7),
        scratch_shapes=[
            pltpu.VMEM((ROWS, CH), BF16),
            pltpu.VMEM((ROWS, CH), BF16),
            pltpu.VMEM((CH, HID), BF16),
            pltpu.VMEM((HID, CH), BF16),
            pltpu.SemaphoreType.DMA((10,)),
            pltpu.SemaphoreType.DMA((10,)),
        ],
        compiler_params=pltpu.CompilerParams(vmem_limit_bytes=62 * 1024 * 1024),
    )(oimg, gimg, up, down, small)


def on_device(
    images, grad_out, dw_weight, dw_bias, ln_gain, ln_bias, w_up, b_up, w_down, b_down, layer_scale
):
    img = images.reshape(ROWS, CH)
    gout = grad_out.reshape(ROWS, CH)
    row = lambda vector: vector.reshape(1, CH)
    std, inv, pn, pb, keep_up, keep_down, got_up, got_down, pbias, pscale = first_call(
        img, gout, dw_weight, row(dw_bias), row(ln_gain), row(ln_bias), row(layer_scale), w_up, w_down, b_up.reshape(1, HID)
    )
    out_img, grad_img, out_up, out_down, small = second_call(
        pn, pb, keep_up, keep_down, got_up, got_down, img, gout, std, inv, dw_weight, row(ln_gain), row(layer_scale), row(b_down), pbias, pscale
    )
    oimg, gimg, up, down, dw, r1, r2, r3, r4, r5, gb = last_call(out_img, grad_img, out_up, out_down, small)
    return (
        oimg.reshape(images.shape),
        gimg.reshape(images.shape),
        up,
        gb.reshape(HID),
        down,
        dw,
        r1,
        r2,
        r3,
        r4,
        r5,
    )


def solution(mesh):
    tokens = P(("dp", "fsdp"), None, None, None)
    up, bias, down = P(None, "fsdp"), P("fsdp"), P("fsdp", None)
    return jax.shard_map(
        on_device,
        mesh=mesh,
        in_specs=(tokens, tokens, P(), P(), P(), P(), up, bias, down, P(), P()),
        out_specs=(tokens, tokens, up, bias, down, P(), P(), P(), P(), P(), P()),
        check_vma=False,
    )
```

```python
import math

import jax
import jax.numpy as jnp
from jax import lax
from jax.experimental import pallas as pl
from jax.experimental.pallas import tpu as pltpu
from jax.sharding import PartitionSpec as P

MESH = pl.DeviceIdType.MESH
F32 = jnp.float32
BF16 = jnp.bfloat16
CH = 3072
HID = 768
ROWS = 128
LANES = 128
BLOCKS = CH // LANES
ANY = pl.BlockSpec(memory_space=pl.ANY)
VMEM = pl.BlockSpec(memory_space=pltpu.VMEM)


class Place:
    def __init__(self):
        d = lax.axis_index("dp")
        f = lax.axis_index("fsdp")
        self.z = lax.div(d, 4)
        self.x_lo = lax.rem(lax.div(d, 2), 2)
        self.core = lax.rem(d, 2)
        self.y = lax.div(f, 2)
        self.x_hi = lax.rem(f, 2)
        self.x = self.x_hi * 2 + self.x_lo
        self.other_core = 1 - self.core
        self.x_cut = 3 - self.x
        self.x_pair = self.x_hi * 2 + (1 - self.x_lo)

    def at(self, x=None, y=None, z=None, core=None):
        x = self.x if x is None else x
        y = self.y if y is None else y
        z = self.z if z is None else z
        core = self.core if core is None else core
        return (z * 4 + lax.rem(x, 2) * 2 + core, y * 2 + lax.div(x, 2))

    def ring(self, axis):
        me = getattr(self, axis)
        right, left, far = lax.rem(me + 1, 4), lax.rem(me + 3, 4), lax.rem(me + 2, 4)
        return self.at(**{axis: right}), self.at(**{axis: left}), me, right, left, far


class Copies:
    def __init__(self, send, recv, local):
        self.send, self.recv, self.local = send, recv, local
        self.used = 0
        self.used_local = 0
        self.sent = []

    def remote(self, src, dst, device):
        index = self.used
        self.used += 1
        return pltpu.make_async_remote_copy(
            src_ref=src,
            dst_ref=dst,
            send_sem=self.send.at[index],
            recv_sem=self.recv.at[index],
            device_id=device,
            device_id_type=MESH,
        )

    def push(self, src, dst, device):
        copy = self.remote(src, dst, device)
        copy.start()
        self.sent.append(copy)
        return copy

    def here(self, src, dst):
        index = self.used_local
        self.used_local += 1
        copy = pltpu.make_async_copy(src, dst, self.local.at[index])
        copy.start()
        return copy

    def drain(self):
        for copy in self.sent:
            copy.wait_send()


def greet(devices):
    barrier = pltpu.get_barrier_semaphore()
    for device in devices:
        pl.semaphore_signal(barrier, inc=1, device_id=device, device_id_type=MESH)
    pl.semaphore_wait(barrier, len(devices))


def rows_at(start, size):
    return pl.ds(pl.multiple_of(start, 16), size)


def lanes_at(block):
    return pl.ds(pl.multiple_of(block * LANES, LANES), LANES)


def shifted(row, by):
    if by == 0:
        return row
    moved = pltpu.roll(row, (-by) % 8, 0)
    place = lax.broadcasted_iota(jnp.int32, row.shape, 0)
    inside = (place + by >= 0) & (place + by < 8)
    return jnp.where(inside, moved, 0.0)


def tile_rows(ref, block):
    tiles = []
    for pair in range(8):
        both = ref[16 * pair : 16 * pair + 16, lanes_at(block)].astype(F32)
        tiles += [both[:8], both[8:]]
    return tiles


def conv_block(block, img, dww, dwb, out):
    pixels = tile_rows(img, block)
    cs = lanes_at(block)
    sums = [jnp.broadcast_to(dwb[0:1, cs], (8, LANES))] * 16
    for horizontal in range(7):
        moved = [shifted(tile, horizontal - 3) for tile in pixels]
        for vertical in range(7):
            weight = jnp.broadcast_to(dww[vertical, horizontal : horizontal + 1, cs], (8, LANES))
            for image in range(2):
                for p in range(8):
                    source = p + vertical - 3
                    if 0 <= source < 8:
                        sums[image * 8 + p] = sums[image * 8 + p] + moved[image * 8 + source] * weight
    for r in range(16):
        out[8 * r : 8 * r + 8, cs] = sums[r]


def gelu_parts(values):
    cdf = 0.5 * (1.0 + lax.erf(values * 0.7071067811865476))
    return values * cdf, cdf + values * jnp.exp(-0.5 * values * values) * 0.3989422804014327


NT = (((1,), (1,)), ((), ()))
TN = (((0,), (0,)), ((), ()))


def first_kernel(
    img, gout, dww, dwb, gain, shift, lscale, wu, wd, bu,
    std, inv, hid_out, gp_out, gs_out, wu_out, wd_out, grad_up, grad_down, bias_sums,
    gn, gs, wuv, wdv, b_own, bo, hid, gp, keep32, up_v, down_v,
    send, recv, local,
):
    me = Place()
    copies = Copies(send, recv, local)
    right, left, y, y_right, y_left, y_far = me.ring("y")
    cut = me.at(x=me.x_cut)
    pair = me.at(x=me.x_pair)
    mate = me.at(core=me.other_core)
    wu_load = copies.here(wu, wuv.at[0])
    wd_load = copies.here(wd, wdv.at[0])
    b_own[...] = jnp.broadcast_to(bu[...][None, :], (8, HID))
    z_right_chip, z_left_chip, z, z_right, z_left, z_far = me.ring("z")
    greet([right, left, cut, pair, mate, z_right_chip, z_left_chip])

    weights = (wuv.at[1], wdv.at[1])
    sizes = (192, 48)
    sides = (me.x_lo, 1 - me.x_lo)

    def piece(m, side, which):
        return rows_at((side * 8 + which * 2 + me.core) * sizes[m], sizes[m])

    def held(m, k, which):
        return weights[m].at[piece(m, sides[k], which)]

    bias = copies.push(b_own, bo, cut)
    over_cut = []
    for m in range(2):
        at = piece(m, sides[1], z)
        over_cut.append(copies.push((wu, wd)[m].at[at], weights[m].at[at], cut))
    swapped, ring_one, ring_two, mates = {}, {}, {}, {0: [], 1: []}

    def to_mate(m, ref):
        mates[m].append(copies.push(ref, ref, mate))

    def around(m, k):
        ref = held(m, k, z)
        ring_one[m, k] = copies.push(ref, ref, z_right_chip), copies.push(ref, ref, z_left_chip)
        to_mate(m, ref)

    def from_cut(m):
        over_cut[m].wait_recv()
        ref = held(m, 0, z)
        swapped[m] = copies.push(ref, ref, pair)
        around(m, 0)

    def from_pair(m):
        swapped[m].wait_recv()
        around(m, 1)

    def from_ring(m, k):
        width = (HID, CH)[m] // 2
        ring_one[m, k][0].wait_recv()
        ref = held(m, k, z_left)
        part = weights[m].at[piece(m, sides[k], z_left), pl.ds(0, width)]
        one = copies.push(part, part, z_right_chip)
        to_mate(m, ref)
        ring_one[m, k][1].wait_recv()
        ref = held(m, k, z_right)
        part = weights[m].at[piece(m, sides[k], z_right), pl.ds(width, width)]
        ring_two[m, k] = one, copies.push(part, part, z_left_chip)
        to_mate(m, ref)

    def from_far(m, k):
        for copy in ring_two[m, k]:
            copy.wait_recv()
        to_mate(m, held(m, k, z_far))

    def arrived(m):
        for copy in mates[m]:
            copy.wait_recv()

    own = rows_at(y * ROWS, ROWS)

    def scale_block(block, carry):
        cs = lanes_at(block)
        gs[own, cs] = (gout[:, cs].astype(F32) * lscale[0:1, cs]).astype(BF16)
        return carry

    lax.fori_loop(0, BLOCKS, scale_block, 0)

    half = ROWS // 2

    def halves(position):
        return rows_at(position * ROWS, half), rows_at(position * ROWS + half, half)

    def spread(buffer):
        low, high = halves(y)
        first = [copies.push(buffer.at[low], buffer.at[low], right), copies.push(buffer.at[high], buffer.at[high], left)]
        second = [copies.push(buffer.at[high], buffer.at[high], right), copies.push(buffer.at[low], buffer.at[low], left)]
        return first, second

    def forward(first, buffer):
        low, high = halves(y_left)[0], halves(y_right)[1]
        first[0].wait_recv()
        to_right = copies.push(buffer.at[low], buffer.at[low], right)
        first[1].wait_recv()
        to_left = copies.push(buffer.at[high], buffer.at[high], left)
        return [to_right, to_left]

    s_first, s_second = spread(gs)

    def conv_step(block, carry):
        conv_block(block, img, dww, dwb, std)
        return carry

    lax.fori_loop(0, BLOCKS // 2, conv_step, 0)
    from_cut(0)
    lax.fori_loop(BLOCKS // 2, BLOCKS, conv_step, 0)

    def add_block(block, total):
        return total + std[:, lanes_at(block)]

    zero = jnp.zeros((ROWS, LANES), F32)
    mean = jnp.sum(lax.fori_loop(0, BLOCKS, add_block, zero), axis=1, keepdims=True) * (1.0 / CH)

    def square_block(block, total):
        centred = std[:, lanes_at(block)] - mean
        return total + centred * centred

    variance = jnp.sum(lax.fori_loop(0, BLOCKS, square_block, zero), axis=1, keepdims=True) * (1.0 / CH)
    inv_std = lax.rsqrt(variance + 1e-06)
    inv[...] = jnp.broadcast_to(inv_std, (ROWS, LANES))

    def norm_block(block, carry):
        cs = lanes_at(block)
        standard = (std[:, cs] - mean) * inv_std
        std[:, cs] = standard
        gn[own, cs] = (standard * gain[0:1, cs] + shift[0:1, cs]).astype(BF16)
        return carry

    lax.fori_loop(0, BLOCKS, norm_block, 0)
    n_first, n_second = spread(gn)
    s_last = forward(s_first, gs)
    from_cut(1)

    tile = 256

    def hidden_tile(index):
        return pl.ds(pl.multiple_of(index * tile, tile), tile)

    bias_sums[...] = jnp.zeros_like(bias_sums)

    def own_grad_hidden():
        def body(index, carry):
            cs = hidden_tile(index)
            keep32[0, :, cs] = lax.dot_general(gs[...], wdv[0, cs, :], NT, preferred_element_type=F32)
            return carry

        lax.fori_loop(0, HID // tile, body, 0)

    def up_rows_of(s, position):
        at = rows_at(position * ROWS, ROWS)
        pre = jnp.dot(gn[at, :], wuv[s], preferred_element_type=F32)
        value, slope = gelu_parts(pre + (b_own if s == 0 else bo)[0:1, :])
        hid[s, at, :] = value.astype(BF16)
        if s == 0:
            grad = (keep32[0, at, :] * slope).astype(BF16)
            gp[0, at, :] = grad
            bias_sums[0:1, :] = bias_sums[0:1, :] + jnp.sum(grad.astype(F32), axis=0, keepdims=True)
        else:
            keep32[1, at, :] = slope

    def other_grad():
        def body(index, carry):
            cs = hidden_tile(index)
            grad = lax.dot_general(gs[...], wdv[1, cs, :], NT, preferred_element_type=F32)
            pre = (grad * keep32[1, :, cs]).astype(BF16)
            gp[1, :, cs] = pre
            bias_sums[1:2, cs] = jnp.sum(pre.astype(F32), axis=0, keepdims=True)
            return carry

        lax.fori_loop(0, HID // tile, body, 0)

    outs = []

    def part_place(matrix, s, part):
        if matrix == 0:
            at = (pl.ds(part * 768, 768), slice(None))
            outs.append(copies.here(up_v.at[(s,) + at], grad_up.at[(s,) + at]))
        else:
            at = (slice(None), pl.ds(part * 768, 768))
            outs.append(copies.here(down_v.at[(s,) + at], grad_down.at[(s,) + at]))

    def part_up(s):
        for part in range(4):
            rows = pl.ds(part * 768, 768)
            up_v[s, rows, :] = lax.dot_general(gn[:, rows], gp[s], TN, preferred_element_type=F32).astype(BF16)
            part_place(0, s, part)

    def part_down(s):
        for part in range(4):
            cs = pl.ds(part * 768, 768)
            down_v[s, :, cs] = lax.dot_general(hid[s], gs[:, cs], TN, preferred_element_type=F32).astype(BF16)
            part_place(1, s, part)

    from_pair(0)
    from_ring(0, 0)
    from_pair(1)
    from_ring(0, 1)
    wu_load.wait()
    wd_load.wait()
    for copy in s_second + s_last:
        copy.wait_recv()
    own_grad_hidden()
    from_ring(1, 0)
    from_ring(1, 1)
    n_last = forward(n_first, gn)
    up_rows_of(0, y)
    from_far(0, 0)
    from_far(0, 1)
    bias.wait_recv()
    for copy in n_second:
        copy.wait_recv()
    up_rows_of(0, y_right)
    up_rows_of(0, y_left)
    from_far(1, 0)
    from_far(1, 1)
    arrived(0)
    up_rows_of(1, y)
    up_rows_of(1, y_right)
    up_rows_of(1, y_left)
    for copy in n_last:
        copy.wait_recv()
    up_rows_of(0, y_far)
    up_rows_of(1, y_far)
    part_down(0)
    part_up(0)
    part_down(1)
    arrived(1)
    outs.append(copies.here(wuv.at[1], wu_out))
    outs.append(copies.here(wdv.at[1], wd_out))
    outs.append(copies.here(hid, hid_out))
    outs.append(copies.here(gs, gs_out))
    other_grad()
    outs.append(copies.here(gp, gp_out))
    part_up(1)
    for copy in outs:
        copy.wait()
    copies.drain()


def first_call(img, gout, dww, dwb, gain, shift, lscale, wu, wd, bu):
    remote = 64
    rows = 4 * ROWS
    return pl.pallas_call(
        first_kernel,
        out_shape=(
            jax.ShapeDtypeStruct((ROWS, CH), F32),
            jax.ShapeDtypeStruct((ROWS, LANES), F32),
            jax.ShapeDtypeStruct((2, rows, HID), BF16),
            jax.ShapeDtypeStruct((2, rows, HID), BF16),
            jax.ShapeDtypeStruct((rows, CH), BF16),
            jax.ShapeDtypeStruct((CH, HID), BF16),
            jax.ShapeDtypeStruct((HID, CH), BF16),
            jax.ShapeDtypeStruct((2, CH, HID), BF16),
            jax.ShapeDtypeStruct((2, HID, CH), BF16),
            jax.ShapeDtypeStruct((8, HID), F32),
        ),
        in_specs=[VMEM] * 7 + [ANY, ANY, VMEM],
        out_specs=(VMEM, VMEM, ANY, ANY, ANY, ANY, ANY, ANY, ANY, VMEM),
        scratch_shapes=[
            pltpu.VMEM((rows, CH), BF16),
            pltpu.VMEM((rows, CH), BF16),
            pltpu.VMEM((2, CH, HID), BF16),
            pltpu.VMEM((2, HID, CH), BF16),
            pltpu.VMEM((8, HID), F32),
            pltpu.VMEM((8, HID), F32),
            pltpu.VMEM((2, rows, HID), BF16),
            pltpu.VMEM((2, rows, HID), BF16),
            pltpu.VMEM((2, rows, HID), F32),
            pltpu.VMEM((2, CH, HID), BF16),
            pltpu.VMEM((2, HID, CH), BF16),
            pltpu.SemaphoreType.DMA((remote,)),
            pltpu.SemaphoreType.DMA((remote,)),
            pltpu.SemaphoreType.DMA((32,)),
        ],
        compiler_params=pltpu.CompilerParams(
            collective_id=0, has_side_effects=True, vmem_limit_bytes=62 * 1024 * 1024
        ),
    )(img, gout, dww, dwb, gain, shift, lscale, wu, wd, bu)


def add_rows(dst, dst_row, sources, rows, column, columns, step=16):
    def body(index, carry):
        at = rows_at(dst_row + index * step, step)
        cs = pl.ds(column, columns)
        total = dst[at, cs].astype(F32)
        for ref, row, first in sources:
            total = total + ref[rows_at(row + index * step, step), pl.ds(first, columns)].astype(F32)
        dst[at, cs] = total.astype(dst.dtype)
        return carry

    lax.fori_loop(0, rows // step, body, 0)


class RingSum:
    def __init__(self, copies, where, data, base, rows, near, far, step=16):
        self.copies, self.data, self.base, self.rows = copies, data, base, rows
        self.right, self.left, self.me, self.at_right, self.at_left, self.at_far = where
        self.near, self.far, self.step = near, far, step
        self.half = data.shape[1] // 2

    def block(self, which):
        return self.base + which * self.rows

    def begin(self):
        at = rows_at(self.block(self.at_far), self.rows)
        h = self.half
        self.one = [
            self.copies.push(self.data.at[at, pl.ds(0, h)], self.far.at[0], self.right),
            self.copies.push(self.data.at[at, pl.ds(h, h)], self.far.at[1], self.left),
        ]

    def sides(self):
        return enumerate(((self.right, self.at_right), (self.left, self.at_left)))

    def own_halves(self):
        h = self.half
        self.two = []
        for side, (device, block) in self.sides():
            at, cs = rows_at(self.block(block), self.rows), pl.ds((1 - side) * h, h)
            self.two.append(self.copies.push(self.data.at[at, cs], self.near.at[side, :, cs], device))

    def middle(self):
        h = self.half
        for side, (device, block) in self.sides():
            self.one[side].wait_recv()
            start = self.block(block)
            add_rows(self.data, start, [(self.far.at[side], 0, 0)], self.rows, side * h, h, self.step)
            at, cs = rows_at(start, self.rows), pl.ds(side * h, h)
            self.two.append(self.copies.push(self.data.at[at, cs], self.near.at[side, :, cs], device))

    def end(self):
        for copy in self.two:
            copy.wait_recv()
        add_rows(
            self.data,
            self.block(self.me),
            [(self.near.at[0], 0, 0), (self.near.at[1], 0, 0)],
            self.rows,
            0,
            2 * self.half,
            self.step,
        )


def small_add(dst, row, sources, rows):
    total = dst[row, :]
    for source in sources:
        total = total + source
    dst[row, :] = total


def second_kernel(
    hid_in, gp_in, gs_in, wu, wd, wuo, wdo, gu, gd, img, gout, std, inv, dww, gain, lscale, bdown, pbias,
    out_img, grad_img, out_up, out_down, out_small,
    guv, gdv, cu, cd, d1a, d1b, u1a, u1b, d2a, d2b, u2a, u2b, tq, fd, fu,
    nv, bv, n1, n2, b1, b2, hid, gp, wu_t, wd_t, gcv, sm, smc, sya, syb, sx, sz, smo,
    send, recv, local,
):
    me = Place()
    copies = Copies(send, recv, local)
    ring_x, ring_y, ring_z = me.ring("x"), me.ring("y"), me.ring("z")
    mate = me.at(core=me.other_core)
    x_cut = me.at(x=me.x_cut)
    x_pair = me.at(x=me.x_pair)
    x, y, z = me.x, me.y, me.z
    factor = 1.0 / math.sqrt(16384.0)

    z_far, z_right, z_left = ring_z[5], ring_z[3], ring_z[4]
    x_far, x_right, x_left = ring_x[5], ring_x[3], ring_x[4]
    order = [(0, z_far), (1, x_far), (0, z_right), (1, x_right), (0, z_left), (1, x_left), (0, z), (1, x)]
    keep = lax.rem(me.x_hi + me.core, 2)
    give = 1 - keep
    swaps, loads = [], []

    def piece(matrix, which):
        return rows_at(which * 192, 192) if matrix == 0 else rows_at(which * 768, 768)

    def fetch(index):
        m, which = order[index]
        src, mine = ((gd, gdv), (gu, guv))[m]
        at = piece(m, which)
        loads.append(copies.here(src.at[keep, at], mine.at[at]))

    wide = 768

    def up_tile(part):
        at = pl.ds(part * wide, wide)
        return [copies.here(ref.at[at], wu_t.at[part % 2, s]) for s, ref in enumerate((wu, wuo))]

    def down_tile(part):
        at = pl.ds(part * wide, wide)
        return [copies.here(ref.at[:, at], wd_t.at[part % 2, s]) for s, ref in enumerate((wd, wdo))]

    fetch(0)
    fetch(1)
    load_gp = copies.here(gp_in, gp)
    tiles = {(0, 0): up_tile(0), (0, 1): up_tile(1)}
    for index in range(2, 8):
        fetch(index)
    load_hid = copies.here(hid_in, hid)
    load_gs = copies.here(gs_in, bv)
    tiles[1, 0], tiles[1, 1] = down_tile(0), down_tile(1)
    greet([ring_x[0], ring_x[1], ring_y[0], ring_y[1], ring_z[0], ring_z[1], mate])
    for m, which in order:
        src, dst = ((gd, cd), (gu, cu))[m]
        at = piece(m, which)
        swaps.append(copies.push(src.at[give, at], dst.at[at], mate))

    def merge(index):
        m, which = order[index]
        mine, other = ((gdv, cd), (guv, cu))[m]
        rows = 192 if m == 0 else 768
        loads[index].wait()
        swaps[index].wait_recv()
        add_rows(mine, which * rows, [(other, which * rows, 0)], rows, 0, mine.shape[1], 16 if m == 0 else 64)

    rs_d1 = RingSum(copies, ring_z, gdv, 0, 192, d1b, d1a)
    rs_u1 = RingSum(copies, ring_x, guv, 0, 768, u1b, u1a)
    merge(0)
    rs_d1.begin()
    merge(1)
    rs_u1.begin()

    load_gp.wait()
    for part in range(4):
        for copy in tiles[0, part]:
            copy.wait()
        slot = part % 2
        total = lax.dot_general(gp[0], wu_t[slot, 0], NT, preferred_element_type=F32)
        total = total + lax.dot_general(gp[1], wu_t[slot, 1], NT, preferred_element_type=F32)
        nv[:, pl.ds(part * wide, wide)] = total.astype(BF16)
        if part < 2:
            tiles[0, part + 2] = up_tile(part + 2)
    rs_n = RingSum(copies, ring_y, nv, 0, ROWS, n2, n1)
    rs_n.begin()
    rs_n.own_halves()
    for index in range(2, 6):
        merge(index)
    rs_d1.own_halves()
    rs_u1.own_halves()
    load_hid.wait()
    load_gs.wait()
    for part in range(4):
        for copy in tiles[1, part]:
            copy.wait()
        slot = part % 2
        cs = pl.ds(part * wide, wide)
        total = jnp.dot(hid[0], wd_t[slot, 0], preferred_element_type=F32)
        total = total + jnp.dot(hid[1], wd_t[slot, 1], preferred_element_type=F32)
        product = jnp.sum(total * bv[:, cs].astype(F32), axis=0, keepdims=True)
        sm[53:54, cs] = product / lscale[0:1, cs]
        bv[:, cs] = total.astype(BF16)
        if part < 2:
            tiles[1, part + 2] = down_tile(part + 2)
    rs_b = RingSum(copies, ring_y, bv, 0, ROWS, b2, b1)
    rs_n.middle()
    rs_b.begin()
    rs_b.own_halves()
    rs_d1.middle()
    rs_u1.middle()
    merge(6)
    merge(7)

    rs_n.end()
    own = y * ROWS
    zero = jnp.zeros((ROWS, LANES), F32)

    def own_rows(ref, cs):
        return ref[rows_at(own, ROWS), cs].astype(F32)

    def norm_sums(block, totals):
        cs = lanes_at(block)
        grad_normed = own_rows(nv, cs)
        standard = std[:, cs]
        product = grad_normed * standard
        sm[50:51, cs] = jnp.sum(product, axis=0, keepdims=True)
        sm[51:52, cs] = jnp.sum(grad_normed, axis=0, keepdims=True)
        weight = gain[0:1, cs]
        return totals[0] + grad_normed * weight, totals[1] + product * weight

    total_g, total_gs = lax.fori_loop(0, BLOCKS, norm_sums, (zero, zero))
    mean_g = jnp.sum(total_g, axis=1, keepdims=True) * (1.0 / CH)
    mean_gs = jnp.sum(total_gs, axis=1, keepdims=True) * (1.0 / CH)
    inv_std = inv[...]

    def norm_apply(block, carry):
        cs = lanes_at(block)
        grad_hat = own_rows(nv, cs) * gain[0:1, cs]
        grad_conv = inv_std * (grad_hat - mean_g - std[:, cs] * mean_gs)
        gcv[:, cs] = grad_conv
        sm[49:50, cs] = jnp.sum(grad_conv, axis=0, keepdims=True)
        upstream = gout[:, cs].astype(F32)
        scaled = (upstream * lscale[0:1, cs]).astype(BF16).astype(F32)
        sm[52:53, cs] = jnp.sum(scaled, axis=0, keepdims=True)
        return carry

    lax.fori_loop(0, BLOCKS, norm_apply, 0)

    def conv_back(block, carry):
        cs = lanes_at(block)
        pixels = tile_rows(img, block)
        upstream = tile_rows(gout, block)
        grads = [gcv[8 * r : 8 * r + 8, cs] for r in range(16)]
        sums = upstream
        for horizontal in range(7):
            moved = [shifted(tile, 3 - horizontal) for tile in grads]
            for vertical in range(7):
                tap = vertical * 7 + horizontal
                weight = jnp.broadcast_to(dww[vertical, horizontal : horizontal + 1, cs], (8, LANES))
                taps = jnp.zeros((8, LANES), F32)
                for image in range(2):
                    for p in range(8):
                        source = p - (vertical - 3)
                        if 0 <= source < 8:
                            tile = moved[image * 8 + source]
                            sums[image * 8 + p] = sums[image * 8 + p] + tile * weight
                            taps = taps + tile * pixels[image * 8 + p]
                sm[tap : tap + 1, cs] = jnp.sum(taps, axis=0, keepdims=True)
        for r in range(8):
            grad_img[16 * r : 16 * r + 16, cs] = jnp.concatenate(sums[2 * r : 2 * r + 2], axis=0).astype(BF16)
        return carry

    lax.fori_loop(0, BLOCKS, conv_back, 0)

    def scale_block(block, carry):
        cs = lanes_at(block)
        upstream = jnp.sum(gout[:, cs].astype(F32), axis=0, keepdims=True)
        sm[53:54, cs] = sm[53:54, cs] + upstream * bdown[0:1, cs]
        return carry

    lax.fori_loop(0, BLOCKS, scale_block, 0)
    sm[54:64, :] = jnp.zeros((10, CH), F32)
    for s in range(2):
        shard = y * 2 + (me.x_hi if s == 0 else 1 - me.x_hi)
        for line in range(2):

            @pl.when(lax.div(shard, 4) == line)
            def _(s=s, line=line):
                at = pl.ds(pl.multiple_of(lax.rem(shard, 4) * HID, LANES), HID)
                sm[54 + line : 55 + line, at] = pbias[s : s + 1, :]

    swap_small = copies.push(sm.at[pl.ds(pl.multiple_of(me.other_core * 32, 8), 32)], smc, mate)
    small_rows = me.core * 32
    sm_at = pl.ds(pl.multiple_of(small_rows, 8), 32)
    yr, yl, yy, y_right, y_left, y_far = ring_y
    zr, zl = ring_z[0], ring_z[1]
    h = CH // 2
    lo, hi = pl.ds(0, h), pl.ds(h, h)

    def small_piece(which):
        return pl.ds(pl.multiple_of(small_rows + which * 8, 8), 8)

    def all_begin(buffer, ring):
        where = ring[2]
        return [
            copies.push(buffer.at[where], buffer.at[where], ring[0]),
            copies.push(buffer.at[where], buffer.at[where], ring[1]),
        ]

    def all_middle(buffer, ring, one):
        at_right, at_left = ring[3], ring[4]
        one[0].wait_recv()
        two = [copies.push(buffer.at[at_left, :, lo], buffer.at[at_left, :, lo], ring[0])]
        one[1].wait_recv()
        two.append(copies.push(buffer.at[at_right, :, hi], buffer.at[at_right, :, hi], ring[1]))
        return two

    def all_end(buffer, two):
        for copy in two:
            copy.wait_recv()
        return buffer[0] + buffer[1] + buffer[2] + buffer[3]

    rs_b.middle()
    swap_small.wait_recv()
    sm[sm_at, :] = sm[sm_at, :] + smc[...]
    s_one = [
        copies.push(sm.at[small_piece(y_far), lo], sya.at[0], yr),
        copies.push(sm.at[small_piece(y_far), hi], sya.at[1], yl),
    ]

    rs_d1.end()
    rs_d2 = RingSum(copies, ring_x, gdv, z * 192, 48, d2b, d2a)
    rs_d2.begin()
    rs_d2.own_halves()
    rs_u1.end()
    rs_u2 = RingSum(copies, ring_z, guv, x * 768, 192, u2b, u2a)
    rs_u2.begin()
    rs_u2.own_halves()

    s_two = []
    for side, (device, which) in enumerate(((yr, y_right), (yl, y_left))):
        s_one[side].wait_recv()
        at = small_piece(which)
        sm[at, pl.ds(side * h, h)] = sm[at, pl.ds(side * h, h)] + sya[side]
        s_two.append(copies.push(sm.at[at], syb.at[side], device))
    rs_d2.middle()
    rs_u2.middle()
    for side in range(2):
        s_two[side].wait_recv()
    at = small_piece(yy)
    sx[pl.ds(x, 1)] = (sm[at, :] + syb[0] + syb[1])[None]
    sx_one = all_begin(sx, ring_x)

    rs_d2.end()
    at_d = z * 192 + x * 48
    at_u = x * 768 + z * 192
    fd[...] = (gdv[rows_at(at_d, 48), :].astype(F32) * factor).astype(BF16)
    needed = me.x_hi == me.core

    def drow(which_x):
        return rows_at(z * 192 + which_x * 48, 48)

    d_cut = copies.remote(fd, out_down.at[drow(x)], x_cut)
    d_swap = copies.remote(fd, out_down.at[drow(x)], x_pair)
    d_cut_swap = copies.remote(out_down.at[drow(me.x_cut)], out_down.at[drow(me.x_cut)], x_pair)
    d_own = pltpu.make_async_copy(fd, out_down.at[drow(x)], local.at[62])

    @pl.when(jnp.logical_not(needed))
    def _():
        d_cut.start()

    @pl.when(needed)
    def _():
        d_own.start()
        d_swap.start()

    rs_u2.end()
    fu[...] = (guv[rows_at(at_u, 192), :].astype(F32) * factor).astype(BF16)

    def slot(which):
        return rows_at(which * 192, 192)

    tq_own = copies.here(fu, tq.at[slot(z)])
    up_one = [copies.push(fu, tq.at[slot(z)], zr), copies.push(fu, tq.at[slot(z)], zl)]
    sx_two = all_middle(sx, ring_x, sx_one)

    rs_b.end()

    def result_block(block, carry):
        cs = lanes_at(block)
        branch = own_rows(bv, cs) + bdown[0:1, cs]
        out_img[:, cs] = (img[:, cs].astype(F32) + lscale[0:1, cs] * branch).astype(BF16)
        return carry

    lax.fori_loop(0, BLOCKS, result_block, 0)

    @pl.when(needed)
    def _():
        d_cut.wait_recv()
        d_cut_swap.start()

    sz[pl.ds(z, 1)] = all_end(sx, sx_two)[None]
    sz_one = all_begin(sz, ring_z)
    hu = HID // 2
    z_left_slot, z_right_slot = slot(z_left), slot(z_right)
    up_one[0].wait_recv()
    up_two = [copies.push(tq.at[z_left_slot, pl.ds(0, hu)], tq.at[z_left_slot, pl.ds(0, hu)], zr)]
    up_one[1].wait_recv()
    up_two.append(copies.push(tq.at[z_right_slot, pl.ds(hu, hu)], tq.at[z_right_slot, pl.ds(hu, hu)], zl))
    sz_two = all_middle(sz, ring_z, sz_one)

    def dblock(which):
        return rows_at(which * 192, 192)

    block = dblock(z)
    d_right = copies.remote(out_down.at[block], out_down.at[block], zr)
    d_left = copies.remote(out_down.at[block], out_down.at[block], zl)
    d_mate = copies.remote(out_down.at[block], out_down.at[block], mate)

    @pl.when(needed)
    def _():
        d_own.wait()
        d_swap.wait_recv()
        d_cut_swap.wait_recv()
        d_right.start()
        d_left.start()
        d_mate.start()

    for copy in up_two:
        copy.wait_recv()
    tq_own.wait()

    def urow(which_x):
        return rows_at(which_x * 768, 768)

    u_cut = copies.remote(tq, out_up.at[urow(x)], x_cut)
    u_swap = copies.remote(tq, out_up.at[urow(x)], x_pair)
    u_mate = copies.remote(tq, out_up.at[urow(x)], mate)
    u_own = pltpu.make_async_copy(tq, out_up.at[urow(x)], local.at[63])

    @pl.when(jnp.logical_not(needed))
    def _():
        u_cut.start()

    @pl.when(needed)
    def _():
        u_swap.start()
        u_mate.start()
        u_own.start()

    total = all_end(sz, sz_two)
    smo_at = small_piece(yy)
    smo[smo_at, :] = total * factor
    so_one = [
        copies.push(smo.at[smo_at], smo.at[smo_at], yr),
        copies.push(smo.at[smo_at], smo.at[smo_at], yl),
    ]
    from_left, from_right = small_piece(y_left), small_piece(y_right)
    so_one[0].wait_recv()
    so_two = [copies.push(smo.at[from_left, lo], smo.at[from_left, lo], yr)]
    so_one[1].wait_recv()
    so_two.append(copies.push(smo.at[from_right, hi], smo.at[from_right, hi], yl))
    for copy in so_two:
        copy.wait_recv()
    small_mate = copies.push(smo.at[sm_at], smo.at[sm_at], mate)

    block_l, block_r, block_f = dblock(z_left), dblock(z_right), dblock(z_far)
    d_fwd_right = copies.remote(out_down.at[block_l, lo], out_down.at[block_l, lo], zr)
    d_fwd_left = copies.remote(out_down.at[block_r, hi], out_down.at[block_r, hi], zl)
    d_mate_l = copies.remote(out_down.at[block_l], out_down.at[block_l], mate)
    d_mate_r = copies.remote(out_down.at[block_r], out_down.at[block_r], mate)
    d_mate_f = copies.remote(out_down.at[block_f], out_down.at[block_f], mate)
    q_cut, q_pair, q_far = urow(me.x_cut), urow(me.x_pair), urow(3 - me.x_pair)
    u_cut_swap = copies.remote(out_up.at[q_cut], out_up.at[q_cut], x_pair)
    u_mate_c = copies.remote(out_up.at[q_cut], out_up.at[q_cut], mate)
    u_mate_p = copies.remote(out_up.at[q_pair], out_up.at[q_pair], mate)
    u_mate_f = copies.remote(out_up.at[q_far], out_up.at[q_far], mate)

    @pl.when(needed)
    def _():
        u_cut.wait_recv()
        u_cut_swap.start()
        u_mate_c.start()
        d_right.wait_recv()
        d_fwd_right.start()
        d_mate_l.start()
        d_left.wait_recv()
        d_fwd_left.start()
        d_mate_r.start()
        u_swap.wait_recv()
        u_mate_p.start()
        d_fwd_right.wait_recv()
        d_fwd_left.wait_recv()
        d_mate_f.start()
        u_cut_swap.wait_recv()
        u_mate_f.start()
        u_own.wait()
        for copy in (
            d_swap, d_cut_swap, d_right, d_left, d_mate, d_fwd_right, d_fwd_left, d_mate_l, d_mate_r, d_mate_f,
            u_swap, u_mate, u_cut_swap, u_mate_c, u_mate_p, u_mate_f,
        ):
            copy.wait_send()

    @pl.when(jnp.logical_not(needed))
    def _():
        for copy in (d_mate, d_mate_l, d_mate_r, d_mate_f, u_mate, u_mate_c, u_mate_p, u_mate_f):
            copy.wait_recv()
        d_cut.wait_send()
        u_cut.wait_send()

    small_mate.wait_recv()
    out_small[...] = smo[...]
    copies.drain()


def second_call(*operands):
    remote = 104
    bf = lambda *shape: pltpu.VMEM(shape, BF16)
    fl = lambda *shape: pltpu.VMEM(shape, F32)
    return pl.pallas_call(
        second_kernel,
        out_shape=(
            jax.ShapeDtypeStruct((ROWS, CH), BF16),
            jax.ShapeDtypeStruct((ROWS, CH), BF16),
            jax.ShapeDtypeStruct((CH, HID), BF16),
            jax.ShapeDtypeStruct((HID, CH), BF16),
            jax.ShapeDtypeStruct((64, CH), F32),
        ),
        in_specs=[ANY] * 9 + [VMEM] * 9,
        out_specs=(VMEM, VMEM, ANY, ANY, VMEM),
        scratch_shapes=[
            bf(CH, HID), bf(HID, CH), bf(CH, HID), bf(HID, CH),
            bf(2, 192, 1536), bf(2, 192, 3072), bf(2, 768, 384), bf(2, 768, 768),
            bf(2, 48, 1536), bf(2, 48, 3072), bf(2, 192, 384), bf(2, 192, 768),
            bf(768, 768), bf(48, 3072), bf(192, 768),
            bf(512, CH), bf(512, CH),
            bf(2, 128, 1536), bf(2, 128, 3072), bf(2, 128, 1536), bf(2, 128, 3072),
            bf(2, 512, HID), bf(2, 512, HID), bf(2, 2, 768, HID), bf(2, 2, HID, 768),
            fl(ROWS, CH), fl(64, CH), fl(32, CH), fl(2, 8, 1536), fl(2, 8, CH),
            fl(4, 8, CH), fl(4, 8, CH), fl(64, CH),
            pltpu.SemaphoreType.DMA((remote,)),
            pltpu.SemaphoreType.DMA((remote,)),
            pltpu.SemaphoreType.DMA((64,)),
        ],
        compiler_params=pltpu.CompilerParams(
            collective_id=1, has_side_effects=True, vmem_limit_bytes=63 * 1024 * 1024
        ),
    )(*operands)


def last_kernel(oimg, gimg, up, down, small, o1, o2, o3, o4, dw, r1, r2, r3, r4, r5, gb, v1, v2, v3, v4, load, store):
    trips = [(oimg, v1, o1), (gimg, v2, o2)]
    for part in range(4):
        rows = pl.ds(part * 768, 768)
        trips.append((up.at[rows], v3.at[rows], o3.at[rows]))
    for part in range(4):
        rows = pl.ds(part * 192, 192)
        trips.append((down.at[rows], v4.at[rows], o4.at[rows]))
    loads = [pltpu.make_async_copy(src, mid, load.at[i]) for i, (src, mid, dst) in enumerate(trips)]
    stores = [pltpu.make_async_copy(mid, dst, store.at[i]) for i, (src, mid, dst) in enumerate(trips)]
    for move in loads:
        move.start()
    for vertical in range(7):
        dw[vertical] = small[vertical * 7 : vertical * 7 + 7, :]
    for index, ref in enumerate((r1, r2, r3, r4, r5)):
        ref[...] = small[49 + index, :]
    shard = lax.axis_index("fsdp")
    at = pl.ds(pl.multiple_of(lax.rem(shard, 4) * HID, LANES), HID)
    line = lax.div(shard, 4)
    gb[...] = jnp.where(line == 0, small[54:55, at], small[55:56, at]).astype(BF16)
    for first, second in zip(loads, stores):
        first.wait()
        second.start()
    for move in stores:
        move.wait()


def last_call(oimg, gimg, up, down, small):
    wide = jax.ShapeDtypeStruct((ROWS, CH), BF16)
    line = jax.ShapeDtypeStruct((CH,), F32)
    return pl.pallas_call(
        last_kernel,
        out_shape=(
            wide,
            wide,
            jax.ShapeDtypeStruct((CH, HID), BF16),
            jax.ShapeDtypeStruct((HID, CH), BF16),
            jax.ShapeDtypeStruct((7, 7, CH), F32),
            line,
            line,
            line,
            line,
            line,
            jax.ShapeDtypeStruct((1, HID), BF16),
        ),
        in_specs=[ANY] * 4 + [VMEM],
        out_specs=tuple([ANY] * 4 + [VMEM] * 7),
        scratch_shapes=[
            pltpu.VMEM((ROWS, CH), BF16),
            pltpu.VMEM((ROWS, CH), BF16),
            pltpu.VMEM((CH, HID), BF16),
            pltpu.VMEM((HID, CH), BF16),
            pltpu.SemaphoreType.DMA((10,)),
            pltpu.SemaphoreType.DMA((10,)),
        ],
        compiler_params=pltpu.CompilerParams(vmem_limit_bytes=62 * 1024 * 1024),
    )(oimg, gimg, up, down, small)


def on_device(
    images, grad_out, dw_weight, dw_bias, ln_gain, ln_bias, w_up, b_up, w_down, b_down, layer_scale
):
    img = images.reshape(ROWS, CH)
    gout = grad_out.reshape(ROWS, CH)
    row = lambda vector: vector.reshape(1, CH)
    std, inv, hid, gp, gs, wuo, wdo, grad_up, grad_down, pbias = first_call(
        img, gout, dw_weight, row(dw_bias), row(ln_gain), row(ln_bias), row(layer_scale), w_up, w_down, b_up
    )
    out_img, grad_img, out_up, out_down, small = second_call(
        hid, gp, gs, w_up, w_down, wuo, wdo, grad_up, grad_down, img, gout, std, inv, dw_weight, row(ln_gain), row(layer_scale), row(b_down), pbias
    )
    oimg, gimg, up, down, dw, r1, r2, r3, r4, r5, gb = last_call(out_img, grad_img, out_up, out_down, small)
    return (
        oimg.reshape(images.shape),
        gimg.reshape(images.shape),
        up,
        gb.reshape(HID),
        down,
        dw,
        r1,
        r2,
        r3,
        r4,
        r5,
    )


def solution(mesh):
    tokens = P(("dp", "fsdp"), None, None, None)
    up, bias, down = P(None, "fsdp"), P("fsdp"), P("fsdp", None)
    return jax.shard_map(
        on_device,
        mesh=mesh,
        in_specs=(tokens, tokens, P(), P(), P(), P(), up, bias, down, P(), P()),
        out_specs=(tokens, tokens, up, bias, down, P(), P(), P(), P(), P(), P()),
        check_vma=False,
    )
```

```python
import math

import jax
import jax.numpy as jnp
from jax import lax
from jax.experimental import pallas as pl
from jax.experimental.pallas import tpu as pltpu
from jax.sharding import PartitionSpec as P

MESH = pl.DeviceIdType.MESH
F32 = jnp.float32
BF16 = jnp.bfloat16
CH = 3072
HID = 768
ROWS = 128
LANES = 128
BLOCKS = CH // LANES
ANY = pl.BlockSpec(memory_space=pl.ANY)
VMEM = pl.BlockSpec(memory_space=pltpu.VMEM)


class Place:
    def __init__(self):
        d = lax.axis_index("dp")
        f = lax.axis_index("fsdp")
        self.z = lax.div(d, 4)
        self.x_lo = lax.rem(lax.div(d, 2), 2)
        self.core = lax.rem(d, 2)
        self.y = lax.div(f, 2)
        self.x_hi = lax.rem(f, 2)
        self.x = self.x_hi * 2 + self.x_lo
        self.other_core = 1 - self.core
        self.x_cut = 3 - self.x
        self.x_pair = self.x_hi * 2 + (1 - self.x_lo)

    def at(self, x=None, y=None, z=None, core=None):
        x = self.x if x is None else x
        y = self.y if y is None else y
        z = self.z if z is None else z
        core = self.core if core is None else core
        return (z * 4 + lax.rem(x, 2) * 2 + core, y * 2 + lax.div(x, 2))

    def ring(self, axis):
        me = getattr(self, axis)
        right, left, far = lax.rem(me + 1, 4), lax.rem(me + 3, 4), lax.rem(me + 2, 4)
        return self.at(**{axis: right}), self.at(**{axis: left}), me, right, left, far


class Copies:
    def __init__(self, send, recv, local):
        self.send, self.recv, self.local = send, recv, local
        self.used = 0
        self.used_local = 0
        self.sent = []

    def remote(self, src, dst, device):
        index = self.used
        self.used += 1
        return pltpu.make_async_remote_copy(
            src_ref=src,
            dst_ref=dst,
            send_sem=self.send.at[index],
            recv_sem=self.recv.at[index],
            device_id=device,
            device_id_type=MESH,
        )

    def push(self, src, dst, device):
        copy = self.remote(src, dst, device)
        copy.start()
        self.sent.append(copy)
        return copy

    def here(self, src, dst):
        index = self.used_local
        self.used_local += 1
        copy = pltpu.make_async_copy(src, dst, self.local.at[index])
        copy.start()
        return copy

    def drain(self):
        for copy in self.sent:
            copy.wait_send()


def greet(devices):
    barrier = pltpu.get_barrier_semaphore()
    for device in devices:
        pl.semaphore_signal(barrier, inc=1, device_id=device, device_id_type=MESH)
    pl.semaphore_wait(barrier, len(devices))


def rows_at(start, size):
    return pl.ds(pl.multiple_of(start, 16), size)


def lanes_at(block):
    return pl.ds(pl.multiple_of(block * LANES, LANES), LANES)


def shifted(row, by):
    if by == 0:
        return row
    moved = pltpu.roll(row, (-by) % 8, 0)
    place = lax.broadcasted_iota(jnp.int32, row.shape, 0)
    inside = (place + by >= 0) & (place + by < 8)
    return jnp.where(inside, moved, 0.0)


def tile_rows(ref, block):
    tiles = []
    for pair in range(8):
        both = ref[16 * pair : 16 * pair + 16, lanes_at(block)].astype(F32)
        tiles += [both[:8], both[8:]]
    return tiles


def conv_block(block, img, dww, dwb, out):
    pixels = tile_rows(img, block)
    cs = lanes_at(block)
    sums = [jnp.broadcast_to(dwb[0:1, cs], (8, LANES))] * 16
    for horizontal in range(7):
        moved = [shifted(tile, horizontal - 3) for tile in pixels]
        for vertical in range(7):
            weight = jnp.broadcast_to(dww[vertical, horizontal : horizontal + 1, cs], (8, LANES))
            for image in range(2):
                for p in range(8):
                    source = p + vertical - 3
                    if 0 <= source < 8:
                        sums[image * 8 + p] = sums[image * 8 + p] + moved[image * 8 + source] * weight
    for r in range(16):
        out[8 * r : 8 * r + 8, cs] = sums[r]


def gelu_parts(values):
    cdf = 0.5 * (1.0 + lax.erf(values * 0.7071067811865476))
    return values * cdf, cdf + values * jnp.exp(-0.5 * values * values) * 0.3989422804014327


NT = (((1,), (1,)), ((), ()))
TN = (((0,), (0,)), ((), ()))


def first_kernel(
    img, gout, dww, dwb, gain, shift, lscale, wu, wd, bu,
    std, inv, hid_out, gp_out, gs_out, wu_out, wd_out, grad_up, grad_down, bias_sums,
    gn, gs, wuv, wdv, b_own, bo, hid, gp, keep32, up_v, down_v,
    send, recv, local,
):
    me = Place()
    copies = Copies(send, recv, local)
    right, left, y, y_right, y_left, y_far = me.ring("y")
    cut = me.at(x=me.x_cut)
    pair = me.at(x=me.x_pair)
    mate = me.at(core=me.other_core)
    wu_load = copies.here(wu, wuv.at[0])
    wd_load = copies.here(wd, wdv.at[0])
    b_own[...] = jnp.broadcast_to(bu[...][None, :], (8, HID))
    z_right_chip, z_left_chip, z, z_right, z_left, z_far = me.ring("z")
    greet([right, left, cut, pair, mate, z_right_chip, z_left_chip])

    weights = (wuv.at[1], wdv.at[1])
    sizes = (192, 48)
    sides = (me.x_lo, 1 - me.x_lo)

    def piece(m, side, which):
        return rows_at((side * 8 + which * 2 + me.core) * sizes[m], sizes[m])

    def held(m, k, which):
        return weights[m].at[piece(m, sides[k], which)]

    bias = copies.push(b_own, bo, cut)
    over_cut = []
    for m in range(2):
        at = piece(m, sides[1], z)
        over_cut.append(copies.push((wu, wd)[m].at[at], weights[m].at[at], cut))
    swapped, ring_one, ring_two, mates = {}, {}, {}, {0: [], 1: []}

    def to_mate(m, ref):
        mates[m].append(copies.push(ref, ref, mate))

    def around(m, k):
        ref = held(m, k, z)
        ring_one[m, k] = copies.push(ref, ref, z_right_chip), copies.push(ref, ref, z_left_chip)
        to_mate(m, ref)

    def from_cut(m):
        over_cut[m].wait_recv()
        ref = held(m, 0, z)
        swapped[m] = copies.push(ref, ref, pair)
        around(m, 0)

    def from_pair(m):
        swapped[m].wait_recv()
        around(m, 1)

    def from_ring(m, k):
        width = (HID, CH)[m] // 2
        ring_one[m, k][0].wait_recv()
        ref = held(m, k, z_left)
        part = weights[m].at[piece(m, sides[k], z_left), pl.ds(0, width)]
        one = copies.push(part, part, z_right_chip)
        to_mate(m, ref)
        ring_one[m, k][1].wait_recv()
        ref = held(m, k, z_right)
        part = weights[m].at[piece(m, sides[k], z_right), pl.ds(width, width)]
        ring_two[m, k] = one, copies.push(part, part, z_left_chip)
        to_mate(m, ref)

    def from_far(m, k):
        for copy in ring_two[m, k]:
            copy.wait_recv()
        to_mate(m, held(m, k, z_far))

    def arrived(m):
        for copy in mates[m]:
            copy.wait_recv()

    own = rows_at(y * ROWS, ROWS)

    def scale_block(block, carry):
        cs = lanes_at(block)
        gs[own, cs] = (gout[:, cs].astype(F32) * lscale[0:1, cs]).astype(BF16)
        return carry

    lax.fori_loop(0, BLOCKS, scale_block, 0)

    half = ROWS // 2

    def halves(position):
        return rows_at(position * ROWS, half), rows_at(position * ROWS + half, half)

    def spread(buffer):
        low, high = halves(y)
        first = [copies.push(buffer.at[low], buffer.at[low], right), copies.push(buffer.at[high], buffer.at[high], left)]
        second = [copies.push(buffer.at[high], buffer.at[high], right), copies.push(buffer.at[low], buffer.at[low], left)]
        return first, second

    def forward(first, buffer):
        low, high = halves(y_left)[0], halves(y_right)[1]
        first[0].wait_recv()
        to_right = copies.push(buffer.at[low], buffer.at[low], right)
        first[1].wait_recv()
        to_left = copies.push(buffer.at[high], buffer.at[high], left)
        return [to_right, to_left]

    s_first, s_second = spread(gs)

    def conv_step(block, carry):
        conv_block(block, img, dww, dwb, std)
        return carry

    lax.fori_loop(0, BLOCKS // 2, conv_step, 0)
    from_cut(0)
    lax.fori_loop(BLOCKS // 2, BLOCKS, conv_step, 0)

    def add_block(block, total):
        return total + std[:, lanes_at(block)]

    zero = jnp.zeros((ROWS, LANES), F32)
    mean = jnp.sum(lax.fori_loop(0, BLOCKS, add_block, zero), axis=1, keepdims=True) * (1.0 / CH)

    def square_block(block, total):
        centred = std[:, lanes_at(block)] - mean
        return total + centred * centred

    variance = jnp.sum(lax.fori_loop(0, BLOCKS, square_block, zero), axis=1, keepdims=True) * (1.0 / CH)
    inv_std = lax.rsqrt(variance + 1e-06)
    inv[...] = jnp.broadcast_to(inv_std, (ROWS, LANES))

    def norm_block(block, carry):
        cs = lanes_at(block)
        standard = (std[:, cs] - mean) * inv_std
        std[:, cs] = standard
        gn[own, cs] = (standard * gain[0:1, cs] + shift[0:1, cs]).astype(BF16)
        return carry

    lax.fori_loop(0, BLOCKS, norm_block, 0)
    n_first, n_second = spread(gn)
    s_last = forward(s_first, gs)
    from_cut(1)

    tile = 256

    def hidden_tile(index):
        return pl.ds(pl.multiple_of(index * tile, tile), tile)

    bias_sums[...] = jnp.zeros_like(bias_sums)

    def own_grad_hidden():
        def body(index, carry):
            cs = hidden_tile(index)
            keep32[0, :, cs] = lax.dot_general(gs[...], wdv[0, cs, :], NT, preferred_element_type=F32)
            return carry

        lax.fori_loop(0, HID // tile, body, 0)

    def up_rows_of(s, position):
        at = rows_at(position * ROWS, ROWS)
        pre = jnp.dot(gn[at, :], wuv[s], preferred_element_type=F32)
        value, slope = gelu_parts(pre + (b_own if s == 0 else bo)[0:1, :])
        hid[s, at, :] = value.astype(BF16)
        if s == 0:
            grad = (keep32[0, at, :] * slope).astype(BF16)
            gp[0, at, :] = grad
            bias_sums[0:1, :] = bias_sums[0:1, :] + jnp.sum(grad.astype(F32), axis=0, keepdims=True)
        else:
            keep32[1, at, :] = slope

    def other_grad():
        def body(index, carry):
            cs = hidden_tile(index)
            grad = lax.dot_general(gs[...], wdv[1, cs, :], NT, preferred_element_type=F32)
            pre = (grad * keep32[1, :, cs]).astype(BF16)
            gp[1, :, cs] = pre
            bias_sums[1:2, cs] = jnp.sum(pre.astype(F32), axis=0, keepdims=True)
            return carry

        lax.fori_loop(0, HID // tile, body, 0)

    outs = []

    def part_place(matrix, s, part):
        if matrix == 0:
            at = (pl.ds(part * 768, 768), slice(None))
            outs.append(copies.here(up_v.at[(s,) + at], grad_up.at[(s,) + at]))
        else:
            at = (slice(None), pl.ds(part * 768, 768))
            outs.append(copies.here(down_v.at[(s,) + at], grad_down.at[(s,) + at]))

    def part_up(s):
        for part in range(4):
            rows = pl.ds(part * 768, 768)
            up_v[s, rows, :] = lax.dot_general(gn[:, rows], gp[s], TN, preferred_element_type=F32).astype(BF16)
            part_place(0, s, part)

    def part_down(s):
        for part in range(4):
            cs = pl.ds(part * 768, 768)
            down_v[s, :, cs] = lax.dot_general(hid[s], gs[:, cs], TN, preferred_element_type=F32).astype(BF16)
            part_place(1, s, part)

    from_pair(0)
    from_ring(0, 0)
    from_pair(1)
    from_ring(0, 1)
    wu_load.wait()
    wd_load.wait()
    for copy in s_second + s_last:
        copy.wait_recv()
    own_grad_hidden()
    n_last = forward(n_first, gn)
    from_ring(1, 0)
    from_ring(1, 1)
    up_rows_of(0, y)
    from_far(0, 0)
    from_far(0, 1)
    bias.wait_recv()
    for copy in n_second:
        copy.wait_recv()
    up_rows_of(0, y_right)
    up_rows_of(0, y_left)
    from_far(1, 0)
    from_far(1, 1)
    arrived(0)
    up_rows_of(1, y)
    up_rows_of(1, y_right)
    up_rows_of(1, y_left)
    for copy in n_last:
        copy.wait_recv()
    up_rows_of(0, y_far)
    up_rows_of(1, y_far)
    part_down(0)
    part_up(0)
    part_down(1)
    arrived(1)
    outs.append(copies.here(wuv.at[1], wu_out))
    outs.append(copies.here(wdv.at[1], wd_out))
    outs.append(copies.here(hid, hid_out))
    outs.append(copies.here(gs, gs_out))
    other_grad()
    outs.append(copies.here(gp, gp_out))
    part_up(1)
    for copy in outs:
        copy.wait()
    copies.drain()


def first_call(img, gout, dww, dwb, gain, shift, lscale, wu, wd, bu):
    remote = 64
    rows = 4 * ROWS
    return pl.pallas_call(
        first_kernel,
        out_shape=(
            jax.ShapeDtypeStruct((ROWS, CH), F32),
            jax.ShapeDtypeStruct((ROWS, LANES), F32),
            jax.ShapeDtypeStruct((2, rows, HID), BF16),
            jax.ShapeDtypeStruct((2, rows, HID), BF16),
            jax.ShapeDtypeStruct((rows, CH), BF16),
            jax.ShapeDtypeStruct((CH, HID), BF16),
            jax.ShapeDtypeStruct((HID, CH), BF16),
            jax.ShapeDtypeStruct((2, CH, HID), BF16),
            jax.ShapeDtypeStruct((2, HID, CH), BF16),
            jax.ShapeDtypeStruct((8, HID), F32),
        ),
        in_specs=[VMEM] * 7 + [ANY, ANY, VMEM],
        out_specs=(VMEM, VMEM, ANY, ANY, ANY, ANY, ANY, ANY, ANY, VMEM),
        scratch_shapes=[
            pltpu.VMEM((rows, CH), BF16),
            pltpu.VMEM((rows, CH), BF16),
            pltpu.VMEM((2, CH, HID), BF16),
            pltpu.VMEM((2, HID, CH), BF16),
            pltpu.VMEM((8, HID), F32),
            pltpu.VMEM((8, HID), F32),
            pltpu.VMEM((2, rows, HID), BF16),
            pltpu.VMEM((2, rows, HID), BF16),
            pltpu.VMEM((2, rows, HID), F32),
            pltpu.VMEM((2, CH, HID), BF16),
            pltpu.VMEM((2, HID, CH), BF16),
            pltpu.SemaphoreType.DMA((remote,)),
            pltpu.SemaphoreType.DMA((remote,)),
            pltpu.SemaphoreType.DMA((32,)),
        ],
        compiler_params=pltpu.CompilerParams(
            collective_id=0, has_side_effects=True, vmem_limit_bytes=62 * 1024 * 1024
        ),
    )(img, gout, dww, dwb, gain, shift, lscale, wu, wd, bu)


def add_rows(dst, dst_row, sources, rows, column, columns, step=16):
    def body(index, carry):
        at = rows_at(dst_row + index * step, step)
        cs = pl.ds(column, columns)
        total = dst[at, cs].astype(F32)
        for ref, row, first in sources:
            total = total + ref[rows_at(row + index * step, step), pl.ds(first, columns)].astype(F32)
        dst[at, cs] = total.astype(dst.dtype)
        return carry

    lax.fori_loop(0, rows // step, body, 0)


class RingSum:
    def __init__(self, copies, where, data, base, rows, near, far, step=16):
        self.copies, self.data, self.base, self.rows = copies, data, base, rows
        self.right, self.left, self.me, self.at_right, self.at_left, self.at_far = where
        self.near, self.far, self.step = near, far, step
        self.half = data.shape[1] // 2

    def block(self, which):
        return self.base + which * self.rows

    def begin(self):
        at = rows_at(self.block(self.at_far), self.rows)
        h = self.half
        self.one = [
            self.copies.push(self.data.at[at, pl.ds(0, h)], self.far.at[0], self.right),
            self.copies.push(self.data.at[at, pl.ds(h, h)], self.far.at[1], self.left),
        ]

    def sides(self):
        return enumerate(((self.right, self.at_right), (self.left, self.at_left)))

    def own_halves(self):
        h = self.half
        self.two = []
        for side, (device, block) in self.sides():
            at, cs = rows_at(self.block(block), self.rows), pl.ds((1 - side) * h, h)
            self.two.append(self.copies.push(self.data.at[at, cs], self.near.at[side, :, cs], device))

    def middle(self):
        h = self.half
        for side, (device, block) in self.sides():
            self.one[side].wait_recv()
            start = self.block(block)
            add_rows(self.data, start, [(self.far.at[side], 0, 0)], self.rows, side * h, h, self.step)
            at, cs = rows_at(start, self.rows), pl.ds(side * h, h)
            self.two.append(self.copies.push(self.data.at[at, cs], self.near.at[side, :, cs], device))

    def end(self):
        for copy in self.two:
            copy.wait_recv()
        add_rows(
            self.data,
            self.block(self.me),
            [(self.near.at[0], 0, 0), (self.near.at[1], 0, 0)],
            self.rows,
            0,
            2 * self.half,
            self.step,
        )


def small_add(dst, row, sources, rows):
    total = dst[row, :]
    for source in sources:
        total = total + source
    dst[row, :] = total


def second_kernel(
    hid_in, gp_in, gs_in, wu, wd, wuo, wdo, gu, gd, img, gout, std, inv, dww, gain, lscale, bdown, pbias,
    out_img, grad_img, out_up, out_down, out_small,
    guv, gdv, cu, cd, d1a, d1b, u1a, u1b, d2a, d2b, u2a, u2b, tq, fd, fu,
    nv, bv, n1, n2, b1, b2, hid, gp, wu_t, wd_t, gcv, sm, smc, sya, syb, sx, sz, smo,
    send, recv, local,
):
    me = Place()
    copies = Copies(send, recv, local)
    ring_x, ring_y, ring_z = me.ring("x"), me.ring("y"), me.ring("z")
    mate = me.at(core=me.other_core)
    x_cut = me.at(x=me.x_cut)
    x_pair = me.at(x=me.x_pair)
    x, y, z = me.x, me.y, me.z
    factor = 1.0 / math.sqrt(16384.0)

    z_far, z_right, z_left = ring_z[5], ring_z[3], ring_z[4]
    x_far, x_right, x_left = ring_x[5], ring_x[3], ring_x[4]
    order = [(0, z_far), (1, x_far), (0, z_right), (1, x_right), (0, z_left), (1, x_left), (0, z), (1, x)]
    keep = lax.rem(me.x_hi + me.core, 2)
    give = 1 - keep
    swaps, loads = [], []

    def piece(matrix, which):
        return rows_at(which * 192, 192) if matrix == 0 else rows_at(which * 768, 768)

    def fetch(index):
        m, which = order[index]
        src, mine = ((gd, gdv), (gu, guv))[m]
        at = piece(m, which)
        loads.append(copies.here(src.at[keep, at], mine.at[at]))

    wide = 768

    def up_tile(part):
        at = pl.ds(part * wide, wide)
        return [copies.here(ref.at[at], wu_t.at[part % 2, s]) for s, ref in enumerate((wu, wuo))]

    def down_tile(part):
        at = pl.ds(part * wide, wide)
        return [copies.here(ref.at[:, at], wd_t.at[part % 2, s]) for s, ref in enumerate((wd, wdo))]

    fetch(0)
    fetch(1)
    load_gp = copies.here(gp_in, gp)
    tiles = {(0, 0): up_tile(0), (0, 1): up_tile(1)}
    for index in range(2, 8):
        fetch(index)
    load_hid = copies.here(hid_in, hid)
    load_gs = copies.here(gs_in, bv)
    tiles[1, 0], tiles[1, 1] = down_tile(0), down_tile(1)
    greet([ring_x[0], ring_x[1], ring_y[0], ring_y[1], ring_z[0], ring_z[1], mate])
    for m, which in order:
        src, dst = ((gd, cd), (gu, cu))[m]
        at = piece(m, which)
        swaps.append(copies.push(src.at[give, at], dst.at[at], mate))

    def merge(index):
        m, which = order[index]
        mine, other = ((gdv, cd), (guv, cu))[m]
        rows = 192 if m == 0 else 768
        loads[index].wait()
        swaps[index].wait_recv()
        add_rows(mine, which * rows, [(other, which * rows, 0)], rows, 0, mine.shape[1], 16 if m == 0 else 64)

    rs_d1 = RingSum(copies, ring_z, gdv, 0, 192, d1b, d1a)
    rs_u1 = RingSum(copies, ring_x, guv, 0, 768, u1b, u1a)
    merge(0)
    rs_d1.begin()
    merge(1)
    rs_u1.begin()

    load_gp.wait()
    for part in range(4):
        for copy in tiles[0, part]:
            copy.wait()
        slot = part % 2
        total = lax.dot_general(gp[0], wu_t[slot, 0], NT, preferred_element_type=F32)
        total = total + lax.dot_general(gp[1], wu_t[slot, 1], NT, preferred_element_type=F32)
        nv[:, pl.ds(part * wide, wide)] = total.astype(BF16)
        if part < 2:
            tiles[0, part + 2] = up_tile(part + 2)
    rs_n = RingSum(copies, ring_y, nv, 0, ROWS, n2, n1)
    rs_n.begin()
    rs_n.own_halves()
    for index in range(2, 6):
        merge(index)
    rs_d1.own_halves()
    rs_u1.own_halves()
    load_hid.wait()
    load_gs.wait()
    for part in range(4):
        for copy in tiles[1, part]:
            copy.wait()
        slot = part % 2
        cs = pl.ds(part * wide, wide)
        total = jnp.dot(hid[0], wd_t[slot, 0], preferred_element_type=F32)
        total = total + jnp.dot(hid[1], wd_t[slot, 1], preferred_element_type=F32)
        product = jnp.sum(total * bv[:, cs].astype(F32), axis=0, keepdims=True)
        sm[53:54, cs] = product / lscale[0:1, cs]
        bv[:, cs] = total.astype(BF16)
        if part < 2:
            tiles[1, part + 2] = down_tile(part + 2)
    rs_b = RingSum(copies, ring_y, bv, 0, ROWS, b2, b1)
    rs_n.middle()
    rs_b.begin()
    rs_b.own_halves()
    rs_d1.middle()
    rs_u1.middle()
    merge(6)
    merge(7)

    rs_n.end()
    own = y * ROWS
    zero = jnp.zeros((ROWS, LANES), F32)

    def own_rows(ref, cs):
        return ref[rows_at(own, ROWS), cs].astype(F32)

    def norm_sums(block, totals):
        cs = lanes_at(block)
        grad_normed = own_rows(nv, cs)
        standard = std[:, cs]
        product = grad_normed * standard
        sm[50:51, cs] = jnp.sum(product, axis=0, keepdims=True)
        sm[51:52, cs] = jnp.sum(grad_normed, axis=0, keepdims=True)
        weight = gain[0:1, cs]
        return totals[0] + grad_normed * weight, totals[1] + product * weight

    total_g, total_gs = lax.fori_loop(0, BLOCKS, norm_sums, (zero, zero))
    mean_g = jnp.sum(total_g, axis=1, keepdims=True) * (1.0 / CH)
    mean_gs = jnp.sum(total_gs, axis=1, keepdims=True) * (1.0 / CH)
    inv_std = inv[...]

    def norm_apply(block, carry):
        cs = lanes_at(block)
        grad_hat = own_rows(nv, cs) * gain[0:1, cs]
        grad_conv = inv_std * (grad_hat - mean_g - std[:, cs] * mean_gs)
        gcv[:, cs] = grad_conv
        sm[49:50, cs] = jnp.sum(grad_conv, axis=0, keepdims=True)
        upstream = gout[:, cs].astype(F32)
        scaled = (upstream * lscale[0:1, cs]).astype(BF16).astype(F32)
        sm[52:53, cs] = jnp.sum(scaled, axis=0, keepdims=True)
        return carry

    lax.fori_loop(0, BLOCKS, norm_apply, 0)

    def conv_back(block, carry):
        cs = lanes_at(block)
        pixels = tile_rows(img, block)
        upstream = tile_rows(gout, block)
        grads = [gcv[8 * r : 8 * r + 8, cs] for r in range(16)]
        sums = upstream
        for horizontal in range(7):
            moved = [shifted(tile, 3 - horizontal) for tile in grads]
            for vertical in range(7):
                tap = vertical * 7 + horizontal
                weight = jnp.broadcast_to(dww[vertical, horizontal : horizontal + 1, cs], (8, LANES))
                taps = jnp.zeros((8, LANES), F32)
                for image in range(2):
                    for p in range(8):
                        source = p - (vertical - 3)
                        if 0 <= source < 8:
                            tile = moved[image * 8 + source]
                            sums[image * 8 + p] = sums[image * 8 + p] + tile * weight
                            taps = taps + tile * pixels[image * 8 + p]
                sm[tap : tap + 1, cs] = jnp.sum(taps, axis=0, keepdims=True)
        for r in range(8):
            grad_img[16 * r : 16 * r + 16, cs] = jnp.concatenate(sums[2 * r : 2 * r + 2], axis=0).astype(BF16)
        return carry

    lax.fori_loop(0, BLOCKS // 2, conv_back, 0)

    rs_d1.end()
    rs_d2 = RingSum(copies, ring_x, gdv, z * 192, 48, d2b, d2a)
    rs_d2.begin()
    rs_d2.own_halves()
    rs_u1.end()
    rs_u2 = RingSum(copies, ring_z, guv, x * 768, 192, u2b, u2a)
    rs_u2.begin()
    rs_u2.own_halves()
    lax.fori_loop(BLOCKS // 2, BLOCKS, conv_back, 0)

    def scale_block(block, carry):
        cs = lanes_at(block)
        upstream = jnp.sum(gout[:, cs].astype(F32), axis=0, keepdims=True)
        sm[53:54, cs] = sm[53:54, cs] + upstream * bdown[0:1, cs]
        return carry

    lax.fori_loop(0, BLOCKS, scale_block, 0)
    sm[54:64, :] = jnp.zeros((10, CH), F32)
    for s in range(2):
        shard = y * 2 + (me.x_hi if s == 0 else 1 - me.x_hi)
        for line in range(2):

            @pl.when(lax.div(shard, 4) == line)
            def _(s=s, line=line):
                at = pl.ds(pl.multiple_of(lax.rem(shard, 4) * HID, LANES), HID)
                sm[54 + line : 55 + line, at] = pbias[s : s + 1, :]

    swap_small = copies.push(sm.at[pl.ds(pl.multiple_of(me.other_core * 32, 8), 32)], smc, mate)
    small_rows = me.core * 32
    sm_at = pl.ds(pl.multiple_of(small_rows, 8), 32)
    yr, yl, yy, y_right, y_left, y_far = ring_y
    zr, zl = ring_z[0], ring_z[1]
    h = CH // 2
    lo, hi = pl.ds(0, h), pl.ds(h, h)

    def small_piece(which):
        return pl.ds(pl.multiple_of(small_rows + which * 8, 8), 8)

    def all_begin(buffer, ring):
        where = ring[2]
        return [
            copies.push(buffer.at[where], buffer.at[where], ring[0]),
            copies.push(buffer.at[where], buffer.at[where], ring[1]),
        ]

    def all_middle(buffer, ring, one):
        at_right, at_left = ring[3], ring[4]
        one[0].wait_recv()
        two = [copies.push(buffer.at[at_left, :, lo], buffer.at[at_left, :, lo], ring[0])]
        one[1].wait_recv()
        two.append(copies.push(buffer.at[at_right, :, hi], buffer.at[at_right, :, hi], ring[1]))
        return two

    def all_end(buffer, two):
        for copy in two:
            copy.wait_recv()
        return buffer[0] + buffer[1] + buffer[2] + buffer[3]

    rs_d2.middle()
    rs_u2.middle()
    swap_small.wait_recv()
    sm[sm_at, :] = sm[sm_at, :] + smc[...]
    s_one = [
        copies.push(sm.at[small_piece(y_far), lo], sya.at[0], yr),
        copies.push(sm.at[small_piece(y_far), hi], sya.at[1], yl),
    ]
    rs_b.middle()

    rs_d2.end()
    at_d = z * 192 + x * 48
    at_u = x * 768 + z * 192
    fd[...] = (gdv[rows_at(at_d, 48), :].astype(F32) * factor).astype(BF16)
    needed = me.x_hi == me.core

    def drow(which_x):
        return rows_at(z * 192 + which_x * 48, 48)

    d_cut = copies.remote(fd, out_down.at[drow(x)], x_cut)
    d_swap = copies.remote(fd, out_down.at[drow(x)], x_pair)
    d_cut_swap = copies.remote(out_down.at[drow(me.x_cut)], out_down.at[drow(me.x_cut)], x_pair)
    d_own = pltpu.make_async_copy(fd, out_down.at[drow(x)], local.at[62])

    @pl.when(jnp.logical_not(needed))
    def _():
        d_cut.start()

    @pl.when(needed)
    def _():
        d_own.start()
        d_swap.start()

    rs_u2.end()
    fu[...] = (guv[rows_at(at_u, 192), :].astype(F32) * factor).astype(BF16)

    def slot(which):
        return rows_at(which * 192, 192)

    def upiece(which_x, which):
        return rows_at(which_x * 768 + which * 192, 192)

    spots = (z, z_left, z_right, z_far)
    u_cut, u_swap, u_cut_swap = [], [], []
    for index, spot in enumerate(spots):
        piece_ref = fu if index == 0 else tq.at[slot(spot)]
        u_cut.append(copies.remote(piece_ref, out_up.at[upiece(x, spot)], x_cut))
        u_swap.append(copies.remote(piece_ref, out_up.at[upiece(x, spot)], x_pair))
        far_ref = out_up.at[upiece(me.x_cut, spot)]
        u_cut_swap.append(copies.remote(far_ref, far_ref, x_pair))

    def start_up(index):
        @pl.when(jnp.logical_not(needed))
        def _():
            u_cut[index].start()

        @pl.when(needed)
        def _():
            u_swap[index].start()

    def cross_up(*indices):
        @pl.when(needed)
        def _():
            for index in indices:
                u_cut[index].wait_recv()
                u_cut_swap[index].start()

    tq_own = copies.here(fu, tq.at[slot(z)])
    up_one = [copies.push(fu, tq.at[slot(z)], zr), copies.push(fu, tq.at[slot(z)], zl)]
    start_up(0)

    s_two = []
    for side, (device, which) in enumerate(((yr, y_right), (yl, y_left))):
        s_one[side].wait_recv()
        at = small_piece(which)
        sm[at, pl.ds(side * h, h)] = sm[at, pl.ds(side * h, h)] + sya[side]
        s_two.append(copies.push(sm.at[at], syb.at[side], device))

    @pl.when(needed)
    def _():
        d_cut.wait_recv()
        d_cut_swap.start()

    for side in range(2):
        s_two[side].wait_recv()
    at = small_piece(yy)
    sz[pl.ds(z, 1)] = (sm[at, :] + syb[0] + syb[1])[None]
    sz_one = all_begin(sz, ring_z)

    hu = HID // 2
    z_left_slot, z_right_slot = slot(z_left), slot(z_right)
    up_one[0].wait_recv()
    up_two = [copies.push(tq.at[z_left_slot, pl.ds(0, hu)], tq.at[z_left_slot, pl.ds(0, hu)], zr)]
    start_up(1)
    up_one[1].wait_recv()
    up_two.append(copies.push(tq.at[z_right_slot, pl.ds(hu, hu)], tq.at[z_right_slot, pl.ds(hu, hu)], zl))
    start_up(2)
    sz_two = all_middle(sz, ring_z, sz_one)

    def dblock(which):
        return rows_at(which * 192, 192)

    block = dblock(z)
    d_right = copies.remote(out_down.at[block], out_down.at[block], zr)
    d_left = copies.remote(out_down.at[block], out_down.at[block], zl)
    d_mate = copies.remote(out_down.at[block], out_down.at[block], mate)

    @pl.when(needed)
    def _():
        d_own.wait()
        d_swap.wait_recv()
        d_cut_swap.wait_recv()
        d_right.start()
        d_left.start()
        d_mate.start()

    for copy in up_two:
        copy.wait_recv()
    start_up(3)
    cross_up(0)
    tq_own.wait()

    def urow(which_x):
        return rows_at(which_x * 768, 768)

    u_mate = copies.remote(tq, out_up.at[urow(x)], mate)
    u_own = pltpu.make_async_copy(tq, out_up.at[urow(x)], local.at[63])

    @pl.when(needed)
    def _():
        u_mate.start()
        u_own.start()

    sx[pl.ds(x, 1)] = all_end(sz, sz_two)[None]
    sx_one = all_begin(sx, ring_x)
    cross_up(1)

    rs_b.end()

    def result_block(block, carry):
        cs = lanes_at(block)
        branch = own_rows(bv, cs) + bdown[0:1, cs]
        out_img[:, cs] = (img[:, cs].astype(F32) + lscale[0:1, cs] * branch).astype(BF16)
        return carry

    lax.fori_loop(0, BLOCKS, result_block, 0)
    sx_two = all_middle(sx, ring_x, sx_one)
    cross_up(2)

    total = all_end(sx, sx_two)
    smo_at = small_piece(yy)
    smo[smo_at, :] = total * factor
    so_one = [
        copies.push(smo.at[smo_at], smo.at[smo_at], yr),
        copies.push(smo.at[smo_at], smo.at[smo_at], yl),
    ]
    from_left, from_right = small_piece(y_left), small_piece(y_right)
    cross_up(3)
    so_one[0].wait_recv()
    so_two = [copies.push(smo.at[from_left, lo], smo.at[from_left, lo], yr)]
    so_one[1].wait_recv()
    so_two.append(copies.push(smo.at[from_right, hi], smo.at[from_right, hi], yl))
    for copy in so_two:
        copy.wait_recv()
    small_mate = copies.push(smo.at[sm_at], smo.at[sm_at], mate)

    block_l, block_r, block_f = dblock(z_left), dblock(z_right), dblock(z_far)
    d_fwd_right = copies.remote(out_down.at[block_l, lo], out_down.at[block_l, lo], zr)
    d_fwd_left = copies.remote(out_down.at[block_r, hi], out_down.at[block_r, hi], zl)
    d_mate_l = copies.remote(out_down.at[block_l], out_down.at[block_l], mate)
    d_mate_r = copies.remote(out_down.at[block_r], out_down.at[block_r], mate)
    d_mate_f = copies.remote(out_down.at[block_f], out_down.at[block_f], mate)
    q_cut, q_pair = urow(me.x_cut), urow(me.x_pair)
    u_mate_c = copies.remote(out_up.at[q_cut], out_up.at[q_cut], mate)
    u_mate_p = copies.remote(out_up.at[q_pair], out_up.at[q_pair], mate)
    u_mate_f = []
    for spot in spots:
        far_ref = out_up.at[upiece(3 - me.x_pair, spot)]
        u_mate_f.append(copies.remote(far_ref, far_ref, mate))

    @pl.when(needed)
    def _():
        u_mate_c.start()
        d_right.wait_recv()
        d_fwd_right.start()
        d_mate_l.start()
        d_left.wait_recv()
        d_fwd_left.start()
        d_mate_r.start()
        for copy in u_swap:
            copy.wait_recv()
        u_mate_p.start()
        for index in range(3):
            u_cut_swap[index].wait_recv()
            u_mate_f[index].start()
        d_fwd_right.wait_recv()
        d_fwd_left.wait_recv()
        d_mate_f.start()
        u_cut_swap[3].wait_recv()
        u_mate_f[3].start()
        u_own.wait()
        for copy in (
            d_swap, d_cut_swap, d_right, d_left, d_mate, d_fwd_right, d_fwd_left, d_mate_l, d_mate_r, d_mate_f,
            u_mate, u_mate_c, u_mate_p, *u_swap, *u_cut_swap, *u_mate_f,
        ):
            copy.wait_send()

    @pl.when(jnp.logical_not(needed))
    def _():
        for copy in (d_mate, d_mate_l, d_mate_r, d_mate_f, u_mate, u_mate_c, u_mate_p, *u_mate_f):
            copy.wait_recv()
        d_cut.wait_send()
        for copy in u_cut:
            copy.wait_send()

    small_mate.wait_recv()
    out_small[...] = smo[...]
    copies.drain()


def second_call(*operands):
    remote = 128
    bf = lambda *shape: pltpu.VMEM(shape, BF16)
    fl = lambda *shape: pltpu.VMEM(shape, F32)
    return pl.pallas_call(
        second_kernel,
        out_shape=(
            jax.ShapeDtypeStruct((ROWS, CH), BF16),
            jax.ShapeDtypeStruct((ROWS, CH), BF16),
            jax.ShapeDtypeStruct((CH, HID), BF16),
            jax.ShapeDtypeStruct((HID, CH), BF16),
            jax.ShapeDtypeStruct((64, CH), F32),
        ),
        in_specs=[ANY] * 9 + [VMEM] * 9,
        out_specs=(VMEM, VMEM, ANY, ANY, VMEM),
        scratch_shapes=[
            bf(CH, HID), bf(HID, CH), bf(CH, HID), bf(HID, CH),
            bf(2, 192, 1536), bf(2, 192, 3072), bf(2, 768, 384), bf(2, 768, 768),
            bf(2, 48, 1536), bf(2, 48, 3072), bf(2, 192, 384), bf(2, 192, 768),
            bf(768, 768), bf(48, 3072), bf(192, 768),
            bf(512, CH), bf(512, CH),
            bf(2, 128, 1536), bf(2, 128, 3072), bf(2, 128, 1536), bf(2, 128, 3072),
            bf(2, 512, HID), bf(2, 512, HID), bf(2, 2, 768, HID), bf(2, 2, HID, 768),
            fl(ROWS, CH), fl(64, CH), fl(32, CH), fl(2, 8, 1536), fl(2, 8, CH),
            fl(4, 8, CH), fl(4, 8, CH), fl(64, CH),
            pltpu.SemaphoreType.DMA((remote,)),
            pltpu.SemaphoreType.DMA((remote,)),
            pltpu.SemaphoreType.DMA((64,)),
        ],
        compiler_params=pltpu.CompilerParams(
            collective_id=1, has_side_effects=True, vmem_limit_bytes=63 * 1024 * 1024
        ),
    )(*operands)


def last_kernel(oimg, gimg, up, down, small, o1, o2, o3, o4, dw, r1, r2, r3, r4, r5, gb, v1, v2, v3, v4, load, store):
    trips = [(oimg, v1, o1), (gimg, v2, o2)]
    for part in range(4):
        rows = pl.ds(part * 768, 768)
        trips.append((up.at[rows], v3.at[rows], o3.at[rows]))
    for part in range(4):
        rows = pl.ds(part * 192, 192)
        trips.append((down.at[rows], v4.at[rows], o4.at[rows]))
    loads = [pltpu.make_async_copy(src, mid, load.at[i]) for i, (src, mid, dst) in enumerate(trips)]
    stores = [pltpu.make_async_copy(mid, dst, store.at[i]) for i, (src, mid, dst) in enumerate(trips)]
    for move in loads:
        move.start()
    for vertical in range(7):
        dw[vertical] = small[vertical * 7 : vertical * 7 + 7, :]
    for index, ref in enumerate((r1, r2, r3, r4, r5)):
        ref[...] = small[49 + index, :]
    shard = lax.axis_index("fsdp")
    at = pl.ds(pl.multiple_of(lax.rem(shard, 4) * HID, LANES), HID)
    line = lax.div(shard, 4)
    gb[...] = jnp.where(line == 0, small[54:55, at], small[55:56, at]).astype(BF16)
    for first, second in zip(loads, stores):
        first.wait()
        second.start()
    for move in stores:
        move.wait()


def last_call(oimg, gimg, up, down, small):
    wide = jax.ShapeDtypeStruct((ROWS, CH), BF16)
    line = jax.ShapeDtypeStruct((CH,), F32)
    return pl.pallas_call(
        last_kernel,
        out_shape=(
            wide,
            wide,
            jax.ShapeDtypeStruct((CH, HID), BF16),
            jax.ShapeDtypeStruct((HID, CH), BF16),
            jax.ShapeDtypeStruct((7, 7, CH), F32),
            line,
            line,
            line,
            line,
            line,
            jax.ShapeDtypeStruct((1, HID), BF16),
        ),
        in_specs=[ANY] * 4 + [VMEM],
        out_specs=tuple([ANY] * 4 + [VMEM] * 7),
        scratch_shapes=[
            pltpu.VMEM((ROWS, CH), BF16),
            pltpu.VMEM((ROWS, CH), BF16),
            pltpu.VMEM((CH, HID), BF16),
            pltpu.VMEM((HID, CH), BF16),
            pltpu.SemaphoreType.DMA((10,)),
            pltpu.SemaphoreType.DMA((10,)),
        ],
        compiler_params=pltpu.CompilerParams(vmem_limit_bytes=62 * 1024 * 1024),
    )(oimg, gimg, up, down, small)


def on_device(
    images, grad_out, dw_weight, dw_bias, ln_gain, ln_bias, w_up, b_up, w_down, b_down, layer_scale
):
    img = images.reshape(ROWS, CH)
    gout = grad_out.reshape(ROWS, CH)
    row = lambda vector: vector.reshape(1, CH)
    std, inv, hid, gp, gs, wuo, wdo, grad_up, grad_down, pbias = first_call(
        img, gout, dw_weight, row(dw_bias), row(ln_gain), row(ln_bias), row(layer_scale), w_up, w_down, b_up
    )
    out_img, grad_img, out_up, out_down, small = second_call(
        hid, gp, gs, w_up, w_down, wuo, wdo, grad_up, grad_down, img, gout, std, inv, dw_weight, row(ln_gain), row(layer_scale), row(b_down), pbias
    )
    oimg, gimg, up, down, dw, r1, r2, r3, r4, r5, gb = last_call(out_img, grad_img, out_up, out_down, small)
    return (
        oimg.reshape(images.shape),
        gimg.reshape(images.shape),
        up,
        gb.reshape(HID),
        down,
        dw,
        r1,
        r2,
        r3,
        r4,
        r5,
    )


def solution(mesh):
    tokens = P(("dp", "fsdp"), None, None, None)
    up, bias, down = P(None, "fsdp"), P("fsdp"), P("fsdp", None)
    return jax.shard_map(
        on_device,
        mesh=mesh,
        in_specs=(tokens, tokens, P(), P(), P(), P(), up, bias, down, P(), P()),
        out_specs=(tokens, tokens, up, bias, down, P(), P(), P(), P(), P(), P()),
        check_vma=False,
    )
```

```python
import math

import jax
import jax.numpy as jnp
from jax import lax
from jax.experimental import pallas as pl
from jax.experimental.pallas import tpu as pltpu
from jax.sharding import PartitionSpec as P

MESH = pl.DeviceIdType.MESH
F32 = jnp.float32
BF16 = jnp.bfloat16
CH = 3072
HID = 768
ROWS = 128
LANES = 128
BLOCKS = CH // LANES
ANY = pl.BlockSpec(memory_space=pl.ANY)
VMEM = pl.BlockSpec(memory_space=pltpu.VMEM)


class Place:
    def __init__(self):
        d = lax.axis_index("dp")
        f = lax.axis_index("fsdp")
        self.z = lax.div(d, 4)
        self.x_lo = lax.rem(lax.div(d, 2), 2)
        self.core = lax.rem(d, 2)
        self.y = lax.div(f, 2)
        self.x_hi = lax.rem(f, 2)
        self.x = self.x_hi * 2 + self.x_lo
        self.other_core = 1 - self.core
        self.x_cut = 3 - self.x
        self.x_pair = self.x_hi * 2 + (1 - self.x_lo)

    def at(self, x=None, y=None, z=None, core=None):
        x = self.x if x is None else x
        y = self.y if y is None else y
        z = self.z if z is None else z
        core = self.core if core is None else core
        return (z * 4 + lax.rem(x, 2) * 2 + core, y * 2 + lax.div(x, 2))

    def ring(self, axis):
        me = getattr(self, axis)
        right, left, far = lax.rem(me + 1, 4), lax.rem(me + 3, 4), lax.rem(me + 2, 4)
        return self.at(**{axis: right}), self.at(**{axis: left}), me, right, left, far


class Copies:
    def __init__(self, send, recv, local):
        self.send, self.recv, self.local = send, recv, local
        self.used = 0
        self.used_local = 0
        self.sent = []

    def remote(self, src, dst, device):
        index = self.used
        self.used += 1
        return pltpu.make_async_remote_copy(
            src_ref=src,
            dst_ref=dst,
            send_sem=self.send.at[index],
            recv_sem=self.recv.at[index],
            device_id=device,
            device_id_type=MESH,
        )

    def push(self, src, dst, device):
        copy = self.remote(src, dst, device)
        copy.start()
        self.sent.append(copy)
        return copy

    def here(self, src, dst):
        index = self.used_local
        self.used_local += 1
        copy = pltpu.make_async_copy(src, dst, self.local.at[index])
        copy.start()
        return copy

    def drain(self):
        for copy in self.sent:
            copy.wait_send()


def greet(devices):
    barrier = pltpu.get_barrier_semaphore()
    for device in devices:
        pl.semaphore_signal(barrier, inc=1, device_id=device, device_id_type=MESH)
    pl.semaphore_wait(barrier, len(devices))


def rows_at(start, size):
    return pl.ds(pl.multiple_of(start, 16), size)


def lanes_at(block):
    return pl.ds(pl.multiple_of(block * LANES, LANES), LANES)


def shifted(row, by):
    if by == 0:
        return row
    moved = pltpu.roll(row, (-by) % 8, 0)
    place = lax.broadcasted_iota(jnp.int32, row.shape, 0)
    inside = (place + by >= 0) & (place + by < 8)
    return jnp.where(inside, moved, 0.0)


def tile_rows(ref, block):
    tiles = []
    for pair in range(8):
        both = ref[16 * pair : 16 * pair + 16, lanes_at(block)].astype(F32)
        tiles += [both[:8], both[8:]]
    return tiles


def conv_block(block, img, dww, dwb, out):
    pixels = tile_rows(img, block)
    cs = lanes_at(block)
    sums = [jnp.broadcast_to(dwb[0:1, cs], (8, LANES))] * 16
    for horizontal in range(7):
        moved = [shifted(tile, horizontal - 3) for tile in pixels]
        for vertical in range(7):
            weight = jnp.broadcast_to(dww[vertical, horizontal : horizontal + 1, cs], (8, LANES))
            for image in range(2):
                for p in range(8):
                    source = p + vertical - 3
                    if 0 <= source < 8:
                        sums[image * 8 + p] = sums[image * 8 + p] + moved[image * 8 + source] * weight
    for r in range(16):
        out[8 * r : 8 * r + 8, cs] = sums[r]


def gelu_parts(values):
    cdf = 0.5 * (1.0 + lax.erf(values * 0.7071067811865476))
    return values * cdf, cdf + values * jnp.exp(-0.5 * values * values) * 0.3989422804014327


NT = (((1,), (1,)), ((), ()))
TN = (((0,), (0,)), ((), ()))


def first_kernel(
    img, gout, dww, dwb, gain, shift, lscale, wu, wd, bu,
    std, inv, hid_out, gp_out, gs_out, wu_out, wd_out, grad_up, grad_down, bias_sums,
    gn, gs, wuv, wdv, b_own, bo, hid, gp, keep32, up_v, down_v,
    send, recv, local,
):
    me = Place()
    copies = Copies(send, recv, local)
    right, left, y, y_right, y_left, y_far = me.ring("y")
    cut = me.at(x=me.x_cut)
    pair = me.at(x=me.x_pair)
    mate = me.at(core=me.other_core)
    wu_load = copies.here(wu, wuv.at[0])
    wd_load = copies.here(wd, wdv.at[0])
    b_own[...] = jnp.broadcast_to(bu[...][None, :], (8, HID))
    z_right_chip, z_left_chip, z, z_right, z_left, z_far = me.ring("z")
    greet([right, left, cut, pair, mate, z_right_chip, z_left_chip])

    weights = (wuv.at[1], wdv.at[1])
    sizes = (192, 48)
    sides = (me.x_lo, 1 - me.x_lo)

    def piece(m, side, which):
        return rows_at((side * 8 + which * 2 + me.core) * sizes[m], sizes[m])

    def held(m, k, which):
        return weights[m].at[piece(m, sides[k], which)]

    bias = copies.push(b_own, bo, cut)
    over_cut = []
    for m in range(2):
        at = piece(m, sides[1], z)
        over_cut.append(copies.push((wu, wd)[m].at[at], weights[m].at[at], cut))
    swapped, ring_one, ring_two, mates = {}, {}, {}, {0: [], 1: []}

    def to_mate(m, ref):
        mates[m].append(copies.push(ref, ref, mate))

    def around(m, k):
        ref = held(m, k, z)
        ring_one[m, k] = copies.push(ref, ref, z_right_chip), copies.push(ref, ref, z_left_chip)
        to_mate(m, ref)

    def from_cut(m):
        over_cut[m].wait_recv()
        ref = held(m, 0, z)
        swapped[m] = copies.push(ref, ref, pair)
        around(m, 0)

    def from_pair(m):
        swapped[m].wait_recv()
        around(m, 1)

    def from_ring(m, k):
        width = (HID, CH)[m] // 2
        ring_one[m, k][0].wait_recv()
        ref = held(m, k, z_left)
        part = weights[m].at[piece(m, sides[k], z_left), pl.ds(0, width)]
        one = copies.push(part, part, z_right_chip)
        to_mate(m, ref)
        ring_one[m, k][1].wait_recv()
        ref = held(m, k, z_right)
        part = weights[m].at[piece(m, sides[k], z_right), pl.ds(width, width)]
        ring_two[m, k] = one, copies.push(part, part, z_left_chip)
        to_mate(m, ref)

    def from_far(m, k):
        for copy in ring_two[m, k]:
            copy.wait_recv()
        to_mate(m, held(m, k, z_far))

    def arrived(m):
        for copy in mates[m]:
            copy.wait_recv()

    own = rows_at(y * ROWS, ROWS)

    def scale_block(block, carry):
        cs = lanes_at(block)
        gs[own, cs] = (gout[:, cs].astype(F32) * lscale[0:1, cs]).astype(BF16)
        return carry

    lax.fori_loop(0, BLOCKS, scale_block, 0)

    half = ROWS // 2

    def halves(position):
        return rows_at(position * ROWS, half), rows_at(position * ROWS + half, half)

    def spread(buffer):
        low, high = halves(y)
        first = [copies.push(buffer.at[low], buffer.at[low], right), copies.push(buffer.at[high], buffer.at[high], left)]
        second = [copies.push(buffer.at[high], buffer.at[high], right), copies.push(buffer.at[low], buffer.at[low], left)]
        return first, second

    def forward(first, buffer):
        low, high = halves(y_left)[0], halves(y_right)[1]
        first[0].wait_recv()
        to_right = copies.push(buffer.at[low], buffer.at[low], right)
        first[1].wait_recv()
        to_left = copies.push(buffer.at[high], buffer.at[high], left)
        return [to_right, to_left]

    s_first, s_second = spread(gs)

    def conv_step(block, carry):
        conv_block(block, img, dww, dwb, std)
        return carry

    lax.fori_loop(0, BLOCKS // 2, conv_step, 0)
    from_cut(0)
    lax.fori_loop(BLOCKS // 2, BLOCKS, conv_step, 0)

    def add_block(block, total):
        return total + std[:, lanes_at(block)]

    zero = jnp.zeros((ROWS, LANES), F32)
    mean = jnp.sum(lax.fori_loop(0, BLOCKS, add_block, zero), axis=1, keepdims=True) * (1.0 / CH)

    def square_block(block, total):
        centred = std[:, lanes_at(block)] - mean
        return total + centred * centred

    variance = jnp.sum(lax.fori_loop(0, BLOCKS, square_block, zero), axis=1, keepdims=True) * (1.0 / CH)
    inv_std = lax.rsqrt(variance + 1e-06)
    inv[...] = jnp.broadcast_to(inv_std, (ROWS, LANES))

    def norm_block(block, carry):
        cs = lanes_at(block)
        standard = (std[:, cs] - mean) * inv_std
        std[:, cs] = standard
        gn[own, cs] = (standard * gain[0:1, cs] + shift[0:1, cs]).astype(BF16)
        return carry

    lax.fori_loop(0, BLOCKS, norm_block, 0)
    n_first, n_second = spread(gn)
    s_last = forward(s_first, gs)
    from_cut(1)

    tile = 256

    def hidden_tile(index):
        return pl.ds(pl.multiple_of(index * tile, tile), tile)

    bias_sums[...] = jnp.zeros_like(bias_sums)

    def own_grad_hidden():
        def body(index, carry):
            cs = hidden_tile(index)
            keep32[0, :, cs] = lax.dot_general(gs[...], wdv[0, cs, :], NT, preferred_element_type=F32)
            return carry

        lax.fori_loop(0, HID // tile, body, 0)

    def up_rows_of(s, position):
        at = rows_at(position * ROWS, ROWS)
        pre = jnp.dot(gn[at, :], wuv[s], preferred_element_type=F32)
        value, slope = gelu_parts(pre + (b_own if s == 0 else bo)[0:1, :])
        hid[s, at, :] = value.astype(BF16)
        if s == 0:
            grad = (keep32[0, at, :] * slope).astype(BF16)
            gp[0, at, :] = grad
            bias_sums[0:1, :] = bias_sums[0:1, :] + jnp.sum(grad.astype(F32), axis=0, keepdims=True)
        else:
            keep32[1, at, :] = slope

    def other_grad():
        def body(index, carry):
            cs = hidden_tile(index)
            grad = lax.dot_general(gs[...], wdv[1, cs, :], NT, preferred_element_type=F32)
            pre = (grad * keep32[1, :, cs]).astype(BF16)
            gp[1, :, cs] = pre
            bias_sums[1:2, cs] = jnp.sum(pre.astype(F32), axis=0, keepdims=True)
            return carry

        lax.fori_loop(0, HID // tile, body, 0)

    outs = []

    def part_place(matrix, s, part):
        if matrix == 0:
            at = (pl.ds(part * 768, 768), slice(None))
            outs.append(copies.here(up_v.at[(s,) + at], grad_up.at[(s,) + at]))
        else:
            at = (slice(None), pl.ds(part * 768, 768))
            outs.append(copies.here(down_v.at[(s,) + at], grad_down.at[(s,) + at]))

    def part_up(s):
        for part in range(4):
            rows = pl.ds(part * 768, 768)
            up_v[s, rows, :] = lax.dot_general(gn[:, rows], gp[s], TN, preferred_element_type=F32).astype(BF16)
            part_place(0, s, part)

    def part_down(s):
        for part in range(4):
            cs = pl.ds(part * 768, 768)
            down_v[s, :, cs] = lax.dot_general(hid[s], gs[:, cs], TN, preferred_element_type=F32).astype(BF16)
            part_place(1, s, part)

    from_pair(0)
    from_ring(0, 0)
    from_pair(1)
    from_ring(0, 1)
    wu_load.wait()
    wd_load.wait()
    for copy in s_second + s_last:
        copy.wait_recv()
    outs.append(copies.here(gs, gs_out))
    own_grad_hidden()
    n_last = forward(n_first, gn)
    from_ring(1, 0)
    from_ring(1, 1)
    up_rows_of(0, y)
    from_far(0, 0)
    from_far(0, 1)
    bias.wait_recv()
    for copy in n_second:
        copy.wait_recv()
    up_rows_of(0, y_right)
    up_rows_of(0, y_left)
    from_far(1, 0)
    from_far(1, 1)
    arrived(0)
    outs.append(copies.here(wuv.at[1], wu_out))
    up_rows_of(1, y)
    up_rows_of(1, y_right)
    up_rows_of(1, y_left)
    for copy in n_last:
        copy.wait_recv()
    up_rows_of(0, y_far)
    up_rows_of(1, y_far)
    outs.append(copies.here(hid, hid_out))
    part_down(0)
    part_up(0)
    part_down(1)
    arrived(1)
    outs.append(copies.here(wdv.at[1], wd_out))
    other_grad()
    outs.append(copies.here(gp, gp_out))
    part_up(1)
    for copy in outs:
        copy.wait()
    copies.drain()


def first_call(img, gout, dww, dwb, gain, shift, lscale, wu, wd, bu):
    remote = 64
    rows = 4 * ROWS
    return pl.pallas_call(
        first_kernel,
        out_shape=(
            jax.ShapeDtypeStruct((ROWS, CH), F32),
            jax.ShapeDtypeStruct((ROWS, LANES), F32),
            jax.ShapeDtypeStruct((2, rows, HID), BF16),
            jax.ShapeDtypeStruct((2, rows, HID), BF16),
            jax.ShapeDtypeStruct((rows, CH), BF16),
            jax.ShapeDtypeStruct((CH, HID), BF16),
            jax.ShapeDtypeStruct((HID, CH), BF16),
            jax.ShapeDtypeStruct((2, CH, HID), BF16),
            jax.ShapeDtypeStruct((2, HID, CH), BF16),
            jax.ShapeDtypeStruct((8, HID), F32),
        ),
        in_specs=[VMEM] * 7 + [ANY, ANY, VMEM],
        out_specs=(VMEM, VMEM, ANY, ANY, ANY, ANY, ANY, ANY, ANY, VMEM),
        scratch_shapes=[
            pltpu.VMEM((rows, CH), BF16),
            pltpu.VMEM((rows, CH), BF16),
            pltpu.VMEM((2, CH, HID), BF16),
            pltpu.VMEM((2, HID, CH), BF16),
            pltpu.VMEM((8, HID), F32),
            pltpu.VMEM((8, HID), F32),
            pltpu.VMEM((2, rows, HID), BF16),
            pltpu.VMEM((2, rows, HID), BF16),
            pltpu.VMEM((2, rows, HID), F32),
            pltpu.VMEM((2, CH, HID), BF16),
            pltpu.VMEM((2, HID, CH), BF16),
            pltpu.SemaphoreType.DMA((remote,)),
            pltpu.SemaphoreType.DMA((remote,)),
            pltpu.SemaphoreType.DMA((32,)),
        ],
        compiler_params=pltpu.CompilerParams(
            collective_id=0, has_side_effects=True, vmem_limit_bytes=62 * 1024 * 1024
        ),
    )(img, gout, dww, dwb, gain, shift, lscale, wu, wd, bu)


def add_rows(dst, dst_row, sources, rows, column, columns, step=16):
    def body(index, carry):
        at = rows_at(dst_row + index * step, step)
        cs = pl.ds(column, columns)
        total = dst[at, cs].astype(F32)
        for ref, row, first in sources:
            total = total + ref[rows_at(row + index * step, step), pl.ds(first, columns)].astype(F32)
        dst[at, cs] = total.astype(dst.dtype)
        return carry

    lax.fori_loop(0, rows // step, body, 0)


class RingSum:
    def __init__(self, copies, where, data, base, rows, near, far, step=16):
        self.copies, self.data, self.base, self.rows = copies, data, base, rows
        self.right, self.left, self.me, self.at_right, self.at_left, self.at_far = where
        self.near, self.far, self.step = near, far, step
        self.half = data.shape[1] // 2

    def block(self, which):
        return self.base + which * self.rows

    def begin(self):
        at = rows_at(self.block(self.at_far), self.rows)
        h = self.half
        self.one = [
            self.copies.push(self.data.at[at, pl.ds(0, h)], self.far.at[0], self.right),
            self.copies.push(self.data.at[at, pl.ds(h, h)], self.far.at[1], self.left),
        ]

    def sides(self):
        return enumerate(((self.right, self.at_right), (self.left, self.at_left)))

    def own_halves(self):
        h = self.half
        self.two = []
        for side, (device, block) in self.sides():
            at, cs = rows_at(self.block(block), self.rows), pl.ds((1 - side) * h, h)
            self.two.append(self.copies.push(self.data.at[at, cs], self.near.at[side, :, cs], device))

    def middle(self):
        h = self.half
        for side, (device, block) in self.sides():
            self.one[side].wait_recv()
            start = self.block(block)
            add_rows(self.data, start, [(self.far.at[side], 0, 0)], self.rows, side * h, h, self.step)
            at, cs = rows_at(start, self.rows), pl.ds(side * h, h)
            self.two.append(self.copies.push(self.data.at[at, cs], self.near.at[side, :, cs], device))

    def end(self):
        for copy in self.two:
            copy.wait_recv()
        add_rows(
            self.data,
            self.block(self.me),
            [(self.near.at[0], 0, 0), (self.near.at[1], 0, 0)],
            self.rows,
            0,
            2 * self.half,
            self.step,
        )


def small_add(dst, row, sources, rows):
    total = dst[row, :]
    for source in sources:
        total = total + source
    dst[row, :] = total


def second_kernel(
    hid_in, gp_in, gs_in, wu, wd, wuo, wdo, gu, gd, img, gout, std, inv, dww, gain, lscale, bdown, pbias,
    out_img, grad_img, out_up, out_down, out_small,
    guv, gdv, cu, cd, d1a, d1b, u1a, u1b, d2a, d2b, u2a, u2b, tq, fd, fu,
    nv, bv, n1, n2, b1, b2, hid, gp, wu_t, wd_t, gcv, sm, smc, sya, syb, sx, sz, smo,
    send, recv, local,
):
    me = Place()
    copies = Copies(send, recv, local)
    ring_x, ring_y, ring_z = me.ring("x"), me.ring("y"), me.ring("z")
    mate = me.at(core=me.other_core)
    x_cut = me.at(x=me.x_cut)
    x_pair = me.at(x=me.x_pair)
    x, y, z = me.x, me.y, me.z
    factor = 1.0 / math.sqrt(16384.0)

    z_far, z_right, z_left = ring_z[5], ring_z[3], ring_z[4]
    x_far, x_right, x_left = ring_x[5], ring_x[3], ring_x[4]
    order = [(0, z_far), (1, x_far), (0, z_right), (1, x_right), (0, z_left), (1, x_left), (0, z), (1, x)]
    keep = lax.rem(me.x_hi + me.core, 2)
    give = 1 - keep
    swaps, loads = [], []

    def piece(matrix, which):
        return rows_at(which * 192, 192) if matrix == 0 else rows_at(which * 768, 768)

    def fetch(index):
        m, which = order[index]
        src, mine = ((gd, gdv), (gu, guv))[m]
        at = piece(m, which)
        loads.append(copies.here(src.at[keep, at], mine.at[at]))

    wide = 768

    def up_tile(part):
        at = pl.ds(part * wide, wide)
        return [copies.here(ref.at[at], wu_t.at[part % 2, s]) for s, ref in enumerate((wu, wuo))]

    def down_tile(part):
        at = pl.ds(part * wide, wide)
        return [copies.here(ref.at[:, at], wd_t.at[part % 2, s]) for s, ref in enumerate((wd, wdo))]

    fetch(0)
    fetch(1)
    load_gp = copies.here(gp_in, gp)
    tiles = {(0, 0): up_tile(0), (0, 1): up_tile(1)}
    for index in range(2, 8):
        fetch(index)
    load_hid = copies.here(hid_in, hid)
    load_gs = copies.here(gs_in, bv)
    tiles[1, 0], tiles[1, 1] = down_tile(0), down_tile(1)
    greet([ring_x[0], ring_x[1], ring_y[0], ring_y[1], ring_z[0], ring_z[1], mate])
    for m, which in order:
        src, dst = ((gd, cd), (gu, cu))[m]
        at = piece(m, which)
        swaps.append(copies.push(src.at[give, at], dst.at[at], mate))

    def merge(index):
        m, which = order[index]
        mine, other = ((gdv, cd), (guv, cu))[m]
        rows = 192 if m == 0 else 768
        loads[index].wait()
        swaps[index].wait_recv()
        add_rows(mine, which * rows, [(other, which * rows, 0)], rows, 0, mine.shape[1], 16 if m == 0 else 64)

    rs_d1 = RingSum(copies, ring_z, gdv, 0, 192, d1b, d1a)
    rs_u1 = RingSum(copies, ring_x, guv, 0, 768, u1b, u1a)
    merge(0)
    rs_d1.begin()
    merge(1)
    rs_u1.begin()

    load_gp.wait()
    for part in range(4):
        for copy in tiles[0, part]:
            copy.wait()
        slot = part % 2
        total = lax.dot_general(gp[0], wu_t[slot, 0], NT, preferred_element_type=F32)
        total = total + lax.dot_general(gp[1], wu_t[slot, 1], NT, preferred_element_type=F32)
        nv[:, pl.ds(part * wide, wide)] = total.astype(BF16)
        if part < 2:
            tiles[0, part + 2] = up_tile(part + 2)
    rs_n = RingSum(copies, ring_y, nv, 0, ROWS, n2, n1)
    rs_n.begin()
    rs_n.own_halves()
    for index in range(2, 6):
        merge(index)
    rs_d1.own_halves()
    rs_u1.own_halves()
    load_hid.wait()
    load_gs.wait()
    for part in range(4):
        for copy in tiles[1, part]:
            copy.wait()
        slot = part % 2
        cs = pl.ds(part * wide, wide)
        total = jnp.dot(hid[0], wd_t[slot, 0], preferred_element_type=F32)
        total = total + jnp.dot(hid[1], wd_t[slot, 1], preferred_element_type=F32)
        product = jnp.sum(total * bv[:, cs].astype(F32), axis=0, keepdims=True)
        sm[53:54, cs] = product / lscale[0:1, cs]
        bv[:, cs] = total.astype(BF16)
        if part < 2:
            tiles[1, part + 2] = down_tile(part + 2)
    rs_b = RingSum(copies, ring_y, bv, 0, ROWS, b2, b1)
    rs_n.middle()
    rs_b.begin()
    rs_b.own_halves()
    rs_d1.middle()
    rs_u1.middle()
    merge(6)
    merge(7)

    rs_n.end()
    own = y * ROWS
    zero = jnp.zeros((ROWS, LANES), F32)

    def own_rows(ref, cs):
        return ref[rows_at(own, ROWS), cs].astype(F32)

    def norm_sums(block, totals):
        cs = lanes_at(block)
        grad_normed = own_rows(nv, cs)
        standard = std[:, cs]
        product = grad_normed * standard
        sm[50:51, cs] = jnp.sum(product, axis=0, keepdims=True)
        sm[51:52, cs] = jnp.sum(grad_normed, axis=0, keepdims=True)
        weight = gain[0:1, cs]
        return totals[0] + grad_normed * weight, totals[1] + product * weight

    total_g, total_gs = lax.fori_loop(0, BLOCKS, norm_sums, (zero, zero))
    mean_g = jnp.sum(total_g, axis=1, keepdims=True) * (1.0 / CH)
    mean_gs = jnp.sum(total_gs, axis=1, keepdims=True) * (1.0 / CH)
    inv_std = inv[...]

    def norm_apply(block, carry):
        cs = lanes_at(block)
        grad_hat = own_rows(nv, cs) * gain[0:1, cs]
        grad_conv = inv_std * (grad_hat - mean_g - std[:, cs] * mean_gs)
        gcv[:, cs] = grad_conv
        sm[49:50, cs] = jnp.sum(grad_conv, axis=0, keepdims=True)
        upstream = gout[:, cs].astype(F32)
        scaled = (upstream * lscale[0:1, cs]).astype(BF16).astype(F32)
        sm[52:53, cs] = jnp.sum(scaled, axis=0, keepdims=True)
        return carry

    lax.fori_loop(0, BLOCKS, norm_apply, 0)

    def conv_back(block, carry):
        cs = lanes_at(block)
        pixels = tile_rows(img, block)
        upstream = tile_rows(gout, block)
        grads = [gcv[8 * r : 8 * r + 8, cs] for r in range(16)]
        sums = upstream
        for horizontal in range(7):
            moved = [shifted(tile, 3 - horizontal) for tile in grads]
            for vertical in range(7):
                tap = vertical * 7 + horizontal
                weight = jnp.broadcast_to(dww[vertical, horizontal : horizontal + 1, cs], (8, LANES))
                taps = jnp.zeros((8, LANES), F32)
                for image in range(2):
                    for p in range(8):
                        source = p - (vertical - 3)
                        if 0 <= source < 8:
                            tile = moved[image * 8 + source]
                            sums[image * 8 + p] = sums[image * 8 + p] + tile * weight
                            taps = taps + tile * pixels[image * 8 + p]
                sm[tap : tap + 1, cs] = jnp.sum(taps, axis=0, keepdims=True)
        for r in range(8):
            grad_img[16 * r : 16 * r + 16, cs] = jnp.concatenate(sums[2 * r : 2 * r + 2], axis=0).astype(BF16)
        return carry

    lax.fori_loop(0, BLOCKS // 2, conv_back, 0)

    rs_d1.end()
    rs_d2 = RingSum(copies, ring_x, gdv, z * 192, 48, d2b, d2a)
    rs_d2.begin()
    rs_d2.own_halves()
    rs_u1.end()
    rs_u2 = RingSum(copies, ring_z, guv, x * 768, 192, u2b, u2a)
    rs_u2.begin()
    rs_u2.own_halves()
    lax.fori_loop(BLOCKS // 2, BLOCKS, conv_back, 0)

    def scale_block(block, carry):
        cs = lanes_at(block)
        upstream = jnp.sum(gout[:, cs].astype(F32), axis=0, keepdims=True)
        sm[53:54, cs] = sm[53:54, cs] + upstream * bdown[0:1, cs]
        return carry

    lax.fori_loop(0, BLOCKS, scale_block, 0)
    sm[54:64, :] = jnp.zeros((10, CH), F32)
    for s in range(2):
        shard = y * 2 + (me.x_hi if s == 0 else 1 - me.x_hi)
        for line in range(2):

            @pl.when(lax.div(shard, 4) == line)
            def _(s=s, line=line):
                at = pl.ds(pl.multiple_of(lax.rem(shard, 4) * HID, LANES), HID)
                sm[54 + line : 55 + line, at] = pbias[s : s + 1, :]

    swap_small = copies.push(sm.at[pl.ds(pl.multiple_of(me.other_core * 32, 8), 32)], smc, mate)
    small_rows = me.core * 32
    sm_at = pl.ds(pl.multiple_of(small_rows, 8), 32)
    yr, yl, yy, y_right, y_left, y_far = ring_y
    zr, zl = ring_z[0], ring_z[1]
    h = CH // 2
    lo, hi = pl.ds(0, h), pl.ds(h, h)

    def small_piece(which):
        return pl.ds(pl.multiple_of(small_rows + which * 8, 8), 8)

    def all_begin(buffer, ring):
        where = ring[2]
        return [
            copies.push(buffer.at[where], buffer.at[where], ring[0]),
            copies.push(buffer.at[where], buffer.at[where], ring[1]),
        ]

    def all_middle(buffer, ring, one):
        at_right, at_left = ring[3], ring[4]
        one[0].wait_recv()
        two = [copies.push(buffer.at[at_left, :, lo], buffer.at[at_left, :, lo], ring[0])]
        one[1].wait_recv()
        two.append(copies.push(buffer.at[at_right, :, hi], buffer.at[at_right, :, hi], ring[1]))
        return two

    def all_end(buffer, two):
        for copy in two:
            copy.wait_recv()
        return buffer[0] + buffer[1] + buffer[2] + buffer[3]

    rs_d2.middle()
    rs_u2.middle()
    swap_small.wait_recv()
    sm[sm_at, :] = sm[sm_at, :] + smc[...]
    s_one = [
        copies.push(sm.at[small_piece(y_far), lo], sya.at[0], yr),
        copies.push(sm.at[small_piece(y_far), hi], sya.at[1], yl),
    ]
    rs_b.middle()

    rs_d2.end()
    at_d = z * 192 + x * 48
    at_u = x * 768 + z * 192
    fd[...] = (gdv[rows_at(at_d, 48), :].astype(F32) * factor).astype(BF16)
    needed = me.x_hi == me.core

    def drow(which_x):
        return rows_at(z * 192 + which_x * 48, 48)

    d_cut = copies.remote(fd, out_down.at[drow(x)], x_cut)
    d_swap = copies.remote(fd, out_down.at[drow(x)], x_pair)
    d_cut_swap = copies.remote(out_down.at[drow(me.x_cut)], out_down.at[drow(me.x_cut)], x_pair)
    d_own = pltpu.make_async_copy(fd, out_down.at[drow(x)], local.at[62])

    @pl.when(jnp.logical_not(needed))
    def _():
        d_cut.start()

    @pl.when(needed)
    def _():
        d_own.start()
        d_swap.start()

    rs_u2.end()
    fu[...] = (guv[rows_at(at_u, 192), :].astype(F32) * factor).astype(BF16)

    def slot(which):
        return rows_at(which * 192, 192)

    def upiece(which_x, which):
        return rows_at(which_x * 768 + which * 192, 192)

    spots = (z, z_left, z_right, z_far)
    u_cut, u_swap, u_cut_swap = [], [], []
    for index, spot in enumerate(spots):
        piece_ref = fu if index == 0 else tq.at[slot(spot)]
        u_cut.append(copies.remote(piece_ref, out_up.at[upiece(x, spot)], x_cut))
        u_swap.append(copies.remote(piece_ref, out_up.at[upiece(x, spot)], x_pair))
        far_ref = out_up.at[upiece(me.x_cut, spot)]
        u_cut_swap.append(copies.remote(far_ref, far_ref, x_pair))

    def start_up(index):
        @pl.when(jnp.logical_not(needed))
        def _():
            u_cut[index].start()

        @pl.when(needed)
        def _():
            u_swap[index].start()

    def cross_up(*indices):
        @pl.when(needed)
        def _():
            for index in indices:
                u_cut[index].wait_recv()
                u_cut_swap[index].start()

    tq_own = copies.here(fu, tq.at[slot(z)])
    up_one = [copies.push(fu, tq.at[slot(z)], zr), copies.push(fu, tq.at[slot(z)], zl)]
    start_up(0)

    s_two = []
    for side, (device, which) in enumerate(((yr, y_right), (yl, y_left))):
        s_one[side].wait_recv()
        at = small_piece(which)
        sm[at, pl.ds(side * h, h)] = sm[at, pl.ds(side * h, h)] + sya[side]
        s_two.append(copies.push(sm.at[at], syb.at[side], device))

    @pl.when(needed)
    def _():
        d_cut.wait_recv()
        d_cut_swap.start()

    for side in range(2):
        s_two[side].wait_recv()
    at = small_piece(yy)
    sz[pl.ds(z, 1)] = (sm[at, :] + syb[0] + syb[1])[None]
    sz_one = all_begin(sz, ring_z)

    hu = HID // 2
    z_left_slot, z_right_slot = slot(z_left), slot(z_right)
    up_one[0].wait_recv()
    up_two = [copies.push(tq.at[z_left_slot, pl.ds(0, hu)], tq.at[z_left_slot, pl.ds(0, hu)], zr)]
    start_up(1)
    up_one[1].wait_recv()
    up_two.append(copies.push(tq.at[z_right_slot, pl.ds(hu, hu)], tq.at[z_right_slot, pl.ds(hu, hu)], zl))
    start_up(2)
    sz_two = all_middle(sz, ring_z, sz_one)

    def dblock(which):
        return rows_at(which * 192, 192)

    block = dblock(z)
    d_right = copies.remote(out_down.at[block], out_down.at[block], zr)
    d_left = copies.remote(out_down.at[block], out_down.at[block], zl)
    d_mate = copies.remote(out_down.at[block], out_down.at[block], mate)

    @pl.when(needed)
    def _():
        d_own.wait()
        d_swap.wait_recv()
        d_cut_swap.wait_recv()
        d_right.start()
        d_left.start()
        d_mate.start()

    for copy in up_two:
        copy.wait_recv()
    start_up(3)
    cross_up(0)
    tq_own.wait()

    def urow(which_x):
        return rows_at(which_x * 768, 768)

    u_mate = copies.remote(tq, out_up.at[urow(x)], mate)
    u_own = pltpu.make_async_copy(tq, out_up.at[urow(x)], local.at[63])

    @pl.when(needed)
    def _():
        u_mate.start()
        u_own.start()

    sx[pl.ds(x, 1)] = all_end(sz, sz_two)[None]
    sx_one = all_begin(sx, ring_x)
    cross_up(1)

    rs_b.end()

    def result_block(block, carry):
        cs = lanes_at(block)
        branch = own_rows(bv, cs) + bdown[0:1, cs]
        out_img[:, cs] = (img[:, cs].astype(F32) + lscale[0:1, cs] * branch).astype(BF16)
        return carry

    lax.fori_loop(0, BLOCKS, result_block, 0)
    sx_two = all_middle(sx, ring_x, sx_one)
    cross_up(2)

    total = all_end(sx, sx_two)
    smo_at = small_piece(yy)
    smo[smo_at, :] = total * factor
    so_one = [
        copies.push(smo.at[smo_at], smo.at[smo_at], yr),
        copies.push(smo.at[smo_at], smo.at[smo_at], yl),
    ]
    from_left, from_right = small_piece(y_left), small_piece(y_right)
    cross_up(3)
    so_one[0].wait_recv()
    so_two = [copies.push(smo.at[from_left, lo], smo.at[from_left, lo], yr)]
    so_one[1].wait_recv()
    so_two.append(copies.push(smo.at[from_right, hi], smo.at[from_right, hi], yl))
    for copy in so_two:
        copy.wait_recv()
    small_mate = copies.push(smo.at[sm_at], smo.at[sm_at], mate)

    block_l, block_r, block_f = dblock(z_left), dblock(z_right), dblock(z_far)
    d_fwd_right = copies.remote(out_down.at[block_l, lo], out_down.at[block_l, lo], zr)
    d_fwd_left = copies.remote(out_down.at[block_r, hi], out_down.at[block_r, hi], zl)
    d_mate_l = copies.remote(out_down.at[block_l], out_down.at[block_l], mate)
    d_mate_r = copies.remote(out_down.at[block_r], out_down.at[block_r], mate)
    d_mate_f = copies.remote(out_down.at[block_f], out_down.at[block_f], mate)
    q_cut, q_pair = urow(me.x_cut), urow(me.x_pair)
    u_mate_c = copies.remote(out_up.at[q_cut], out_up.at[q_cut], mate)
    u_mate_p = copies.remote(out_up.at[q_pair], out_up.at[q_pair], mate)
    u_mate_f = []
    for spot in spots:
        far_ref = out_up.at[upiece(3 - me.x_pair, spot)]
        u_mate_f.append(copies.remote(far_ref, far_ref, mate))

    @pl.when(needed)
    def _():
        u_mate_c.start()
        d_right.wait_recv()
        d_fwd_right.start()
        d_mate_l.start()
        d_left.wait_recv()
        d_fwd_left.start()
        d_mate_r.start()
        for copy in u_swap:
            copy.wait_recv()
        u_mate_p.start()
        for index in range(3):
            u_cut_swap[index].wait_recv()
            u_mate_f[index].start()
        d_fwd_right.wait_recv()
        d_fwd_left.wait_recv()
        d_mate_f.start()
        u_cut_swap[3].wait_recv()
        u_mate_f[3].start()
        u_own.wait()
        for copy in (
            d_swap, d_cut_swap, d_right, d_left, d_mate, d_fwd_right, d_fwd_left, d_mate_l, d_mate_r, d_mate_f,
            u_mate, u_mate_c, u_mate_p, *u_swap, *u_cut_swap, *u_mate_f,
        ):
            copy.wait_send()

    @pl.when(jnp.logical_not(needed))
    def _():
        for copy in (d_mate, d_mate_l, d_mate_r, d_mate_f, u_mate, u_mate_c, u_mate_p, *u_mate_f):
            copy.wait_recv()
        d_cut.wait_send()
        for copy in u_cut:
            copy.wait_send()

    small_mate.wait_recv()
    out_small[...] = smo[...]
    copies.drain()


def second_call(*operands):
    remote = 128
    bf = lambda *shape: pltpu.VMEM(shape, BF16)
    fl = lambda *shape: pltpu.VMEM(shape, F32)
    return pl.pallas_call(
        second_kernel,
        out_shape=(
            jax.ShapeDtypeStruct((ROWS, CH), BF16),
            jax.ShapeDtypeStruct((ROWS, CH), BF16),
            jax.ShapeDtypeStruct((CH, HID), BF16),
            jax.ShapeDtypeStruct((HID, CH), BF16),
            jax.ShapeDtypeStruct((64, CH), F32),
        ),
        in_specs=[ANY] * 9 + [VMEM] * 9,
        out_specs=(VMEM, VMEM, ANY, ANY, VMEM),
        scratch_shapes=[
            bf(CH, HID), bf(HID, CH), bf(CH, HID), bf(HID, CH),
            bf(2, 192, 1536), bf(2, 192, 3072), bf(2, 768, 384), bf(2, 768, 768),
            bf(2, 48, 1536), bf(2, 48, 3072), bf(2, 192, 384), bf(2, 192, 768),
            bf(768, 768), bf(48, 3072), bf(192, 768),
            bf(512, CH), bf(512, CH),
            bf(2, 128, 1536), bf(2, 128, 3072), bf(2, 128, 1536), bf(2, 128, 3072),
            bf(2, 512, HID), bf(2, 512, HID), bf(2, 2, 768, HID), bf(2, 2, HID, 768),
            fl(ROWS, CH), fl(64, CH), fl(32, CH), fl(2, 8, 1536), fl(2, 8, CH),
            fl(4, 8, CH), fl(4, 8, CH), fl(64, CH),
            pltpu.SemaphoreType.DMA((remote,)),
            pltpu.SemaphoreType.DMA((remote,)),
            pltpu.SemaphoreType.DMA((64,)),
        ],
        compiler_params=pltpu.CompilerParams(
            collective_id=1, has_side_effects=True, vmem_limit_bytes=63 * 1024 * 1024
        ),
    )(*operands)


def last_kernel(oimg, gimg, up, down, small, o1, o2, o3, o4, dw, r1, r2, r3, r4, r5, gb, v1, v2, v3, v4, load, store):
    trips = [(oimg, v1, o1), (gimg, v2, o2)]
    for part in range(4):
        rows = pl.ds(part * 768, 768)
        trips.append((up.at[rows], v3.at[rows], o3.at[rows]))
    for part in range(4):
        rows = pl.ds(part * 192, 192)
        trips.append((down.at[rows], v4.at[rows], o4.at[rows]))
    loads = [pltpu.make_async_copy(src, mid, load.at[i]) for i, (src, mid, dst) in enumerate(trips)]
    stores = [pltpu.make_async_copy(mid, dst, store.at[i]) for i, (src, mid, dst) in enumerate(trips)]
    for move in loads:
        move.start()
    for vertical in range(7):
        dw[vertical] = small[vertical * 7 : vertical * 7 + 7, :]
    for index, ref in enumerate((r1, r2, r3, r4, r5)):
        ref[...] = small[49 + index, :]
    shard = lax.axis_index("fsdp")
    at = pl.ds(pl.multiple_of(lax.rem(shard, 4) * HID, LANES), HID)
    line = lax.div(shard, 4)
    gb[...] = jnp.where(line == 0, small[54, at], small[55, at]).astype(BF16)
    for first, second in zip(loads, stores):
        first.wait()
        second.start()
    for move in stores:
        move.wait()


def last_call(oimg, gimg, up, down, small):
    wide = jax.ShapeDtypeStruct((ROWS, CH), BF16)
    line = jax.ShapeDtypeStruct((CH,), F32)
    return pl.pallas_call(
        last_kernel,
        out_shape=(
            wide,
            wide,
            jax.ShapeDtypeStruct((CH, HID), BF16),
            jax.ShapeDtypeStruct((HID, CH), BF16),
            jax.ShapeDtypeStruct((7, 7, CH), F32),
            line,
            line,
            line,
            line,
            line,
            jax.ShapeDtypeStruct((HID,), BF16),
        ),
        in_specs=[ANY] * 4 + [VMEM],
        out_specs=tuple([ANY] * 4 + [VMEM] * 7),
        scratch_shapes=[
            pltpu.VMEM((ROWS, CH), BF16),
            pltpu.VMEM((ROWS, CH), BF16),
            pltpu.VMEM((CH, HID), BF16),
            pltpu.VMEM((HID, CH), BF16),
            pltpu.SemaphoreType.DMA((10,)),
            pltpu.SemaphoreType.DMA((10,)),
        ],
        compiler_params=pltpu.CompilerParams(vmem_limit_bytes=62 * 1024 * 1024),
    )(oimg, gimg, up, down, small)


def on_device(
    images, grad_out, dw_weight, dw_bias, ln_gain, ln_bias, w_up, b_up, w_down, b_down, layer_scale
):
    img = images.reshape(ROWS, CH)
    gout = grad_out.reshape(ROWS, CH)
    row = lambda vector: vector.reshape(1, CH)
    std, inv, hid, gp, gs, wuo, wdo, grad_up, grad_down, pbias = first_call(
        img, gout, dw_weight, row(dw_bias), row(ln_gain), row(ln_bias), row(layer_scale), w_up, w_down, b_up
    )
    out_img, grad_img, out_up, out_down, small = second_call(
        hid, gp, gs, w_up, w_down, wuo, wdo, grad_up, grad_down, img, gout, std, inv, dw_weight, row(ln_gain), row(layer_scale), row(b_down), pbias
    )
    oimg, gimg, up, down, dw, r1, r2, r3, r4, r5, gb = last_call(out_img, grad_img, out_up, out_down, small)
    return (
        oimg.reshape(images.shape),
        gimg.reshape(images.shape),
        up,
        gb,
        down,
        dw,
        r1,
        r2,
        r3,
        r4,
        r5,
    )


def solution(mesh):
    tokens = P(("dp", "fsdp"), None, None, None)
    up, bias, down = P(None, "fsdp"), P("fsdp"), P("fsdp", None)
    return jax.shard_map(
        on_device,
        mesh=mesh,
        in_specs=(tokens, tokens, P(), P(), P(), P(), up, bias, down, P(), P()),
        out_specs=(tokens, tokens, up, bias, down, P(), P(), P(), P(), P(), P()),
        check_vma=False,
    )
```
